128 devices in a mesh: dp: 4 (over x), expert: 16 (over y, z), blk: 2 (over core).
Axes of the slice: x: 4, y: 4, z: 4, core: 2. Of those that a mesh axis runs over, the one named last changes fastest.
Arguments:
- tokens_in: bfloat16 [8192, 1536], P(('dp', 'expert'), 'blk'), may hold values from -6 to 6
- seq_lengths: int32 [64, 3], P(('dp', 'expert')), may hold values from 1 to 64, 128 in all within a row
- expert_ids: int32 [2, 8192, 4], P(None, ('dp', 'expert')), may hold values from 0 to 31, all different within a row; in each aligned block of 128 rows (0 to 127, 128 to 255, ..., all dimensions but the last counted through in order) at most 24 rows name the same one
- gate_weights: float32 [2, 8192, 4], P(None, ('dp', 'expert')), may hold values from 0.12 to 0.48
- attention_gain: bfloat16 [2, 1536], P(None, ('dp', 'expert')), may hold values from 0.099609375 to 1.8984375
- query_weight: bfloat16 [2, 1536, 1536], P(None, ('dp', 'expert'), 'blk'), may hold values from -0.15625 to 0.15625
- key_weight: bfloat16 [2, 1536, 256], P(None, ('dp', 'expert'), 'blk'), may hold values from -0.15625 to 0.15625
- value_weight: bfloat16 [2, 1536, 256], P(None, ('dp', 'expert'), 'blk'), may hold values from -0.15625 to 0.15625
- out_weight: bfloat16 [2, 1536, 1536], P(None, 'blk', ('dp', 'expert')), may hold values from -0.625 to 0.625
- expert_gain: bfloat16 [2, 1536], P(None, ('dp', 'expert')), may hold values from 0.099609375 to 1.8984375
- gate_weight: bfloat16 [2, 32, 1536, 768], P(None, 'expert', None, 'blk'), may hold values from -0.15625 to 0.15625
- up_weight: bfloat16 [2, 32, 1536, 768], P(None, 'expert', None, 'blk'), may hold values from -0.15625 to 0.15625
- down_weight: bfloat16 [2, 32, 768, 1536], P(None, 'expert', 'blk'), may hold values from -0.4375 to 0.4375
- cotangent: bfloat16 [8192, 1536], P(('dp', 'expert'), 'blk'), may hold values from -6 to 6
Outputs:
- block_out: bfloat16 [8192, 1536], P(('dp', 'expert'), 'blk')
- grad_tokens: float32 [8192, 1536], P(('dp', 'expert'), 'blk')
- grad_attention_gain: float32 [2, 1536], P(None, ('dp', 'expert'))
- grad_query_weight: float32 [2, 1536, 1536], P(None, ('dp', 'expert'), 'blk')
- grad_key_weight: float32 [2, 1536, 256], P(None, ('dp', 'expert'), 'blk')
- grad_value_weight: float32 [2, 1536, 256], P(None, ('dp', 'expert'), 'blk')
- grad_out_weight: float32 [2, 1536, 1536], P(None, 'blk', ('dp', 'expert'))
- grad_expert_gain: float32 [2, 1536], P(None, ('dp', 'expert'))
- grad_gate_weight: float32 [2, 32, 1536, 768], P(None, 'expert', 'dp', 'blk')
- grad_up_weight: float32 [2, 32, 1536, 768], P(None, 'expert', 'dp', 'blk')
- grad_down_weight: float32 [2, 32, 768, 1536], P(None, 'expert', 'blk', 'dp')
The draws below stay inside these ranges and needn't reach their ends.
Inputs may be any that keep to these rules, and one draw needn't show every extreme that they name: `seq_lengths`: each row holds one group's 3 sequence lengths, which sum to 128; the longest is exactly 64. `expert_ids`: a token's 4 ids in a layer differ; in one layer, among the 128 tokens of one group (the rows of one device), no expert is named more than 24 times, a bound that some block reaches.
All inputs are finite; a program needn't handle non-finite values.
Results may differ from the reference program's by a relative error of at most 0.025.
Values may be sent and summed in bfloat16 or wider, within the bound.
A program may use at most 256 MiB of HBM per device.

```python
import math
import jax
import jax.numpy as jnp
import numpy as np
from jax import lax

D = 1536
HEADS = 12
KV_HEADS = 2
HEAD = 128
FF = 768
TOP = 4
LAYERS = 2
NSEQ = 3
TOK_GRP = 128
SEQ_MOST = 64
EXPERTS = 32
GROUPS = 64
TOKENS = 8192
QD = 1536
KD = 256
CAP = 24
N_BLK = 2


def steps_of(rng, dims, shards, smallest, top_value):
    loudness = 1.0
    for axis_at, blocks in shards:
        steps = jax.random.uniform(jax.random.fold_in(jax.random.fold_in(rng, 6), axis_at), (blocks,), jnp.float32, smallest / len(shards), top_value / len(shards))
        loudness = loudness * jnp.repeat(jnp.exp(steps), dims[axis_at] // blocks).reshape((-1,) + (1,) * (len(dims) - 1 - axis_at))
    return loudness


def split_up(number_of, total, limit, slope):
    weights = [(1 << 20) // math.isqrt(rank ** slope) + 1 for rank in range(2, number_of + 1)]
    spare, counts = total - limit - (number_of - 1), [1] * (number_of - 1)
    while spare > 0:
        candidates = [i for i in range(number_of - 1) if counts[i] < limit]
        mass, remaining = sum([weights[i] for i in candidates]), spare
        for i in candidates:
            extra = min(limit - counts[i], max(1, remaining * weights[i] // mass), spare)
            counts[i] = counts[i] + extra
            spare = spare - extra
    return np.array([limit] + counts)


def ragged(rng, count, total, reach, skew):
    if count == 2:
        one = jax.random.randint(rng, (), max(1, total - reach), min(reach, total - 1) + 1)
        return jnp.stack([one, total - one])
    tallies = jnp.asarray(split_up(count, total, reach, skew), jnp.int32)
    pairs = (count - 1) // 2
    giver, sink = tallies[1:1 + 2 * pairs:2], tallies[2:2 + 2 * pairs:2]
    slack = jnp.minimum(giver - 1, reach - sink)
    shifted = jax.random.randint(jax.random.fold_in(rng, 1), (pairs,), 0, 1 << 20) % (slack + 1)
    tallies = tallies.at[1:1 + 2 * pairs:2].set(giver - shifted).at[2:2 + 2 * pairs:2].set(sink + shifted)
    return tallies[jax.random.permutation(jax.random.fold_in(rng, 2), count)]


def deal_out(key, own, number, rows, count, top, bound, skew):
    ranking = jax.random.permutation(key, count)
    crowded, usual = load_shares(count, rows * top, bound, skew, True), load_shares(count, rows * top, bound, skew, False)
    places = jnp.arange(count)

    def named(sizes, offset_by):
        used = int((sizes > 0).sum())
        fixed = max(1, used // 4)
        passed = fixed + (places - fixed + offset_by * (used - fixed)) % max(1, count - fixed)
        return jnp.zeros((count,), jnp.int32).at[ranking[jnp.where(places < fixed, places, passed)]].set(jnp.asarray(sizes, jnp.int32))

    sizes = jnp.where(number % 4 == 0, named(crowded, number // 4), named(usual, number - number // 4 - 1))
    mixed = jax.random.permutation(jax.random.fold_in(own, 3), count)
    giver, receiver = mixed[0:count // 2 * 2:2], mixed[1:count // 2 * 2:2]
    margin = jnp.minimum(sizes[giver] - 1, bound - sizes[receiver]) // 2
    margin = jnp.where((giver == ranking[0]) | (receiver == ranking[0]) | (sizes[receiver] == 0), 0, jnp.maximum(margin, 0))
    passed = jax.random.randint(jax.random.fold_in(own, 4), (count // 2,), 0, 1 << 20) % (margin + 1)
    sizes = sizes.at[giver].add(-passed).at[receiver].add(passed)
    items = jnp.searchsorted(jnp.cumsum(sizes), jnp.arange(rows * top), side="right").astype(jnp.int32)
    listing = items.reshape(top, rows).T
    listing = listing[jax.random.permutation(jax.random.fold_in(own, 1), rows)]
    offset_by = jax.random.randint(jax.random.fold_in(own, 2), (rows, 1), 0, top)
    return jnp.take_along_axis(listing, (jnp.arange(top)[None, :] + offset_by) % top, axis=1)


def load_shares(count, total, reach, skew, full):
    weights = [(1 << 20) // math.isqrt(rank ** skew) + 1 for rank in range(1, count + 1)]
    largest = reach if full else min(reach, max(-(-total // count), total * weights[0] // sum(weights)))
    least = 1 if total - largest >= count - 1 else 0
    given, rest = [largest] + [least] * (count - 1), total - largest - least * (count - 1)
    while rest > 0:
        movable = [i for i in range(1, count) if given[i] < largest] or [i for i in range(1, count) if given[i] < reach]
        mass, budget = sum([weights[i] for i in movable]), rest
        for i in movable:
            more = min(reach - given[i], max(1, budget * weights[i] // mass), rest)
            given[i] = given[i] + more
            rest = rest - more
    return np.array(given)


def scatter_about(own_key, shape, spread, bound, shards=(), kind=jnp.bfloat16):
    loudness = steps_of(own_key, shape, shards, -0.22, 0.18) if shards else 1.0
    entries = jax.random.normal(own_key, shape, jnp.float32) * spread * loudness
    return jnp.minimum(jnp.maximum(entries, -bound), bound).astype(kind)


def setup_inputs(seed: int = 0) -> dict:
    seeds = jax.random.split(jax.random.key(seed), 15)
    tokens_in = scatter_about(seeds[0], (TOKENS, D), 1.0, 6.0, ((0, 64), (1, 2)))
    seq_lengths = jax.vmap(lambda own: ragged(own, NSEQ, TOK_GRP, SEQ_MOST, 2))(jax.random.split(seeds[1], GROUPS)).reshape((GROUPS, NSEQ)).astype(jnp.int32)
    expert_ids_keys = jax.random.split(jax.random.fold_in(seeds[2], 1), LAYERS * TOKENS // TOK_GRP)
    expert_ids_turns = jax.random.permutation(jax.random.fold_in(seeds[2], 3), LAYERS * TOKENS // TOK_GRP)
    expert_ids = jax.vmap(lambda own, number: deal_out(jax.random.fold_in(seeds[2], 2), own, number, TOK_GRP, EXPERTS, TOP, CAP, 1))(expert_ids_keys, expert_ids_turns).reshape((LAYERS, TOKENS, TOP))
    gate_weights = jnp.clip(jnp.exp(math.log(0.48) - 1.3862944 * jax.random.uniform(seeds[3], (LAYERS, TOKENS, TOP), jnp.float32) ** steps_of(seeds[3], (LAYERS, TOKENS, TOP), ((1, 64),), -0.2, 0.2)), 0.12, 0.48)
    attention_gain = jnp.clip(1.0 + 0.18 * jax.random.normal(seeds[4], (LAYERS, D), jnp.float32), 0.099609375, 1.8984375).astype(jnp.bfloat16)
    query_weight = scatter_about(seeds[5], (LAYERS, D, QD), D ** -0.5, 0.15625, ((1, 64), (2, 2)))
    key_weight = scatter_about(seeds[6], (LAYERS, D, KD), D ** -0.5, 0.15625, ((1, 64), (2, 2)))
    value_weight = scatter_about(seeds[7], (LAYERS, D, KD), D ** -0.5, 0.15625, ((1, 64), (2, 2)))
    out_weight = scatter_about(seeds[8], (LAYERS, QD, D), (QD // 16) ** -0.5, 0.625, ((1, 2), (2, 64)))
    expert_gain = jnp.clip(1.0 + 0.18 * jax.random.normal(seeds[9], (LAYERS, D), jnp.float32), 0.099609375, 1.8984375).astype(jnp.bfloat16)
    gate_weight = scatter_about(seeds[10], (LAYERS, EXPERTS, D, FF), D ** -0.5, 0.15625, ((1, 16), (3, 2)))
    up_weight = scatter_about(seeds[11], (LAYERS, EXPERTS, D, FF), D ** -0.5, 0.15625, ((1, 16), (3, 2)))
    down_weight = scatter_about(seeds[12], (LAYERS, EXPERTS, FF, D), (FF // 4) ** -0.5, 0.4375, ((1, 16), (2, 2)))
    cotangent = scatter_about(seeds[13], (TOKENS, D), 1.0, 6.0, ((0, 64), (1, 2)))
    return dict(tokens_in=tokens_in, seq_lengths=seq_lengths, expert_ids=expert_ids, gate_weights=gate_weights, attention_gain=attention_gain, query_weight=query_weight, key_weight=key_weight, value_weight=value_weight, out_weight=out_weight, expert_gain=expert_gain, gate_weight=gate_weight, up_weight=up_weight, down_weight=down_weight, cotangent=cotangent)


@jax.custom_vjp
def low(v):
    return lax.optimization_barrier(v.astype(jnp.bfloat16)).astype(jnp.float32)

@jax.custom_vjp
def low_back(v):
    return v

def low_keep(v):
    return (low(v), None)

def low_pass(kept, grad):
    return (grad,)

def back_keep(v):
    return (v, None)

def back_low(kept, grad):
    return (low(grad),)
low.defvjp(low_keep, low_pass)
low_back.defvjp(back_keep, back_low)
epsilon = 1e-06
rope_base = 1000000.0
highest = lax.Precision.HIGHEST

def positions(lengths, row_count):
    seq_ends = jnp.cumsum(lengths).astype(jnp.int32)
    starts = (seq_ends - lengths).astype(jnp.int32)
    places = jnp.arange(row_count, dtype=jnp.int32)
    segment = lax.optimization_barrier(jnp.sum((places[:, None] >= seq_ends[None, :]).astype(jnp.int32), axis=1)).astype(jnp.int32)
    chosen = segment[:, None] == jnp.arange(lengths.shape[0], dtype=jnp.int32)[None, :]
    offset = lax.optimization_barrier(jnp.sum(jnp.where(chosen, starts[None, :], 0), axis=1)).astype(jnp.int32)
    return (segment, (places - offset).astype(jnp.int32))

def rope_tables(places):
    half_dim = HEAD // 2
    frequency = rope_base ** (-2.0 * jnp.arange(half_dim, dtype=jnp.float32) / HEAD)
    angles = places.astype(jnp.float32)[:, None] * frequency[None, :]
    cosine_table = jnp.concatenate([jnp.cos(angles), jnp.cos(angles)], axis=-1)
    sine_table = jnp.concatenate([jnp.sin(angles), jnp.sin(angles)], axis=-1)
    return (cosine_table, sine_table)

def rotate(tensor, cosine_table, sine_table):
    half_dim = tensor.shape[-1] // 2
    turned = jnp.concatenate([-tensor[..., half_dim:], tensor[..., :half_dim]], axis=-1)
    return tensor * cosine_table + turned * sine_table

def rms_scale(values_in, gain_vec):
    return values_in * lax.rsqrt(lax.optimization_barrier(jnp.mean(values_in * values_in, axis=-1, keepdims=True)) + epsilon) * gain_vec

def regroup(tensor):
    return tensor.reshape((GROUPS, TOK_GRP) + tensor.shape[1:])

def attend_group(packed):
    query_block, key_block, value_block, segment, places = packed
    head_share = HEADS // KV_HEADS
    key_heads = jnp.repeat(key_block, head_share, axis=1)
    value_heads = jnp.repeat(value_block, head_share, axis=1)
    raw_scores = jnp.einsum('qhd,khd->hqk', query_block, key_heads, precision=highest)
    scores = low_back(raw_scores * HEAD ** (-0.5))
    allowed = (segment[:, None] == segment[None, :]) & (places[None, :] <= places[:, None])
    scores = jnp.where(allowed[None], scores, -1e+30)
    probability = low(jax.nn.softmax(scores, axis=-1))
    return jnp.einsum('hqk,khd->qhd', probability, value_heads, precision=highest)

def expert_group(packed, normed_rows, half_width):
    slot_token, slot_gate, gate_matrix, up_matrix, down_matrix = packed
    slot_rows = normed_rows[slot_token]
    row_copy = low_back(slot_rows)
    total = jnp.zeros(slot_rows.shape, jnp.float32)
    for half_index in range(N_BLK):
        first_unit = half_index * half_width
        upper_end = first_unit + half_width
        gate_act = low_back(jnp.dot(row_copy, gate_matrix[:, first_unit:upper_end], precision=highest))
        up_act = low_back(jnp.dot(row_copy, up_matrix[:, first_unit:upper_end], precision=highest))
        inner_act = low(jax.nn.silu(gate_act) * up_act)
        total = total + jnp.dot(inner_act, down_matrix[first_unit:upper_end], precision=highest)
    summed = low(low_back(total))
    return summed * slot_gate[:, None]

def slot_tables(expert_rows, gate_rows):
    grouped = expert_rows.reshape(GROUPS, TOK_GRP * TOP)
    onehot = (grouped[:, :, None] == jnp.arange(EXPERTS, dtype=jnp.int32)[None, None, :]).astype(jnp.int32)
    arrival = (lax.optimization_barrier(jnp.sum(jnp.cumsum(onehot, axis=1) * onehot, axis=2)) - 1).astype(jnp.int32)
    group_number = jnp.arange(GROUPS, dtype=jnp.int32)[:, None]
    where_to = (grouped * (GROUPS * CAP) + group_number * CAP + arrival).reshape(-1).astype(jnp.int32)
    owners = (group_number * TOK_GRP + jnp.arange(TOK_GRP * TOP, dtype=jnp.int32)[None, :] // TOP).reshape(-1).astype(jnp.int32)
    slot_token = jnp.zeros((EXPERTS * GROUPS * CAP,), jnp.int32).at[where_to].set(owners)
    slot_gate = jnp.zeros((EXPERTS * GROUPS * CAP,), jnp.float32).at[where_to].set(gate_rows.reshape(-1))
    return (slot_token.reshape(EXPERTS, GROUPS * CAP), slot_gate.reshape(EXPERTS, GROUPS * CAP))

def block(stream, attention_gain, query_weight, key_weight, value_weight, out_weight, expert_gain, gate_weight, up_weight, down_weight, table, segment, places, cosine_table, sine_table):
    normed = low(rms_scale(stream, attention_gain))
    query_heads = low_back(jnp.dot(normed, query_weight, precision=highest)).reshape(TOKENS, HEADS, HEAD)
    key_heads = low_back(jnp.dot(normed, key_weight, precision=highest)).reshape(TOKENS, KV_HEADS, HEAD)
    value_heads = low(low_back(jnp.dot(normed, value_weight, precision=highest))).reshape(TOKENS, KV_HEADS, HEAD)
    query_heads = low(rotate(query_heads, cosine_table[:, None], sine_table[:, None]))
    key_heads = low(rotate(key_heads, cosine_table[:, None], sine_table[:, None]))
    mixed_heads = lax.map(jax.checkpoint(attend_group), (regroup(query_heads), regroup(key_heads), regroup(value_heads), segment, places))
    mixed_heads = low(low_back(mixed_heads.reshape(TOKENS, QD)))
    hidden = stream + low_back(jnp.dot(mixed_heads, out_weight, precision=highest))
    normed_exp = low(rms_scale(hidden, expert_gain))
    slot_token, slot_gate = table

    def serve(packed):
        return expert_group(packed, normed_exp, FF // N_BLK)
    weighted = lax.map(jax.checkpoint(serve), (slot_token, slot_gate, gate_weight, up_weight, down_weight))
    mixture = jnp.zeros_like(hidden).at[slot_token.reshape(-1)].add(weighted.reshape(-1, D))
    return hidden + mixture

def reference(tokens_in, seq_lengths, expert_ids, gate_weights, attention_gain, query_weight, key_weight, value_weight, out_weight, expert_gain, gate_weight, up_weight, down_weight, cotangent):
    segment, places = jax.vmap(lambda lengths: positions(lengths, TOK_GRP))(seq_lengths)
    cosine_table, sine_table = rope_tables(places.reshape(-1))
    tables = [slot_tables(expert_ids[layer_index], gate_weights[layer_index].astype(jnp.float32)) for layer_index in range(LAYERS)]

    def forward(stream, attention_gain, query_weight, key_weight, value_weight, out_weight, expert_gain, gate_weight, up_weight, down_weight):
        for layer_index in range(LAYERS):
            stream = block(stream, attention_gain[layer_index], query_weight[layer_index], key_weight[layer_index], value_weight[layer_index], out_weight[layer_index], expert_gain[layer_index], gate_weight[layer_index], up_weight[layer_index], down_weight[layer_index], tables[layer_index], segment, places, cosine_table, sine_table)
        return stream
    floats = (tokens_in.astype(jnp.float32), attention_gain.astype(jnp.float32), query_weight.astype(jnp.float32), key_weight.astype(jnp.float32), value_weight.astype(jnp.float32), out_weight.astype(jnp.float32), expert_gain.astype(jnp.float32), gate_weight.astype(jnp.float32), up_weight.astype(jnp.float32), down_weight.astype(jnp.float32))
    result, pull = jax.vjp(forward, *floats)
    grads = pull(cotangent.astype(jnp.float32))
    return (result.astype(jnp.bfloat16), grads[0], grads[1], grads[2], grads[3], grads[4], grads[5], grads[6], grads[7], grads[8], grads[9])
```

```python
import functools

import jax
import jax.numpy as jnp
from jax import lax
from jax.experimental import pallas as pl
from jax.experimental.pallas import tpu as pltpu
from jax.sharding import PartitionSpec as P

HEAD = 128
TOP = 4
LAYERS = 2
F32 = jnp.float32
BF = jnp.bfloat16
MESH = pl.DeviceIdType.MESH

epsilon = 1e-06
rope_base = 1000000.0

TOKENS = 128
WIDE = 1536
HALF = WIDE // 2
HEADS = 6
HIDDEN = 384
PEERS = 16
CAP = 24
SLOTS = PEERS * CAP
SHARD = 24
QKV = 1024
OUT = 768
COLS = QKV + OUT + 128
PART = COLS // 3
ORDERS = ((0, 1, 2), (1, 2, 0), (2, 0, 1))
LIMIT = 60 << 20

ANY = pl.BlockSpec(memory_space=pl.ANY)
VMEM = pl.BlockSpec(memory_space=pltpu.VMEM)


def dot(a, b, ca=1, cb=0):
    return lax.dot_general(a, b, (((ca,), (cb,)), ((), ())), preferred_element_type=F32)


def coords():
    ex = lax.axis_index("expert")
    return [lax.axis_index("dp"), lax.div(ex, 4), lax.rem(ex, 4)]


def shifted(xyz, axis, by):
    moved = list(xyz)
    moved[axis] = lax.rem(xyz[axis] + by, 4)
    return moved


def device_at(xyz, core):
    return (xyz[0], xyz[1] * 4 + xyz[2], core)


def partner():
    return (lax.axis_index("dp"), lax.axis_index("expert"), 1 - lax.axis_index("blk"))


def greet(devices):
    barrier = pltpu.get_barrier_semaphore()
    for device in devices:
        pl.semaphore_signal(barrier, inc=1, device_id=device, device_id_type=MESH)
    pl.semaphore_wait(barrier, len(devices))


def peer(step):
    dp, ex, core = (lax.axis_index(a) for a in ("dp", "expert", "blk"))
    return (dp, lax.rem(ex + step, PEERS), core)


def greet_peers():
    greet([peer(d) for d in range(1, PEERS)] + [partner()])


class Sender:
    def __init__(self, send, recv):
        self.send, self.recv, self.at = send, recv, 0

    def start(self, src, dst, device):
        assert self.at < self.send.shape[0]
        copy = pltpu.make_async_remote_copy(
            src_ref=src,
            dst_ref=dst,
            send_sem=self.send.at[self.at],
            recv_sem=self.recv.at[self.at],
            device_id=device,
            device_id_type=MESH,
        )
        self.at += 1
        copy.start()
        return copy


def exchange_copy(src, dst, send, recv, step):
    me = lax.axis_index("expert")
    target = peer(step)
    return pltpu.make_async_remote_copy(
        src_ref=src.at[target[1]],
        dst_ref=dst.at[me],
        send_sem=send.at[step],
        recv_sem=recv.at[step],
        device_id=target,
        device_id_type=MESH,
    )


def exchange_start(src, dst, send, recv):
    me = lax.axis_index("expert")

    def begin(step, carry):
        exchange_copy(src, dst, send, recv, step).start()
        return carry

    lax.fori_loop(1, PEERS, begin, 0)
    pltpu.make_async_copy(src.at[me], dst.at[me], send.at[0]).start()


def exchange_wait(src, dst, send, recv):
    me = lax.axis_index("expert")

    def end(step, carry):
        exchange_copy(src, dst, send, recv, step).wait()
        return carry

    lax.fori_loop(1, PEERS, end, 0)
    pltpu.make_async_copy(src.at[me], dst.at[me], send.at[0]).wait()


def rows_of(ref):
    return ref[...].astype(F32).reshape(SLOTS, WIDE).astype(BF)


def store_rows(ref, rows):
    ref[...] = rows.reshape(PEERS, CAP, WIDE).astype(BF)


def slot_matrices(ids, weights):
    core = lax.axis_index("blk")
    expert = 2 * lax.broadcasted_iota(jnp.int32, (PEERS, TOKENS), 0) + core
    chosen = jnp.zeros((PEERS, TOKENS), F32)
    gate = jnp.zeros((PEERS, TOKENS), F32)
    for j in range(TOP):
        hit = jnp.where(ids[j : j + 1, :] == expert, 1.0, 0.0)
        chosen = chosen + hit
        gate = gate + hit * weights[j : j + 1, :]
    before = lax.broadcasted_iota(jnp.int32, (TOKENS, TOKENS), 0) < lax.broadcasted_iota(
        jnp.int32, (TOKENS, TOKENS), 1
    )
    rank = dot(chosen.astype(BF), jnp.where(before, 1.0, 0.0).astype(BF))
    rank = jnp.where(chosen > 0.0, rank, -1.0)
    shape = (PEERS, CAP, TOKENS)
    place = lax.broadcasted_iota(jnp.int32, shape, 1).astype(F32)
    onehot = jnp.where(jnp.broadcast_to(rank[:, None, :], shape) == place, 1.0, 0.0)
    weighted = onehot * jnp.broadcast_to(gate[:, None, :], shape)
    return onehot.reshape(SLOTS, TOKENS), weighted.reshape(SLOTS, TOKENS)


def halves(value):
    high = value.astype(BF)
    return high, (value - high.astype(F32)).astype(BF)


def combine(weighted, rows):
    high, low = halves(weighted)
    return dot(high, rows, 0, 0) + dot(low, rows, 0, 0)


def gain_rows(w_ref):
    unit = jnp.where(
        lax.broadcasted_iota(jnp.int32, (8, 128), 0) == lax.broadcasted_iota(jnp.int32, (8, 128), 1),
        1.0,
        0.0,
    ).astype(BF)
    rows = dot(unit, w_ref[:, QKV + OUT : COLS], 1, 1)
    return rows[0:1, :], rows[1:2, :]


def inverse_norm(u):
    return lax.rsqrt(jnp.mean(u * u, axis=-1, keepdims=True) + epsilon)


def norm_back(u, inverse, gain, upstream):
    scaled = upstream * gain
    inward = inverse * scaled - u * (inverse * inverse * inverse) * jnp.mean(
        u * scaled, axis=-1, keepdims=True
    )
    return inward, upstream * u * inverse


def rotate(u, cos, sin):
    return u * cos + pltpu.roll(u, HEAD // 2, 1) * sin


def unrotate(u, cos, sin):
    return u * cos - pltpu.roll(u, HEAD // 2, 1) * sin


def head_of(value, h):
    return value[:, h * HEAD : (h + 1) * HEAD]


def attention(x, gain, w_ref, cos, sin, allow, n_ref, qkv_ref, prob_ref, o_ref):
    n = (x * inverse_norm(x) * gain).astype(BF)
    n_ref[...] = n
    flat = dot(n, w_ref[:, 0:QKV])
    for h in range(HEADS + 1):
        qkv_ref[:, h * HEAD : (h + 1) * HEAD] = rotate(head_of(flat, h), cos, sin).astype(BF)
    qkv_ref[:, (HEADS + 1) * HEAD :] = flat[:, (HEADS + 1) * HEAD :].astype(BF)
    key = qkv_ref[:, HEADS * HEAD : (HEADS + 1) * HEAD]
    value = qkv_ref[:, (HEADS + 1) * HEAD :]
    for h in range(HEADS):
        scores = dot(qkv_ref[:, h * HEAD : (h + 1) * HEAD], key, 1, 1) * HEAD ** (-0.5)
        scores = jnp.where(allow > 0.0, scores, -1e30)
        weight = jnp.exp(scores - jnp.max(scores, axis=-1, keepdims=True))
        prob = weight / jnp.sum(weight, axis=-1, keepdims=True)
        prob_ref[h] = prob
        o_ref[:, h * HEAD : (h + 1) * HEAD] = dot(prob.astype(BF), value).astype(BF)
    return dot(o_ref[...], w_ref[:, QKV : QKV + OUT], 1, 1)


def expert_weight_copies(layer, own, other, held, sem):
    core = lax.axis_index("blk")
    copies = []
    for i in range(3):
        copies.append(pltpu.make_async_copy(own[i].at[layer, core], held[i].at[0], sem.at[2 * i]))
        copies.append(pltpu.make_async_copy(other[i].at[layer], held[i].at[1], sem.at[2 * i + 1]))
    for copy in copies:
        copy.start()
    return copies


def expert_forward(rows, held, a_ref, b_ref):
    gate, up, down = held
    total = None
    for c in range(2):
        a = dot(rows, gate[c])
        b = dot(rows, up[c])
        a_ref[c] = a
        b_ref[c] = b
        z = (a / (1.0 + jnp.exp(-a)) * b).astype(BF)
        term = dot(z, down[c])
        total = term if total is None else total + term
    return total


def expert_backward(dy, held, a_ref, b_ref, z_ref, d_ref):
    gate, up, down = held
    total = None
    for c in range(2):
        a = a_ref[c]
        b = b_ref[c]
        sg = 1.0 / (1.0 + jnp.exp(-a))
        z_ref[:, c * HIDDEN : (c + 1) * HIDDEN] = (a * sg * b).astype(BF)
        dz = dot(dy, down[c], 1, 1)
        da = (dz * b * sg * (1.0 + a * (1.0 - sg))).astype(BF)
        db = (dz * a * sg).astype(BF)
        d_ref[:, 2 * c * HIDDEN : (2 * c + 1) * HIDDEN] = da
        d_ref[:, (2 * c + 1) * HIDDEN : (2 * c + 2) * HIDDEN] = db
        term = dot(da, gate[c], 1, 1) + dot(db, up[c], 1, 1)
        total = term if total is None else total + term
    return total


def expert_gradients(rows_ref, dy_ref, z_ref, d_ref, grad_ref):
    for q in range(4):
        columns = slice(q * HIDDEN, (q + 1) * HIDDEN)
        both = dot(rows_ref[:, columns], d_ref[...], 0, 0)
        for c in range(2):
            for i in range(2):
                at = (2 * c + i) * HIDDEN
                grad_ref[q, 3 * c + i] = both[:, at : at + HIDDEN].astype(BF)
        low = dot(z_ref[...], dy_ref[:, columns], 0, 0)
        for c in range(2):
            grad_ref[q, 3 * c + 2] = low[c * HIDDEN : (c + 1) * HIDDEN].astype(BF)


def gather_kernel(
    shard, tok, cot, gate, up, down, w0, w1, tok_all, cot_all, gate_o, up_o, down_o, send, recv, local
):
    xyz, core = coords(), lax.axis_index("blk")
    ring = [device_at(shifted(xyz, axis, by), core) for axis in range(3) for by in (1, 2, 3)]
    greet(ring + [partner()])
    sender = Sender(send, recv)
    whole = (w0, w1)
    mine = pl.ds(pl.multiple_of(core * HALF, HALF), HALF)
    here = [
        pltpu.make_async_copy(shard.at[l], whole[l].at[xyz[0], xyz[1], xyz[2]], local.at[l])
        for l in range(LAYERS)
    ]
    here.append(pltpu.make_async_copy(tok, tok_all.at[:, mine], local.at[2]))
    here.append(pltpu.make_async_copy(cot, cot_all.at[:, mine], local.at[3]))
    for copy in here:
        copy.start()
    others = []

    def slab(l, p, known, at, half=None):
        index = list(at)
        for axis in known:
            index[axis] = pl.ds(0, 4)
        if half is not None:
            index[known[0]] = pl.ds(2 * half, 2)
        return whole[l].at[index[0], index[1], index[2], :, pl.ds(p * PART, PART)]

    first = []
    for l in range(LAYERS):
        for p, order in enumerate(ORDERS):
            source = shard.at[l, :, pl.ds(p * PART, PART)]
            for by in (1, 3, 2):
                target = device_at(shifted(xyz, order[0], by), core)
                first.append(sender.start(source, slab(l, p, (), xyz), target))
    others.append(sender.start(tok, tok_all.at[:, mine], partner()))
    others.append(sender.start(cot, cot_all.at[:, mine], partner()))
    for ref, to in ((gate, gate_o), (up, up_o), (down, down_o)):
        for l in range(LAYERS):
            others.append(sender.start(ref.at[l, 1 - core], to.at[l], partner()))
    for copy in here + first:
        copy.wait()
    for stage in (1, 2):
        nears = []
        for l in range(LAYERS):
            for p, order in enumerate(ORDERS):
                known, axis = order[:stage], order[stage]
                block = slab(l, p, known, xyz)
                nears.append(
                    [
                        sender.start(block, block, device_at(shifted(xyz, axis, by), core))
                        for by in (1, 3)
                    ]
                )
        relays = []
        for l in range(LAYERS):
            for p, order in enumerate(ORDERS):
                known, axis = order[:stage], order[stage]
                for copy, by, half in zip(nears[l * 3 + p], (1, 3), (0, 1)):
                    copy.wait_recv()
                    block = slab(l, p, known, shifted(xyz, axis, 4 - by), half)
                    relays.append(
                        sender.start(block, block, device_at(shifted(xyz, axis, by), core))
                    )
        for pair in nears:
            for copy in pair:
                copy.wait_send()
        for copy in relays:
            copy.wait()
    for copy in others:
        copy.wait()


def attention_part(x, refs, part, theirs, pair):
    gain_a, gain_e = gain_rows(refs["w"])
    part[...] = attention(
        x,
        gain_a,
        refs["w"],
        refs["cos"][...],
        refs["sin"][...],
        refs["allow"][...],
        refs["n"],
        refs["qkv"],
        refs["prob"],
        refs["o"],
    )
    copy = pair.start(part, theirs, partner())
    copy.wait()
    h = x + (part[...] + theirs[...])
    refs["h"][...] = h
    return h, (h * inverse_norm(h) * gain_e).astype(BF)


FRONT_OUT = (
    ("h", (TOKENS, WIDE), F32),
    ("n", (TOKENS, WIDE), BF),
    ("qkv", (TOKENS, QKV), BF),
    ("prob", (HEADS, TOKENS, TOKENS), F32),
    ("o", (TOKENS, OUT), BF),
    ("onehot", (SLOTS, TOKENS), BF),
    ("weighted", (SLOTS, TOKENS), F32),
)
HELD = [
    pltpu.VMEM((2, WIDE, HIDDEN), BF),
    pltpu.VMEM((2, WIDE, HIDDEN), BF),
    pltpu.VMEM((2, HIDDEN, WIDE), BF),
    pltpu.SemaphoreType.DMA((6,)),
]
BLOCKS = pltpu.VMEM((PEERS, CAP, WIDE), BF)
PLANE = pltpu.VMEM((TOKENS, WIDE), F32)
EACH = pltpu.SemaphoreType.DMA((PEERS,))
PAIRED = pltpu.SemaphoreType.DMA((4,))


def forward_kernel(
    layer, x_ref, w_any, cos, sin, allow, ids, weights, gate, up, down, gate_o, up_o, down_o,
    h, n, qkv, prob, o, onehot, weighted, rows, a, b, out,
    w, w_sem, held_g, held_u, held_d, held_sem, sent, came, back, part0, theirs0, part1, theirs1,
    send0, recv0, send1, recv1, pair_send, pair_recv,
):
    load = pltpu.make_async_copy(w_any, w, w_sem)
    load.start()
    held = (held_g, held_u, held_d)
    loads = expert_weight_copies(layer, (gate, up, down), (gate_o, up_o, down_o), held, held_sem)
    greet_peers()
    pair = Sender(pair_send, pair_recv)
    refs = dict(w=w, cos=cos, sin=sin, allow=allow, h=h, n=n, qkv=qkv, prob=prob, o=o)
    hot, heavy = slot_matrices(ids[...], weights[...])
    onehot[...] = hot.astype(BF)
    weighted[...] = heavy
    load.wait()
    x = x_ref[...].astype(F32)
    _, m = attention_part(x, refs, part0, theirs0, pair)
    store_rows(sent, dot(onehot[...], m))
    exchange_start(sent, came, send0, recv0)
    for copy in loads:
        copy.wait()
    exchange_wait(sent, came, send0, recv0)
    rows[...] = rows_of(came)
    store_rows(sent, expert_forward(rows[...], held, a, b))
    exchange_start(sent, back, send1, recv1)
    exchange_wait(sent, back, send1, recv1)
    part1[...] = combine(weighted[...], rows_of(back))
    pair.start(part1, theirs1, partner()).wait()
    out[...] = h[...] + (part1[...] + theirs1[...])


def middle_kernel(
    layer, x_ref, cot, w_any, cos, sin, allow, ids, weights, gate, up, down, gate_o, up_o, down_o,
    h, n, qkv, prob, o, onehot, weighted, y_rows, m_back, grads,
    w, w_sem, held_g, held_u, held_d, held_sem, sent, came, sent_g, came_g, part0, theirs0,
    rows, dy, a, b, z, d, send0, recv0, send1, recv1, pair_send, pair_recv,
):
    load = pltpu.make_async_copy(w_any, w, w_sem)
    load.start()
    held = (held_g, held_u, held_d)
    loads = expert_weight_copies(layer, (gate, up, down), (gate_o, up_o, down_o), held, held_sem)
    greet_peers()
    pair = Sender(pair_send, pair_recv)
    refs = dict(w=w, cos=cos, sin=sin, allow=allow, h=h, n=n, qkv=qkv, prob=prob, o=o)
    hot, heavy = slot_matrices(ids[...], weights[...])
    onehot[...] = hot.astype(BF)
    weighted[...] = heavy
    slot_weight = jnp.sum(heavy, axis=1, keepdims=True)
    store_rows(sent_g, dot(onehot[...], cot[...]) * slot_weight)
    exchange_start(sent_g, came_g, send1, recv1)
    load.wait()
    _, m = attention_part(x_ref[...], refs, part0, theirs0, pair)
    store_rows(sent, dot(onehot[...], m))
    exchange_start(sent, came, send0, recv0)
    for copy in loads:
        copy.wait()
    exchange_wait(sent_g, came_g, send1, recv1)
    dy[...] = rows_of(came_g)
    exchange_wait(sent, came, send0, recv0)
    rows[...] = rows_of(came)
    store_rows(y_rows, expert_forward(rows[...], held, a, b))
    store_rows(m_back, expert_backward(dy[...], held, a, b, z, d))
    expert_gradients(rows, dy, z, d, grads)


def expert_kernel(
    layer, g_ref, onehot, weighted, rows, a, b, gate, up, down, gate_o, up_o, down_o,
    m_back, grads,
    held_g, held_u, held_d, held_sem, sent, came, dy, z, d, send0, recv0,
):
    held = (held_g, held_u, held_d)
    loads = expert_weight_copies(layer, (gate, up, down), (gate_o, up_o, down_o), held, held_sem)
    slot_weight = jnp.sum(weighted[...], axis=1, keepdims=True)
    high, low = halves(g_ref[...])
    store_rows(sent, (dot(onehot[...], high) + dot(onehot[...], low)) * slot_weight)
    greet([peer(s) for s in range(1, PEERS)])
    exchange_start(sent, came, send0, recv0)
    for copy in loads:
        copy.wait()
    exchange_wait(sent, came, send0, recv0)
    dy[...] = rows_of(came)
    store_rows(m_back, expert_backward(dy[...], held, a, b, z, d))
    expert_gradients(rows, dy, z, d, grads)


def back_kernel(
    last, x_ref, g_ref, w_any, cos, sin, h, n, qkv, prob, o, onehot, weighted, m_back, y_rows,
    out, w_grad, block_out,
    w, w_sem, came, back, part0, theirs0, part1, theirs1, part2, theirs2, lin,
    send0, recv0, send1, recv1, pair_send, pair_recv,
):
    load = pltpu.make_async_copy(w_any, w, w_sem)
    load.start()
    greet_peers()
    pair = Sender(pair_send, pair_recv)
    core = lax.axis_index("blk")
    exchange_start(m_back, came, send0, recv0)
    if last:
        exchange_start(y_rows, back, send1, recv1)
    load.wait()
    gain_a, gain_e = gain_rows(w)
    exchange_wait(m_back, came, send0, recv0)
    part0[...] = dot(onehot[...], rows_of(came), 0, 0)
    pair.start(part0, theirs0, partner()).wait()
    dm = part0[...] + theirs0[...]
    hidden = h[...]
    inward, gain_grad_e = norm_back(hidden, inverse_norm(hidden), gain_e, dm)
    gh = g_ref[...].astype(F32) + inward
    out[...] = gh
    da = gh.astype(BF)
    w_grad[:, QKV : QKV + OUT] = dot(da, o[...], 0, 0).astype(BF)
    do = dot(da, w[:, QKV : QKV + OUT]).astype(BF)
    key = qkv[:, HEADS * HEAD : (HEADS + 1) * HEAD]
    value = qkv[:, (HEADS + 1) * HEAD :]
    scale = HEAD ** (-0.5)
    key_grad, value_grad = None, None
    cosine, sine = cos[...], sin[...]
    for i in range(HEADS):
        prob_i = prob[i]
        do_i = head_of(do, i)
        q_i = qkv[:, i * HEAD : (i + 1) * HEAD]
        dprob = dot(do_i, value, 1, 1)
        centre = jnp.sum(prob_i * dprob, axis=-1, keepdims=True)
        ds = (prob_i * (dprob - centre)).astype(BF)
        dq = dot(ds, key) * scale
        lin[:, i * HEAD : (i + 1) * HEAD] = unrotate(dq, cosine, sine).astype(BF)
        dk = dot(ds, q_i, 0, 0)
        dv = dot(prob_i.astype(BF), do_i, 0, 0)
        key_grad = dk if key_grad is None else key_grad + dk
        value_grad = dv if value_grad is None else value_grad + dv
    lin[:, HEADS * HEAD : (HEADS + 1) * HEAD] = unrotate(key_grad * scale, cosine, sine).astype(BF)
    lin[:, (HEADS + 1) * HEAD :] = value_grad.astype(BF)
    part1[...] = dot(lin[...], w[:, 0:QKV], 1, 1)
    across = pair.start(part1, theirs1, partner())
    w_grad[:, 0:QKV] = dot(n[...], lin[...], 0, 0).astype(BF)
    if last:
        exchange_wait(y_rows, back, send1, recv1)
        mixed = combine(weighted[...], rows_of(back))
        theirs_first = core == 1
        part2[...] = jnp.where(theirs_first, mixed[:, :HALF], mixed[:, HALF:])
        second = pair.start(part2, theirs2, partner())
        own = jnp.where(theirs_first, mixed[:, HALF:], mixed[:, :HALF])
        kept = jnp.where(theirs_first, h[:, HALF:], h[:, :HALF])
        second.wait()
        block_out[...] = (kept + (own + theirs2[...])).astype(BF)
    else:
        block_out[...] = jnp.zeros(block_out.shape, BF)
    across.wait()
    dn = part1[...] + theirs1[...]
    x = x_ref[...].astype(F32)
    inward, gain_grad_a = norm_back(x, inverse_norm(x), gain_a, dn)
    out[...] = out[...] + inward
    lane = lax.broadcasted_iota(jnp.int32, (TOKENS, 128), 1)
    total = jnp.zeros((WIDE, 128), F32)
    for i, grad in enumerate((gain_grad_a, gain_grad_e)):
        pick = jnp.where(lane == i, 1.0, 0.0).astype(BF)
        for piece in halves(grad):
            total = total + dot(piece, pick, 0, 0)
    w_grad[:, QKV + OUT :] = total.astype(BF)


def ring_start(sender, block, near, relay, plus, minus):
    relays = [
        sender.start(block(2, 0), relay(0), plus),
        sender.start(block(2, 1), relay(1), minus),
    ]
    plain = [
        sender.start(block(1, 1), near(0, 1), plus),
        sender.start(block(3, 0), near(1, 0), minus),
    ]
    return relays, plain


def ring_relay(sender, block, near, relay, plus, minus, relays):
    sums = []
    for side, (by, target) in enumerate(((1, plus), (3, minus))):
        relays[side].wait_recv()
        held = relay(side)
        held[...] = (block(by, side)[...].astype(F32) + held[...].astype(F32)).astype(BF)
        sums.append(sender.start(held, near(side, side), target))
    return sums


def rings(sender, stages):
    begun = [ring_start(sender, *stage) for stage in stages]
    sums = [ring_relay(sender, *stage, relays) for stage, (relays, _) in zip(stages, begun)]
    for (relays, plain), added in zip(begun, sums):
        for copy in plain + added:
            copy.wait()
        for copy in relays:
            copy.wait_send()


def scatter_kernel(
    grad0, grad1, out0, out1, near1, relay1, sum1, near2, relay2, sum2, near3, send, recv
):
    xyz, core = coords(), lax.axis_index("blk")
    greet([device_at(shifted(xyz, axis, by), core) for axis in range(3) for by in (1, 2, 3)])
    sender = Sender(send, recv)
    grads, outs = (grad0, grad1), (out0, out1)
    jobs = [(l, p) for l in range(LAYERS) for p in range(3)]
    sides = [
        [device_at(shifted(xyz, axis, by), core) for by in (1, 3)] for axis in range(3)
    ]

    def first(l, p):
        axis, split = ORDERS[p][0], ORDERS[p][1]
        left = [a for a in range(3) if a != axis]
        lanes = pl.ds(p * PART, PART)

        def block(by, half):
            index = [pl.ds(0, 4)] * 3
            index[axis] = shifted(xyz, axis, by)[axis]
            if half is not None:
                index[split] = pl.ds(2 * half, 2)
            return grads[l].at[index[0], index[1], index[2], :, lanes]

        def near(side, half):
            index = [pl.ds(2 * half, 2) if a == split else pl.ds(0, 4) for a in left]
            return near1.at[l, p, side, index[0], index[1]]

        def relay(side):
            index = [pl.ds(0, 2) if a == split else pl.ds(0, 4) for a in left]
            return relay1.at[l, p, side, index[0], index[1]]

        return block, near, relay, *sides[axis]

    def second(l, p):
        axis, split = ORDERS[p][1], ORDERS[p][2]
        left = [a for a in range(3) if a != ORDERS[p][0]]

        def block(by, half):
            rest = pl.ds(0, 4) if half is None else pl.ds(2 * half, 2)
            index = [shifted(xyz, axis, by)[axis] if a == axis else rest for a in left]
            return sum1.at[l, p, index[0], index[1]]

        def near(side, half):
            return near2.at[l, p, side, pl.ds(2 * half, 2)]

        def relay(side):
            return relay2.at[l, p, side]

        return block, near, relay, *sides[axis]

    rings(sender, [first(l, p) for l, p in jobs])
    for l, p in jobs:
        mine = first(l, p)[0](0, None)
        sum1[l, p] = (
            mine[...].astype(F32) + near1[l, p, 0].astype(F32) + near1[l, p, 1].astype(F32)
        ).astype(BF)
    rings(sender, [second(l, p) for l, p in jobs])
    for l, p in jobs:
        mine = second(l, p)[0](0, None)
        sum2[l, p] = (
            mine[...].astype(F32) + near2[l, p, 0].astype(F32) + near2[l, p, 1].astype(F32)
        ).astype(BF)
    copies = []
    for l, p in jobs:
        axis = ORDERS[p][2]
        for by in (1, 3, 2):
            there = shifted(xyz, axis, by)
            copies.append(
                sender.start(sum2.at[l, p, there[axis]], near3.at[l, p, by - 1], device_at(there, core))
            )
    for copy in copies:
        copy.wait()
    for l, p in jobs:
        total = sum2[l, p, xyz[ORDERS[p][2]]].astype(F32)
        for side in range(3):
            total = total + near3[l, p, side].astype(F32)
        outs[l][:, p * PART : (p + 1) * PART] = total


def kernel_call(kernel, cid, outs, scratch, operands):
    return pl.pallas_call(
        kernel,
        out_shape=[jax.ShapeDtypeStruct(o[0], o[1]) for o in outs],
        in_specs=[ANY if stays else VMEM for _, stays in operands],
        out_specs=[ANY if o[2] else VMEM for o in outs],
        scratch_shapes=scratch,
        compiler_params=pltpu.CompilerParams(
            collective_id=cid, has_side_effects=True, vmem_limit_bytes=LIMIT
        ),
    )(*[array for array, _ in operands])


def sems(*counts):
    return [pltpu.SemaphoreType.DMA((n,)) for n in counts]


def positions(lengths, row_count):
    seq_ends = jnp.cumsum(lengths)
    starts = seq_ends - lengths
    places = jnp.arange(row_count, dtype=jnp.int32)
    segment = jnp.sum((places[:, None] >= seq_ends[None, :]).astype(jnp.int32), axis=1)
    chosen = segment[:, None] == jnp.arange(lengths.shape[0], dtype=jnp.int32)[None, :]
    offset = jnp.sum(jnp.where(chosen, starts[None, :], 0), axis=1)
    return (segment, places - offset)


def rope_tables(places):
    half_dim = HEAD // 2
    frequency = rope_base ** (-2.0 * jnp.arange(half_dim, dtype=F32) / HEAD)
    angles = places.astype(F32)[:, None] * frequency[None, :]
    cos, sin = jnp.cos(angles), jnp.sin(angles)
    return jnp.concatenate([cos, cos], axis=-1), jnp.concatenate([-sin, sin], axis=-1)


def per_device(
    tokens_in,
    seq_lengths,
    expert_ids,
    gate_weights,
    attention_gain,
    query_weight,
    key_weight,
    value_weight,
    out_weight,
    expert_gain,
    gate_weight,
    up_weight,
    down_weight,
    cotangent,
):
    core = lax.axis_index("blk")
    gains = jnp.stack([attention_gain, expert_gain], axis=-1)
    shard = jnp.concatenate(
        [
            query_weight,
            key_weight,
            value_weight,
            jnp.swapaxes(out_weight, 1, 2),
            jnp.pad(gains, ((0, 0), (0, 0), (0, 126))),
        ],
        axis=2,
    )
    cube = (4, 4, 4, SHARD, COLS)
    w0, w1, tokens, cot, gate_o, up_o, down_o = kernel_call(
        gather_kernel,
        1,
        [
            (cube, BF, True),
            (cube, BF, True),
            ((TOKENS, WIDE), BF, False),
            ((TOKENS, WIDE), BF, False),
            ((LAYERS, WIDE, HIDDEN), BF, True),
            ((LAYERS, WIDE, HIDDEN), BF, True),
            ((LAYERS, HIDDEN, WIDE), BF, True),
        ],
        sems(80, 80, 4),
        [
            (shard, False),
            (tokens_in, False),
            (cotangent, False),
            (gate_weight, True),
            (up_weight, True),
            (down_weight, True),
        ],
    )
    whole = [w.reshape(WIDE, COLS) for w in (w0, w1)]
    experts = [(a, True) for a in (gate_weight, up_weight, down_weight, gate_o, up_o, down_o)]
    segment, places = positions(seq_lengths[0], TOKENS)
    cos, sin = rope_tables(places)
    allow = (segment[:, None] == segment[None, :]) & (places[None, :] <= places[:, None])
    tables = [(cos, False), (sin, False), (allow.astype(F32), False)]
    slots = [
        [(expert_ids[l].T, False), (gate_weights[l].T, False)] for l in range(LAYERS)
    ]
    front = [(shape, kind, False) for _, shape, kind in FRONT_OUT]
    names = [name for name, _, _ in FRONT_OUT]
    inner = ((2, SLOTS, HIDDEN), F32, False)
    block = ((PEERS, CAP, WIDE), BF, False)
    plane = ((TOKENS, WIDE), F32, False)
    grads = ((4, 6, HIDDEN, HIDDEN), BF, False)
    load = [pltpu.VMEM((WIDE, COLS), BF), pltpu.SemaphoreType.DMA]
    rows_in = pltpu.VMEM((SLOTS, WIDE), BF)

    *kept0, rows0, a0, b0, stream = kernel_call(
        functools.partial(forward_kernel, 0),
        2,
        front + [((SLOTS, WIDE), BF, False), inner, inner, plane],
        load
        + HELD
        + [BLOCKS] * 3
        + [PLANE] * 4
        + sems(PEERS, PEERS, PEERS, PEERS, 4, 4),
        [(tokens, False), (whole[0], True)] + tables + slots[0] + experts,
    )
    kept0 = dict(zip(names, kept0))
    *kept1, y_rows, m_back1, grads1 = kernel_call(
        functools.partial(middle_kernel, 1),
        3,
        front + [block, block, grads],
        load
        + HELD
        + [BLOCKS] * 4
        + [PLANE] * 2
        + [rows_in, rows_in]
        + [pltpu.VMEM((2, SLOTS, HIDDEN), F32)] * 2
        + [pltpu.VMEM((SLOTS, 2 * HIDDEN), BF), pltpu.VMEM((SLOTS, 4 * HIDDEN), BF)]
        + sems(PEERS, PEERS, PEERS, PEERS, 4, 4),
        [(stream, False), (cot, False), (whole[1], True)] + tables + slots[1] + experts,
    )
    kept1 = dict(zip(names, kept1))

    def back(last, cid, x, upstream, w, kept, m_back, y_rows):
        fields = ("h", "n", "qkv", "prob", "o", "onehot", "weighted")
        return kernel_call(
            functools.partial(back_kernel, last),
            cid,
            [plane, ((WIDE, COLS), BF, False), ((TOKENS, HALF), BF, False)],
            load
            + [BLOCKS] * 2
            + [PLANE] * 4
            + [pltpu.VMEM((TOKENS, HALF), F32)] * 2
            + [pltpu.VMEM((TOKENS, QKV), BF)]
            + sems(PEERS, PEERS, PEERS, PEERS, 4, 4),
            [(x, False), (upstream, False), (w, True)]
            + tables[:2]
            + [(kept[f], False) for f in fields]
            + [(m_back, False), (y_rows, False)],
        )

    def summed(grads):
        total = lax.psum_scatter(grads, "dp", scatter_dimension=0, tiled=True)[0]
        theirs = lax.ppermute(total[3:], "blk", [(0, 1), (1, 0)])
        first = jnp.where(core == 0, total[:3], theirs).astype(F32)
        second = jnp.where(core == 0, theirs, total[:3]).astype(F32)
        return [jnp.stack([first[i], second[i]]) for i in range(3)]

    expert1 = summed(grads1)
    upstream, w_grad1, block_out = back(
        True, 4, stream, cot, whole[1], kept1, m_back1, y_rows
    )
    m_back0, grads0 = kernel_call(
        functools.partial(expert_kernel, 0),
        5,
        [block, grads],
        HELD
        + [BLOCKS] * 2
        + [rows_in]
        + [pltpu.VMEM((SLOTS, 2 * HIDDEN), BF), pltpu.VMEM((SLOTS, 4 * HIDDEN), BF)]
        + sems(PEERS, PEERS),
        [(upstream, False), (kept0["onehot"], False), (kept0["weighted"], False)]
        + [(rows0, False), (a0, False), (b0, False)]
        + experts,
    )
    expert0 = summed(grads0)
    upstream, w_grad0, _ = back(False, 6, tokens, upstream, whole[0], kept0, m_back0, m_back0)
    ring = (LAYERS, 3, 2, 4, 4, SHARD, PART)
    att0, att1 = kernel_call(
        scatter_kernel,
        7,
        [((SHARD, COLS), F32, False)] * 2,
        [
            pltpu.VMEM(ring, BF),
            pltpu.VMEM(ring, BF),
            pltpu.VMEM((LAYERS, 3, 4, 4, SHARD, PART), BF),
            pltpu.VMEM((LAYERS, 3, 2, 4, SHARD, PART), BF),
            pltpu.VMEM((LAYERS, 3, 2, 2, SHARD, PART), BF),
            pltpu.VMEM((LAYERS, 3, 4, SHARD, PART), BF),
            pltpu.VMEM((LAYERS, 3, 3, SHARD, PART), BF),
        ]
        + sems(90, 90),
        [(w_grad0.reshape(cube), False), (w_grad1.reshape(cube), False)],
    )
    att = jnp.stack([att0, att1])
    grad_tokens = lax.dynamic_slice_in_dim(upstream, core * HALF, HALF, 1)
    return (
        block_out,
        grad_tokens,
        att[:, :, QKV + OUT],
        att[:, :, :768],
        att[:, :, 768:896],
        att[:, :, 896:QKV],
        jnp.swapaxes(att[:, :, QKV : QKV + OUT], 1, 2),
        att[:, :, QKV + OUT + 1],
        *[jnp.stack([first, second]) for first, second in zip(expert0, expert1)],
    )


def solution(mesh):
    placed = (
        P(("dp", "expert"), "blk"),
        P(("dp", "expert"), None),
        P(None, ("dp", "expert"), None),
        P(None, ("dp", "expert"), None),
        P(None, ("dp", "expert")),
        P(None, ("dp", "expert"), "blk"),
        P(None, ("dp", "expert"), "blk"),
        P(None, ("dp", "expert"), "blk"),
        P(None, "blk", ("dp", "expert")),
        P(None, ("dp", "expert")),
        P(None, "expert", None, "blk"),
        P(None, "expert", None, "blk"),
        P(None, "expert", "blk", None),
        P(("dp", "expert"), "blk"),
    )
    return jax.shard_map(
        per_device,
        mesh=mesh,
        in_specs=placed,
        out_specs=(
            P(("dp", "expert"), "blk"),
            P(("dp", "expert"), "blk"),
            P(None, ("dp", "expert")),
            P(None, ("dp", "expert"), "blk"),
            P(None, ("dp", "expert"), "blk"),
            P(None, ("dp", "expert"), "blk"),
            P(None, "blk", ("dp", "expert")),
            P(None, ("dp", "expert")),
            P(None, "expert", "dp", "blk"),
            P(None, "expert", "dp", "blk"),
            P(None, "expert", "blk", "dp"),
        ),
        check_vma=False,
    )
```

```python
import functools
import math
import types

import jax
import jax.numpy as jnp
from jax import lax
from jax.experimental import pallas as pl
from jax.experimental.pallas import tpu as pltpu
from jax.sharding import PartitionSpec as P

HEAD = 128
TOP = 4
LAYERS = 2
F32 = jnp.float32
BF = jnp.bfloat16
MESH = pl.DeviceIdType.MESH

epsilon = 1e-06
rope_base = 1000000.0

TOKENS = 128
WIDE = 1536
HALF = WIDE // 2
HEADS = 6
HIDDEN = 384
PEERS = 16
CAP = 24
SLOTS = PEERS * CAP
SHARD = 24
QKV = 1024
OUT = 768
COLS = QKV + OUT + 128
PART = COLS // 3
ORDERS = ((0, 1, 2), (1, 2, 0), (2, 0, 1))
LIMIT = 60 << 20
LATER = ((0, 640, (1, 2, 0)), (640, 640, (2, 1, 0)), (1280, 384, (0, 2, 1)), (1664, 256, (0, 1, 2)))

ANY = pl.BlockSpec(memory_space=pl.ANY)
VMEM = pl.BlockSpec(memory_space=pltpu.VMEM)
SMEM = pl.BlockSpec(memory_space=pltpu.SMEM)


def dot(a, b, ca=1, cb=0):
    return lax.dot_general(a, b, (((ca,), (cb,)), ((), ())), preferred_element_type=F32)


def coords():
    ex = lax.axis_index("expert")
    return [lax.axis_index("dp"), lax.div(ex, 4), lax.rem(ex, 4)]


def shifted(xyz, axis, by):
    moved = list(xyz)
    moved[axis] = lax.rem(xyz[axis] + by, 4)
    return moved


def device_at(xyz, core):
    return (xyz[0], xyz[1] * 4 + xyz[2], core)


def partner():
    return (lax.axis_index("dp"), lax.axis_index("expert"), 1 - lax.axis_index("blk"))


def hail(devices):
    barrier = pltpu.get_barrier_semaphore()
    for device in devices:
        pl.semaphore_signal(barrier, inc=1, device_id=device, device_id_type=MESH)
    return len(devices)


def heard(count):
    pl.semaphore_wait(pltpu.get_barrier_semaphore(), count)


def peer(step):
    dp, ex, core = (lax.axis_index(a) for a in ("dp", "expert", "blk"))
    return (dp, lax.rem(ex + step, PEERS), core)


def peers():
    return [peer(d) for d in range(1, PEERS)] + [partner()]


class Local:
    def __init__(self, sem):
        self.sem, self.at, self.kept = sem, 0, []

    def start(self, src, dst):
        assert self.at < self.sem.shape[0]
        copy = pltpu.make_async_copy(src, dst, self.sem.at[self.at])
        self.at += 1
        copy.start()
        return copy

    def keep(self, src, dst):
        self.kept.append(self.start(src, dst))

    def wait_kept(self):
        for copy in self.kept:
            copy.wait()


class Sender:
    def __init__(self, send, recv):
        self.send, self.recv, self.at = send, recv, 0

    def start(self, src, dst, device):
        assert self.at < self.send.shape[0]
        copy = pltpu.make_async_remote_copy(
            src_ref=src,
            dst_ref=dst,
            send_sem=self.send.at[self.at],
            recv_sem=self.recv.at[self.at],
            device_id=device,
            device_id_type=MESH,
        )
        self.at += 1
        copy.start()
        return copy


def exchange_copy(src, dst, send, recv, step):
    me = lax.axis_index("expert")
    target = peer(step)
    return pltpu.make_async_remote_copy(
        src_ref=src.at[target[1]],
        dst_ref=dst.at[me],
        send_sem=send.at[step],
        recv_sem=recv.at[step],
        device_id=target,
        device_id_type=MESH,
    )


def exchange_start(src, dst, send, recv):
    me = lax.axis_index("expert")

    def begin(step, carry):
        exchange_copy(src, dst, send, recv, step).start()
        return carry

    lax.fori_loop(1, PEERS, begin, 0)
    pltpu.make_async_copy(src.at[me], dst.at[me], send.at[0]).start()


def exchange_wait(src, dst, send, recv):
    me = lax.axis_index("expert")

    def end(step, carry):
        exchange_copy(src, dst, send, recv, step).wait()
        return carry

    lax.fori_loop(1, PEERS, end, 0)
    pltpu.make_async_copy(src.at[me], dst.at[me], send.at[0]).wait()


def rows_of(ref):
    return ref[...].astype(F32).reshape(SLOTS, WIDE).astype(BF)


def store_rows(ref, rows):
    ref[...] = rows.reshape(PEERS, CAP, WIDE).astype(BF)


def slot_matrices(ids, weights):
    core = lax.axis_index("blk")
    lane = lax.broadcasted_iota(jnp.int32, (TOKENS, 128), 1)
    expert = 2 * lane + core
    chosen = jnp.zeros((TOKENS, 128), F32)
    gate = jnp.zeros((TOKENS, 128), F32)
    for j in range(TOP):
        hit = jnp.where(ids[:, j : j + 1] == expert, 1.0, 0.0)
        chosen = chosen + hit
        gate = gate + hit * weights[:, j : j + 1]
    chosen, gate = chosen.T[:PEERS], gate.T[:PEERS]
    before = lax.broadcasted_iota(jnp.int32, (TOKENS, TOKENS), 0) < lax.broadcasted_iota(
        jnp.int32, (TOKENS, TOKENS), 1
    )
    rank = dot(chosen.astype(BF), jnp.where(before, 1.0, 0.0).astype(BF))
    rank = jnp.where(chosen > 0.0, rank, -1.0)
    shape = (PEERS, CAP, TOKENS)
    place = lax.broadcasted_iota(jnp.int32, shape, 1).astype(F32)
    onehot = jnp.where(jnp.broadcast_to(rank[:, None, :], shape) == place, 1.0, 0.0)
    weighted = onehot * jnp.broadcast_to(gate[:, None, :], shape)
    return onehot.reshape(SLOTS, TOKENS), weighted.reshape(SLOTS, TOKENS)


def halves(value):
    high = value.astype(BF)
    return high, (value - high.astype(F32)).astype(BF)


def combine(weighted, rows):
    high, low = halves(weighted)
    return dot(high, rows, 0, 0) + dot(low, rows, 0, 0)


def gain_rows(w_ref):
    unit = jnp.where(
        lax.broadcasted_iota(jnp.int32, (8, 128), 0) == lax.broadcasted_iota(jnp.int32, (8, 128), 1),
        1.0,
        0.0,
    ).astype(BF)
    rows = dot(unit, w_ref[:, QKV + OUT : COLS], 1, 1)
    return rows[0:1, :], rows[1:2, :]


def inverse_norm(u):
    return lax.rsqrt(jnp.mean(u * u, axis=-1, keepdims=True) + epsilon)


def norm_back(u, inverse, gain, upstream):
    scaled = upstream * gain
    inward = inverse * scaled - u * (inverse * inverse * inverse) * jnp.mean(
        u * scaled, axis=-1, keepdims=True
    )
    return inward, upstream * u * inverse


def rotate(u, cos, sin):
    return u * cos + pltpu.roll(u, HEAD // 2, 1) * sin


def unrotate(u, cos, sin):
    return u * cos - pltpu.roll(u, HEAD // 2, 1) * sin


def head_of(value, h):
    return value[:, h * HEAD : (h + 1) * HEAD]


def attention(x, gain, w_ref, cos, sin, allow, n_ref, qkv_ref, prob_ref, o_ref):
    n = (x * inverse_norm(x) * gain).astype(BF)
    n_ref[...] = n
    flat = dot(n, w_ref[:, 0:QKV])
    for h in range(HEADS + 1):
        qkv_ref[:, h * HEAD : (h + 1) * HEAD] = rotate(head_of(flat, h), cos, sin).astype(BF)
    qkv_ref[:, (HEADS + 1) * HEAD :] = flat[:, (HEADS + 1) * HEAD :].astype(BF)
    key = qkv_ref[:, HEADS * HEAD : (HEADS + 1) * HEAD]
    value = qkv_ref[:, (HEADS + 1) * HEAD :]
    for h in range(HEADS):
        scores = dot(qkv_ref[:, h * HEAD : (h + 1) * HEAD], key, 1, 1) * HEAD ** (-0.5)
        scores = jnp.where(allow > 0.0, scores, -1e30)
        weight = jnp.exp(scores - jnp.max(scores, axis=-1, keepdims=True))
        prob = weight / jnp.sum(weight, axis=-1, keepdims=True)
        prob_ref[h] = prob
        o_ref[:, h * HEAD : (h + 1) * HEAD] = dot(prob.astype(BF), value).astype(BF)
    return dot(o_ref[...], w_ref[:, QKV : QKV + OUT], 1, 1)


def expert_weight_copies(layer, r, local):
    core = lax.axis_index("blk")
    copies = []
    for name in ("gate", "up", "down"):
        held = getattr(r, "held_" + name)
        copies.append(local.start(getattr(r, name).at[layer, core], held.at[0]))
        copies.append(local.start(getattr(r, name + "_other").at[layer], held.at[1]))
    return copies


def expert_forward(rows, held, a_ref, b_ref):
    gate, up, down = held
    total = None
    for c in range(2):
        a = dot(rows, gate[c])
        b = dot(rows, up[c])
        a_ref[c] = a
        b_ref[c] = b
        z = (a / (1.0 + jnp.exp(-a)) * b).astype(BF)
        term = dot(z, down[c])
        total = term if total is None else total + term
    return total


def expert_backward(dy, held, a_ref, b_ref, z_ref, d_ref):
    gate, up, down = held
    total = None
    for c in range(2):
        a = a_ref[c]
        b = b_ref[c]
        sg = 1.0 / (1.0 + jnp.exp(-a))
        z_ref[:, c * HIDDEN : (c + 1) * HIDDEN] = (a * sg * b).astype(BF)
        dz = dot(dy, down[c], 1, 1)
        da = (dz * b * sg * (1.0 + a * (1.0 - sg))).astype(BF)
        db = (dz * a * sg).astype(BF)
        d_ref[:, 2 * c * HIDDEN : (2 * c + 1) * HIDDEN] = da
        d_ref[:, (2 * c + 1) * HIDDEN : (2 * c + 2) * HIDDEN] = db
        term = dot(da, gate[c], 1, 1) + dot(db, up[c], 1, 1)
        total = term if total is None else total + term
    return total


def expert_gradients(rows_ref, dy_ref, z_ref, d_ref, stage, grads, local):
    sent = []
    for q in range(4):
        if q >= 2:
            sent[q - 2].wait()
        columns = slice(q * HIDDEN, (q + 1) * HIDDEN)
        slot = q % 2
        both = dot(rows_ref[:, columns], d_ref[...], 0, 0)
        for c in range(2):
            for i in range(2):
                at = (2 * c + i) * HIDDEN
                stage[slot, 3 * c + i] = both[:, at : at + HIDDEN].astype(BF)
        low = dot(z_ref[...], dy_ref[:, columns], 0, 0)
        for c in range(2):
            stage[slot, 3 * c + 2] = low[c * HIDDEN : (c + 1) * HIDDEN].astype(BF)
        sent.append(local.start(stage.at[slot], grads.at[q]))
    return sent[2:]


def ring_devices(xyz, core, axis, steps=(1, 2, 3)):
    return [device_at(shifted(xyz, axis, by), core) for by in steps]


class Gather:
    def __init__(self, sender, xyz, core):
        self.sender, self.xyz, self.core = sender, xyz, core

    def slab(self, job, stage, at, half=None):
        whole, lane, lanes, order = job
        index = list(at)
        for axis in order[:stage]:
            index[axis] = pl.ds(0, 4)
        if half is not None:
            index[order[0]] = pl.ds(2 * half, 2)
        return whole.at[index[0], index[1], index[2], :, pl.ds(lane, lanes)]

    def to(self, job, stage, by):
        return device_at(shifted(self.xyz, job[3][stage], by), self.core)

    def first(self, job, shard):
        source = shard.at[:, pl.ds(job[1], job[2])]
        target = self.slab(job, 0, self.xyz)
        return [self.sender.start(source, target, self.to(job, 0, by)) for by in (1, 3, 2)]

    def near(self, job, stage):
        block = self.slab(job, stage, self.xyz)
        return [self.sender.start(block, block, self.to(job, stage, by)) for by in (1, 3)]

    def relay(self, job, stage, near):
        copies = []
        for half, by in enumerate((1, 3)):
            near[half].wait_recv()
            at = shifted(self.xyz, job[3][stage], 4 - by)
            block = self.slab(job, stage, at, half)
            copies.append(self.sender.start(block, block, self.to(job, stage, by)))
        return copies

    def finish(self, near, relays):
        for copy in near:
            copy.wait_send()
        for copy in relays:
            copy.wait()


class ExpertSum:
    def __init__(self, r, sender, local, xyz, core):
        self.r, self.sender, self.core = r, sender, core
        self.plus, self.minus = ring_devices(xyz, core, 0, (1, 3))
        self.grads, self.near, self.passing = r.grads_in, r.near, r.passing
        self.quarter = [shifted(xyz, 0, by)[0] for by in range(4)]
        self.loads = [
            local.start(self.half(1, 0), r.mine.at[pl.ds(0, 3)]),
            local.start(self.half(3, 1), r.mine.at[pl.ds(3, 3)]),
            local.start(self.grads.at[self.quarter[0]], r.mine.at[pl.ds(6, 6)]),
        ]

    def half(self, by, half):
        return self.grads.at[self.quarter[by], pl.ds(3 * half, 3)]

    def near_half(self, side, half):
        return self.near.at[side, pl.ds(3 * half, 3)]

    def start(self):
        go = self.sender.start
        self.far = [
            go(self.half(2, 0), self.passing.at[0], self.plus),
            go(self.half(2, 1), self.passing.at[1], self.minus),
        ]
        self.plain = [
            go(self.half(1, 1), self.near_half(0, 1), self.plus),
            go(self.half(3, 0), self.near_half(1, 0), self.minus),
        ]

    def relay(self):
        for side, target in enumerate((self.plus, self.minus)):
            self.loads[side].wait()
            self.far[side].wait_recv()
            for i in range(3):
                own = self.r.mine[3 * side + i].astype(F32)
                self.passing[side, i] = (own + self.passing[side, i].astype(F32)).astype(BF)
            self.plain.append(
                self.sender.start(self.passing.at[side], self.near_half(side, side), target)
            )

    def finish(self):
        r = self.r
        self.loads[2].wait()
        for copy in self.plain:
            copy.wait()
        for copy in self.far:
            copy.wait_send()
        for i in (3, 4, 5, 0, 1, 2):
            value = r.mine[6 + i].astype(F32) + r.near[0, i].astype(F32) + r.near[1, i].astype(F32)
            if i >= 3:
                r.ship[i - 3] = value.astype(BF)
            else:
                r.total[self.core, i] = value.astype(BF)
            if i == 5:
                copy = self.sender.start(r.ship, r.total.at[self.core], partner())
        copy.wait()


EXPERT_SUM = dict(
    near=pltpu.VMEM((2, 6, HIDDEN, HIDDEN), BF),
    passing=pltpu.VMEM((2, 3, HIDDEN, HIDDEN), BF),
    mine=pltpu.VMEM((12, HIDDEN, HIDDEN), BF),
    ship=pltpu.VMEM((3, HIDDEN, HIDDEN), BF),
)


def tables(r):
    first = r.lengths[0, 0]
    second = first + r.lengths[0, 1]

    def place(index):
        segment = jnp.where(index >= first, 1, 0) + jnp.where(index >= second, 1, 0)
        start = jnp.where(segment == 0, 0, jnp.where(segment == 1, first, second))
        return segment, index - start

    shape = (TOKENS, TOKENS)
    lane = lax.broadcasted_iota(jnp.int32, shape, 1)
    row_segment, row_place = place(lax.broadcasted_iota(jnp.int32, shape, 0))
    key_segment, key_place = place(lane)
    allowed = (row_segment == key_segment) & (key_place <= row_place)
    r.allow[...] = jnp.where(allowed, 1.0, 0.0)
    half = jnp.where(lane < HEAD // 2, lane, lane - HEAD // 2).astype(F32)
    frequency = jnp.exp(half * (-2.0 / HEAD * math.log(rope_base)))
    angles = row_place.astype(F32) * frequency
    sign = jnp.where(lane < HEAD // 2, -1.0, 1.0)
    r.cos[...] = jnp.cos(angles)
    r.sin[...] = jnp.sin(angles) * sign


def assemble(r):
    square = (SHARD, SHARD)
    eye = lax.broadcasted_iota(jnp.int32, square, 0) == lax.broadcasted_iota(jnp.int32, square, 1)
    lane = lax.broadcasted_iota(jnp.int32, (SHARD, 128), 1)
    for l in range(LAYERS):
        r.shard[l, :, 0:768] = r.query[l]
        r.shard[l, :, 768:896] = r.key[l]
        r.shard[l, :, 896:QKV] = r.value[l]
        turned = dot(jnp.where(eye, 1.0, 0.0).astype(BF), r.out[l], 1, 1)
        r.shard[l, :, QKV : QKV + OUT] = turned.astype(BF)
        column = jnp.zeros((SHARD, 128), F32)
        for i, gain in enumerate((r.gain_a, r.gain_e)):
            spread = jnp.broadcast_to(gain[l : l + 1, :].astype(F32), square)
            spread = jnp.where(eye, spread, 0.0).astype(BF)
            column = column + dot(spread, jnp.where(lane == i, 1.0, 0.0).astype(BF))
        r.shard[l, :, QKV + OUT :] = column.astype(BF)


def gather_body(r):
    xyz, core = coords(), lax.axis_index("blk")
    count = hail([d for axis in range(3) for d in ring_devices(xyz, core, axis)] + [partner()])
    sender, local = Sender(r.send, r.recv), Local(r.local)
    mine = pl.ds(pl.multiple_of(core * HALF, HALF), HALF)
    here = [
        local.start(r.tok, r.tokens.at[:, mine]),
        local.start(r.cot_half, r.cot.at[:, mine]),
    ]
    assemble(r)
    for l, whole in enumerate((r.w0, r.w1)):
        here.append(local.start(r.shard.at[l], whole.at[xyz[0], xyz[1], xyz[2]]))
    heard(count)
    gather = Gather(sender, xyz, core)
    now = [(r.w0, p * PART, PART, order) for p, order in enumerate(ORDERS)]
    later = [(r.w1, *job) for job in LATER]
    first = [c for job in now for c in gather.first(job, r.shard.at[0])]
    first_later = [c for job in later for c in gather.first(job, r.shard.at[1])]
    others = [
        sender.start(r.tok, r.tokens.at[:, mine], partner()),
        sender.start(r.cot_half, r.cot.at[:, mine], partner()),
    ]
    for l in range(LAYERS):
        for name in ("gate", "up", "down"):
            ref = getattr(r, name).at[l, 1 - core]
            others.append(sender.start(ref, getattr(r, name + "_other").at[l], partner()))
    tables(r)
    for copy in here + first:
        copy.wait()
    near = [gather.near(job, 1) for job in now]
    for copy in first_later:
        copy.wait()
    near_later = [gather.near(job, 1) for job in later]
    relays = [gather.relay(job, 1, n) for job, n in zip(now, near)]
    relays_later = [gather.relay(job, 1, n) for job, n in zip(later, near_later)]
    for n, relay in zip(near, relays):
        gather.finish(n, relay)
    near = [gather.near(job, 2) for job in now]
    for n, relay in zip(near_later, relays_later):
        gather.finish(n, relay)
    relays = [gather.relay(job, 2, n) for job, n in zip(now, near)]
    for n, relay in zip(near, relays):
        gather.finish(n, relay)
    for copy in others:
        copy.wait()


KEPT = dict(
    h=((TOKENS, WIDE), F32),
    n=((TOKENS, WIDE), BF),
    qkv=((TOKENS, QKV), BF),
    prob=((HEADS, TOKENS, TOKENS), F32),
    o=((TOKENS, OUT), BF),
    onehot=((SLOTS, TOKENS), BF),
    weighted=((SLOTS, TOKENS), F32),
)
KEPT_SPACE = {name: pltpu.VMEM(*spec) for name, spec in KEPT.items()}
HELD = dict(
    held_gate=pltpu.VMEM((2, WIDE, HIDDEN), BF),
    held_up=pltpu.VMEM((2, WIDE, HIDDEN), BF),
    held_down=pltpu.VMEM((2, HIDDEN, WIDE), BF),
)
ROWS = ((SLOTS, WIDE), BF)
INNER = ((2, SLOTS, HIDDEN), F32)
BLOCKS = ((PEERS, CAP, WIDE), BF)
PLANE = ((TOKENS, WIDE), F32)
GRADS = ((4, 6, HIDDEN, HIDDEN), BF)
BACKWARD = dict(
    z=pltpu.VMEM((SLOTS, 2 * HIDDEN), BF),
    d=pltpu.VMEM((SLOTS, 4 * HIDDEN), BF),
    dy=pltpu.VMEM(*ROWS),
    stage=pltpu.VMEM((2, 6, HIDDEN, HIDDEN), BF),
)


def sems(**counts):
    return {name: pltpu.SemaphoreType.DMA((n,)) for name, n in counts.items()}


def spaces(**specs):
    return {name: pltpu.VMEM(*spec) for name, spec in specs.items()}


def front(r, x, pair, local):
    gain_a, gain_e = gain_rows(r.w)
    r.part0[...] = attention(
        x, gain_a, r.w, r.cos[...], r.sin[...], r.allow[...], r.n, r.qkv, r.prob, r.o
    )
    copy = pair.start(r.part0, r.theirs0, partner())
    for name in ("n", "qkv", "prob", "o", "onehot", "weighted"):
        local.keep(getattr(r, name), getattr(r, name + "_out"))
    copy.wait()
    h = x + (r.part0[...] + r.theirs0[...])
    r.h[...] = h
    local.keep(r.h, r.h_out)
    return (h * inverse_norm(h) * gain_e).astype(BF)


def forward_body(layer, r):
    xyz, core = coords(), lax.axis_index("blk")
    local, pair = Local(r.local), Sender(r.pair_send, r.pair_recv)
    load = local.start(r.w_any, r.w)
    count = hail(peers() + ring_devices(xyz, core, 0, (1, 3)))
    loads = expert_weight_copies(layer, r, local)
    hot, heavy = slot_matrices(r.ids[layer], r.weights[layer])
    r.onehot[...] = hot.astype(BF)
    r.weighted[...] = heavy
    heard(count)
    gather = Gather(Sender(r.wide_send, r.wide_recv), xyz, core)
    jobs = [(r.w1, *job) for job in LATER]
    near = [gather.near(job, 2) for job in jobs]
    load.wait()
    m = front(r, r.x[...].astype(F32), pair, local)
    store_rows(r.sent, dot(r.onehot[...], m))
    relays = {i: gather.relay(jobs[i], 2, near[i]) for i in (2, 3)}
    exchange_start(r.sent, r.came, r.send0, r.recv0)
    for copy in loads:
        copy.wait()
    exchange_wait(r.sent, r.came, r.send0, r.recv0)
    relays[0] = gather.relay(jobs[0], 2, near[0])
    r.rows[...] = rows_of(r.came)
    local.keep(r.rows, r.rows_out)
    held = (r.held_gate, r.held_up, r.held_down)
    store_rows(r.sent, expert_forward(r.rows[...], held, r.a, r.b))
    exchange_start(r.sent, r.back, r.send1, r.recv1)
    relays[1] = gather.relay(jobs[1], 2, near[1])
    local.keep(r.a, r.a_out)
    local.keep(r.b, r.b_out)
    exchange_wait(r.sent, r.back, r.send1, r.recv1)
    r.part1[...] = combine(r.weighted[...], rows_of(r.back))
    pair.start(r.part1, r.theirs1, partner()).wait()
    r.stream[...] = r.h[...] + (r.part1[...] + r.theirs1[...])
    for i in range(4):
        gather.finish(near[i], relays[i])
    local.wait_kept()


def middle_body(layer, r):
    local, pair = Local(r.local), Sender(r.pair_send, r.pair_recv)
    load = local.start(r.w_any, r.w)
    count = hail(peers())
    loads = expert_weight_copies(layer, r, local)
    hot, heavy = slot_matrices(r.ids[layer], r.weights[layer])
    r.onehot[...] = hot.astype(BF)
    r.weighted[...] = heavy
    slot_weight = jnp.sum(heavy, axis=1, keepdims=True)
    store_rows(r.sent_g, dot(r.onehot[...], r.cot[...]) * slot_weight)
    heard(count)
    exchange_start(r.sent_g, r.came_g, r.send1, r.recv1)
    load.wait()
    m = front(r, r.x[...], pair, local)
    store_rows(r.sent, dot(r.onehot[...], m))
    exchange_wait(r.sent_g, r.came_g, r.send1, r.recv1)
    exchange_start(r.sent, r.came, r.send0, r.recv0)
    r.dy[...] = rows_of(r.came_g)
    for copy in loads:
        copy.wait()
    exchange_wait(r.sent, r.came, r.send0, r.recv0)
    r.rows[...] = rows_of(r.came)
    held = (r.held_gate, r.held_up, r.held_down)
    store_rows(r.sent, expert_forward(r.rows[...], held, r.a, r.b))
    exchange_start(r.sent, r.y_back, r.send2, r.recv2)
    store_rows(r.turn, expert_backward(r.dy[...], held, r.a, r.b, r.z, r.d))
    local.keep(r.turn, r.m_back)
    local.kept += expert_gradients(r.rows, r.dy, r.z, r.d, r.stage, r.grads, local)
    exchange_wait(r.sent, r.y_back, r.send2, r.recv2)
    local.wait_kept()


def turned(value):
    return value.astype(F32).T.reshape(4, 4, 4, SHARD, TOKENS).astype(BF)


def own_part(ref, axis, index):
    return ref.at[:, index] if axis == 1 else ref.at[:, :, index]


def share_factor(ref, into, axis, sender, xyz, core):
    copies = []
    for by in (1, 3, 2):
        there = shifted(xyz, axis, by)
        copies.append(
            sender.start(own_part(ref, axis, there[axis]), into.at[by - 1], device_at(there, core))
        )
    return copies


def share_whole(ref, into, axis, sender, xyz, core):
    return [
        sender.start(ref, into.at[pl.ds(by * TOKENS, TOKENS)], device_at(shifted(xyz, axis, by), core))
        for by in (1, 3, 2)
    ]


def quarter_sum(own, came, axis, xyz, right):
    first = own_part(own, axis, xyz[axis])[...]
    pieces = [first] + [came[i] for i in range(3)]
    left = [p.astype(F32).reshape(HIDDEN, TOKENS).astype(BF) for p in pieces]
    return dot(jnp.concatenate(left, axis=1), right[...])


def back_body(last, r):
    xyz, core = coords(), lax.axis_index("blk")
    local, pair = Local(r.local), Sender(r.pair_send, r.pair_recv)
    sender = Sender(r.wide_send, r.wide_recv)
    load = local.start(r.w_any, r.w)
    count = hail(peers() + ring_devices(xyz, core, 0, (1, 3) if last else (1, 2, 3)))
    expert_sum = ExpertSum(r, sender, local, xyz, core)
    heard(count)
    exchange_start(r.m_came, r.came, r.send0, r.recv0)
    expert_sum.start()
    if last:
        loads = expert_weight_copies(0, r, local)
    r.n_turned[...] = turned(r.n[...])
    if not last:
        r.sum_a[1] = r.sum_a_in[...]
        r.sum_b[1] = r.sum_b_in[...]
    r.o_all[0:TOKENS] = r.o[...]
    load.wait()
    gain_a, gain_e = gain_rows(r.w)
    if not last:
        old = late_start(r, 1, sender, xyz, core)
    exchange_wait(r.m_came, r.came, r.send0, r.recv0)
    r.part0[...] = dot(r.onehot[...], rows_of(r.came), 0, 0)
    copy = pair.start(r.part0, r.theirs0, partner())
    shared = share_factor(r.n_turned, r.n_came, 1, sender, xyz, core)
    shared += share_whole(r.o, r.o_all, 2, sender, xyz, core)
    if not last:
        old = late_middle(r, 1, sender, xyz, core, old)
    copy.wait()
    dm = r.part0[...] + r.theirs0[...]
    hidden = r.h[...]
    inward, gain_grad_e = norm_back(hidden, inverse_norm(hidden), gain_e, dm)
    gh = r.upstream[...].astype(F32) + inward
    r.flow[...] = gh
    da = gh.astype(BF)
    r.da_turned[...] = turned(gh)
    shared += share_factor(r.da_turned, r.da_came, 2, sender, xyz, core)
    do = dot(da, r.w[:, QKV : QKV + OUT]).astype(BF)
    key = r.qkv[:, HEADS * HEAD : (HEADS + 1) * HEAD]
    value = r.qkv[:, (HEADS + 1) * HEAD :]
    scale = HEAD ** (-0.5)
    key_grad, value_grad = None, None
    cosine, sine = r.cos[...], r.sin[...]
    lin = r.lin_all
    for i in range(HEADS):
        prob_i = r.prob[i]
        do_i = head_of(do, i)
        q_i = r.qkv[:, i * HEAD : (i + 1) * HEAD]
        dprob = dot(do_i, value, 1, 1)
        centre = jnp.sum(prob_i * dprob, axis=-1, keepdims=True)
        ds = (prob_i * (dprob - centre)).astype(BF)
        dq = dot(ds, key) * scale
        lin[0:TOKENS, i * HEAD : (i + 1) * HEAD] = unrotate(dq, cosine, sine).astype(BF)
        dk = dot(ds, q_i, 0, 0)
        dv = dot(prob_i.astype(BF), do_i, 0, 0)
        key_grad = dk if key_grad is None else key_grad + dk
        value_grad = dv if value_grad is None else value_grad + dv
    lin[0:TOKENS, HEADS * HEAD : (HEADS + 1) * HEAD] = unrotate(
        key_grad * scale, cosine, sine
    ).astype(BF)
    lin[0:TOKENS, (HEADS + 1) * HEAD :] = value_grad.astype(BF)
    r.part1[...] = dot(lin[0:TOKENS, :], r.w[:, 0:QKV], 1, 1)
    across = pair.start(r.part1, r.theirs1, partner())
    if not last:
        shared += share_whole(lin.at[pl.ds(0, TOKENS)], lin, 1, sender, xyz, core)
        expert_sum.relay()
    across.wait()
    dn = r.part1[...] + r.theirs1[...]
    x = r.x[...].astype(F32)
    inward, gain_grad_a = norm_back(x, inverse_norm(x), gain_a, dn)
    flow = r.flow[...] + inward
    row = lax.broadcasted_iota(jnp.int32, (8, WIDE), 0)
    gains = jnp.zeros((8, WIDE), F32)
    for i, grad in enumerate((gain_grad_a, gain_grad_e)):
        grad = jnp.sum(grad, axis=0, keepdims=True)
        gains = jnp.where(row == i + (2 if last else 0), jnp.broadcast_to(grad, (8, WIDE)), gains)
    if not last:
        r.tokens_grad[...] = jnp.where(core == 1, flow[:, HALF:], flow[:, :HALF])
        finish_sums(r, shared, gains + r.gains_in[...], old, expert_sum, sender, xyz, core)
        return
    r.gains[...] = gains
    r.flow[...] = flow
    slot_weight = jnp.sum(r.weighted_next[...], axis=1, keepdims=True)
    high, low = halves(flow)
    hot = r.onehot_next[...]
    store_rows(r.sent, (dot(hot, high) + dot(hot, low)) * slot_weight)
    exchange_start(r.sent, r.came_g, r.send1, r.recv1)
    local.keep(r.flow, r.flow_out)
    expert_sum.relay()
    shared += share_whole(lin.at[pl.ds(0, TOKENS)], lin, 1, sender, xyz, core)
    mixed = combine(r.weighted[...], rows_of(r.y_back))
    r.half[...] = jnp.where(core == 1, mixed[:, :HALF], mixed[:, HALF:])
    copy = pair.start(r.half, r.half_theirs, partner())
    own = jnp.where(core == 1, mixed[:, HALF:], mixed[:, :HALF])
    kept = jnp.where(core == 1, r.h[:, HALF:], r.h[:, :HALF])
    copy.wait()
    r.block_out[...] = (kept + (own + r.half_theirs[...])).astype(BF)
    for copy in loads:
        copy.wait()
    exchange_wait(r.sent, r.came_g, r.send1, r.recv1)
    r.dy[...] = rows_of(r.came_g)
    held = (r.held_gate, r.held_up, r.held_down)
    store_rows(r.turn, expert_backward(r.dy[...], held, r.a, r.b, r.z, r.d))
    local.keep(r.turn, r.m_back)
    local.kept += expert_gradients(r.rows, r.dy, r.z, r.d, r.stage, r.grads, local)
    for copy in shared:
        copy.wait()
    wide = (4, 4, SHARD, QKV)
    r.sum_a[...] = quarter_sum(r.n_turned, r.n_came, 1, xyz, lin).reshape(wide).astype(BF)
    wide = (4, 4, SHARD, OUT)
    r.sum_b[...] = quarter_sum(r.da_turned, r.da_came, 2, xyz, r.o_all).reshape(wide).astype(BF)
    expert_sum.finish()
    local.wait_kept()


def late_start(r, l, sender, xyz, core):
    copies = []
    for ref, came, axis in ((r.sum_a, r.near_a, 2), (r.sum_b, r.near_b, 1)):
        for by in (1, 3, 2):
            there = shifted(xyz, axis, by)
            copies.append(
                sender.start(ref.at[l, :, there[axis]], came.at[l, by - 1], device_at(there, core))
            )
    return copies


def late_middle(r, l, sender, xyz, core, copies):
    for copy in copies:
        copy.wait()
    for ref, came, axis, lanes in (
        (r.sum_a, r.near_a, 2, slice(0, QKV)),
        (r.sum_b, r.near_b, 1, slice(QKV, QKV + OUT)),
    ):
        total = ref[l, :, xyz[axis]].astype(F32)
        for i in range(3):
            total = total + came[l, i].astype(F32)
        r.line[l, :, :, lanes] = total.astype(BF)
    copies = []
    for by in (1, 3, 2):
        there = shifted(xyz, 0, by)
        copies.append(
            sender.start(r.line.at[l, there[0]], r.line_came.at[l, by - 1], device_at(there, core))
        )
    return copies


def late_end(r, l, xyz, copies):
    for copy in copies:
        copy.wait()
    total = r.line[l, xyz[0]].astype(F32)
    for i in range(3):
        total = total + r.line_came[l, i].astype(F32)
    r.weight_grad[l] = total


def gains_along(r, axis, sender, xyz, core):
    return [
        sender.start(r.gain_sum.at[axis], r.gain_came.at[axis, by - 1], device_at(shifted(xyz, axis, by), core))
        for by in (1, 3, 2)
    ]


def gains_next(r, axis, copies):
    for copy in copies:
        copy.wait()
    total = r.gain_sum[axis]
    for i in range(3):
        total = total + r.gain_came[axis, i]
    return total


def finish_sums(r, shared, gains, old, expert_sum, sender, xyz, core):
    r.gain_sum[1] = gains
    along = gains_along(r, 1, sender, xyz, core)
    for copy in shared:
        copy.wait()
    wide = (4, 4, SHARD, QKV)
    r.sum_a[0] = quarter_sum(r.n_turned, r.n_came, 1, xyz, r.lin_all).reshape(wide).astype(BF)
    wide = (4, 4, SHARD, OUT)
    r.sum_b[0] = quarter_sum(r.da_turned, r.da_came, 2, xyz, r.o_all).reshape(wide).astype(BF)
    new = late_start(r, 0, sender, xyz, core)
    r.gain_sum[2] = gains_next(r, 1, along)
    along = gains_along(r, 2, sender, xyz, core)
    late_end(r, 1, xyz, old)
    new = late_middle(r, 0, sender, xyz, core, new)
    r.gain_sum[0] = gains_next(r, 2, along)
    along = gains_along(r, 0, sender, xyz, core)
    late_end(r, 0, xyz, new)
    r.gain_total[...] = gains_next(r, 0, along)
    expert_sum.finish()


def kernel_call(body, name, cid, ins, outs, scratch, aliases=()):
    names = [*ins, *outs, *scratch]
    assert len(set(names)) == len(names)

    def kernel(*refs):
        body(types.SimpleNamespace(**dict(zip(names, refs))))

    results = pl.pallas_call(
        kernel,
        out_shape=[jax.ShapeDtypeStruct(shape, kind) for shape, kind, _ in outs.values()],
        in_specs=[space for _, space in ins.values()],
        out_specs=[space for _, _, space in outs.values()],
        scratch_shapes=list(scratch.values()),
        input_output_aliases={list(ins).index(a): list(outs).index(b) for a, b in aliases},
        compiler_params=pltpu.CompilerParams(
            collective_id=cid, has_side_effects=True, vmem_limit_bytes=LIMIT
        ),
        name=name,
    )(*[array for array, _ in ins.values()])
    return types.SimpleNamespace(**dict(zip(outs, results)))


def per_device(
    tokens_in,
    seq_lengths,
    expert_ids,
    gate_weights,
    attention_gain,
    query_weight,
    key_weight,
    value_weight,
    out_weight,
    expert_gain,
    gate_weight,
    up_weight,
    down_weight,
    cotangent,
):
    cube = (4, 4, 4, SHARD, COLS)
    own = dict(gate=(gate_weight, ANY), up=(up_weight, ANY), down=(down_weight, ANY))
    start = kernel_call(
        gather_body,
        "gather",
        1,
        dict(
            lengths=(seq_lengths, SMEM),
            query=(query_weight, VMEM),
            key=(key_weight, VMEM),
            value=(value_weight, VMEM),
            out=(out_weight, VMEM),
            gain_a=(attention_gain, VMEM),
            gain_e=(expert_gain, VMEM),
            tok=(tokens_in, VMEM),
            cot_half=(cotangent, VMEM),
            **own,
        ),
        dict(
            w0=(cube, BF, ANY),
            w1=(cube, BF, ANY),
            tokens=((TOKENS, WIDE), BF, VMEM),
            cot=((TOKENS, WIDE), BF, VMEM),
            cos=((TOKENS, HEAD), F32, VMEM),
            sin=((TOKENS, HEAD), F32, VMEM),
            allow=((TOKENS, TOKENS), F32, VMEM),
            gate_other=((LAYERS, WIDE, HIDDEN), BF, ANY),
            up_other=((LAYERS, WIDE, HIDDEN), BF, ANY),
            down_other=((LAYERS, HIDDEN, WIDE), BF, ANY),
        ),
        dict(
            shard=pltpu.VMEM((LAYERS, SHARD, COLS), BF),
            **sems(send=72, recv=72, local=4),
        ),
    )
    experts = dict(
        own,
        gate_other=(start.gate_other, ANY),
        up_other=(start.up_other, ANY),
        down_other=(start.down_other, ANY),
    )
    trig = dict(cos=(start.cos, VMEM), sin=(start.sin, VMEM))
    routing = dict(ids=(expert_ids, VMEM), weights=(gate_weights, VMEM))
    kept_out = {name + "_out": (*spec, ANY) for name, spec in KEPT.items()}
    w_space = dict(w=pltpu.VMEM((WIDE, COLS), BF))
    exchanges = sems(send0=PEERS, recv0=PEERS, send1=PEERS, recv1=PEERS, pair_send=4, pair_recv=4)
    w0 = start.w0.reshape(WIDE, COLS)
    below = kernel_call(
        functools.partial(forward_body, 0),
        "forward",
        2,
        dict(
            x=(start.tokens, VMEM),
            w_any=(w0, ANY),
            w1_in=(start.w1, ANY),
            allow=(start.allow, VMEM),
            **trig,
            **routing,
            **experts,
        ),
        dict(
            w1=(cube, BF, ANY),
            stream=(*PLANE, VMEM),
            rows_out=(*ROWS, ANY),
            a_out=(*INNER, ANY),
            b_out=(*INNER, ANY),
            **kept_out,
        ),
        dict(
            **w_space,
            **KEPT_SPACE,
            **HELD,
            **spaces(sent=BLOCKS, came=BLOCKS, back=BLOCKS, rows=ROWS, a=INNER, b=INNER),
            **spaces(part0=PLANE, theirs0=PLANE, part1=PLANE, theirs1=PLANE),
            **exchanges,
            **sems(wide_send=16, wide_recv=16, local=20),
        ),
        [("w1_in", "w1")],
    )
    w1 = below.w1.reshape(WIDE, COLS)
    above = kernel_call(
        functools.partial(middle_body, 1),
        "middle",
        3,
        dict(
            x=(below.stream, VMEM),
            cot=(start.cot, VMEM),
            w_any=(w1, ANY),
            allow=(start.allow, VMEM),
            **trig,
            **routing,
            **experts,
        ),
        dict(
            y_back=(*BLOCKS, ANY),
            m_back=(*BLOCKS, ANY),
            grads=(*GRADS, ANY),
            **kept_out,
        ),
        dict(
            **w_space,
            **KEPT_SPACE,
            **HELD,
            **spaces(sent=BLOCKS, came=BLOCKS, sent_g=BLOCKS, came_g=BLOCKS, turn=BLOCKS),
            **spaces(rows=ROWS, a=INNER, b=INNER, part0=PLANE, theirs0=PLANE),
            **BACKWARD,
            **exchanges,
            **sems(send2=PEERS, recv2=PEERS, local=20),
        ),
    )

    def kept(of):
        return {name: (getattr(of, name + "_out"), VMEM) for name in KEPT}

    total = ((2, 3, HIDDEN, HIDDEN), BF, VMEM)
    part_a, part_b = (4, 4, SHARD, QKV), (4, 4, SHARD, OUT)
    back_space = dict(
        **w_space,
        **EXPERT_SUM,
        **spaces(came=BLOCKS, part0=PLANE, theirs0=PLANE, part1=PLANE, theirs1=PLANE, flow=PLANE),
        n_turned=pltpu.VMEM((4, 4, 4, SHARD, TOKENS), BF),
        da_turned=pltpu.VMEM((4, 4, 4, SHARD, TOKENS), BF),
        n_came=pltpu.VMEM((3, 4, 4, SHARD, TOKENS), BF),
        da_came=pltpu.VMEM((3, 4, 4, SHARD, TOKENS), BF),
        lin_all=pltpu.VMEM((4 * TOKENS, QKV), BF),
        o_all=pltpu.VMEM((4 * TOKENS, OUT), BF),
        **exchanges,
        **sems(local=20),
    )
    turn = kernel_call(
        functools.partial(back_body, True),
        "back_above",
        4,
        dict(
            x=(below.stream, VMEM),
            upstream=(start.cot, VMEM),
            w_any=(w1, ANY),
            **trig,
            **kept(above),
            m_came=(above.m_back, ANY),
            y_back=(above.y_back, VMEM),
            grads_in=(above.grads, ANY),
            onehot_next=(below.onehot_out, VMEM),
            weighted_next=(below.weighted_out, VMEM),
            rows=(below.rows_out, VMEM),
            a=(below.a_out, VMEM),
            b=(below.b_out, VMEM),
            **experts,
        ),
        dict(
            flow_out=(*PLANE, ANY),
            m_back=(*BLOCKS, ANY),
            grads=(*GRADS, ANY),
            block_out=((TOKENS, HALF), BF, VMEM),
            total=total,
            gains=((8, WIDE), F32, VMEM),
            sum_a=(part_a, BF, VMEM),
            sum_b=(part_b, BF, VMEM),
        ),
        dict(
            **back_space,
            **HELD,
            **BACKWARD,
            **spaces(sent=BLOCKS, came_g=BLOCKS, turn=BLOCKS),
            half=pltpu.VMEM((TOKENS, HALF), F32),
            half_theirs=pltpu.VMEM((TOKENS, HALF), F32),
            **sems(wide_send=24, wide_recv=24),
        ),
    )
    end = kernel_call(
        functools.partial(back_body, False),
        "back_below",
        5,
        dict(
            x=(start.tokens, VMEM),
            upstream=(turn.flow_out, VMEM),
            w_any=(w0, ANY),
            **trig,
            **kept(below),
            m_came=(turn.m_back, ANY),
            grads_in=(turn.grads, ANY),
            gains_in=(turn.gains, VMEM),
            sum_a_in=(turn.sum_a, VMEM),
            sum_b_in=(turn.sum_b, VMEM),
        ),
        dict(
            tokens_grad=((TOKENS, HALF), F32, VMEM),
            total=total,
            weight_grad=((LAYERS, SHARD, QKV + OUT), F32, VMEM),
            gain_total=((8, WIDE), F32, VMEM),
        ),
        dict(
            **back_space,
            sum_a=pltpu.VMEM((LAYERS, *part_a), BF),
            sum_b=pltpu.VMEM((LAYERS, *part_b), BF),
            near_a=pltpu.VMEM((LAYERS, 3, 4, SHARD, QKV), BF),
            near_b=pltpu.VMEM((LAYERS, 3, 4, SHARD, OUT), BF),
            line=pltpu.VMEM((LAYERS, 4, SHARD, QKV + OUT), BF),
            line_came=pltpu.VMEM((LAYERS, 3, SHARD, QKV + OUT), BF),
            gain_sum=pltpu.VMEM((3, 8, WIDE), F32),
            gain_came=pltpu.VMEM((3, 3, 8, WIDE), F32),
            **sems(wide_send=48, wide_recv=48),
        ),
    )
    place = (lax.axis_index("dp") * PEERS + lax.axis_index("expert")) * SHARD
    gains = lax.dynamic_slice_in_dim(end.gain_total, place, SHARD, 1)
    att = end.weight_grad
    both = [jnp.stack([end.total[:, i], turn.total[:, i]]).astype(F32) for i in range(3)]
    return (
        turn.block_out,
        end.tokens_grad,
        gains[0:4:2],
        att[:, :, :768],
        att[:, :, 768:896],
        att[:, :, 896:QKV],
        jnp.swapaxes(att[:, :, QKV:], 1, 2),
        gains[1:4:2],
        *both,
    )


def solution(mesh):
    placed = (
        P(("dp", "expert"), "blk"),
        P(("dp", "expert"), None),
        P(None, ("dp", "expert"), None),
        P(None, ("dp", "expert"), None),
        P(None, ("dp", "expert")),
        P(None, ("dp", "expert"), "blk"),
        P(None, ("dp", "expert"), "blk"),
        P(None, ("dp", "expert"), "blk"),
        P(None, "blk", ("dp", "expert")),
        P(None, ("dp", "expert")),
        P(None, "expert", None, "blk"),
        P(None, "expert", None, "blk"),
        P(None, "expert", "blk", None),
        P(("dp", "expert"), "blk"),
    )
    return jax.shard_map(
        per_device,
        mesh=mesh,
        in_specs=placed,
        out_specs=(
            P(("dp", "expert"), "blk"),
            P(("dp", "expert"), "blk"),
            P(None, ("dp", "expert")),
            P(None, ("dp", "expert"), "blk"),
            P(None, ("dp", "expert"), "blk"),
            P(None, ("dp", "expert"), "blk"),
            P(None, "blk", ("dp", "expert")),
            P(None, ("dp", "expert")),
            P(None, "expert", "dp", "blk"),
            P(None, "expert", "dp", "blk"),
            P(None, "expert", "blk", "dp"),
        ),
        check_vma=False,
    )
```

```python
import functools
import math
import types

import jax
import jax.numpy as jnp
from jax import lax
from jax.experimental import pallas as pl
from jax.experimental.pallas import tpu as pltpu
from jax.sharding import PartitionSpec as P

HEAD = 128
TOP = 4
LAYERS = 2
F32 = jnp.float32
BF = jnp.bfloat16
MESH = pl.DeviceIdType.MESH

epsilon = 1e-06
rope_base = 1000000.0

TOKENS = 128
WIDE = 1536
HALF = WIDE // 2
HEADS = 6
HIDDEN = 384
PEERS = 16
CAP = 24
SLOTS = PEERS * CAP
SHARD = 24
QKV = 1024
OUT = 768
COLS = QKV + OUT + 128
PART = COLS // 3
ORDERS = ((0, 1, 2), (1, 2, 0), (2, 0, 1))
LIMIT = 60 << 20
LATER = ((0, 768, (1, 2, 0)), (768, 768, (2, 1, 0)), (1536, 128, (0, 2, 1)), (1664, 256, (0, 1, 2)))

ANY = pl.BlockSpec(memory_space=pl.ANY)
VMEM = pl.BlockSpec(memory_space=pltpu.VMEM)
SMEM = pl.BlockSpec(memory_space=pltpu.SMEM)


def dot(a, b, ca=1, cb=0):
    return lax.dot_general(a, b, (((ca,), (cb,)), ((), ())), preferred_element_type=F32)


def coords():
    ex = lax.axis_index("expert")
    return [lax.axis_index("dp"), lax.div(ex, 4), lax.rem(ex, 4)]


def shifted(xyz, axis, by):
    moved = list(xyz)
    moved[axis] = lax.rem(xyz[axis] + by, 4)
    return moved


def device_at(xyz, core):
    return (xyz[0], xyz[1] * 4 + xyz[2], core)


def partner():
    return (lax.axis_index("dp"), lax.axis_index("expert"), 1 - lax.axis_index("blk"))


def hail(devices):
    barrier = pltpu.get_barrier_semaphore()
    for device in devices:
        pl.semaphore_signal(barrier, inc=1, device_id=device, device_id_type=MESH)
    return len(devices)


def heard(count):
    pl.semaphore_wait(pltpu.get_barrier_semaphore(), count)


def peer(step):
    dp, ex, core = (lax.axis_index(a) for a in ("dp", "expert", "blk"))
    return (dp, lax.rem(ex + step, PEERS), core)


def peers():
    return [peer(d) for d in range(1, PEERS)] + [partner()]


class Local:
    def __init__(self, sem):
        self.sem, self.at, self.kept = sem, 0, []

    def start(self, src, dst):
        assert self.at < self.sem.shape[0]
        copy = pltpu.make_async_copy(src, dst, self.sem.at[self.at])
        self.at += 1
        copy.start()
        return copy

    def keep(self, src, dst):
        self.kept.append(self.start(src, dst))

    def wait_kept(self):
        for copy in self.kept:
            copy.wait()


class Sender:
    def __init__(self, send, recv):
        self.send, self.recv, self.at = send, recv, 0

    def start(self, src, dst, device):
        assert self.at < self.send.shape[0]
        copy = pltpu.make_async_remote_copy(
            src_ref=src,
            dst_ref=dst,
            send_sem=self.send.at[self.at],
            recv_sem=self.recv.at[self.at],
            device_id=device,
            device_id_type=MESH,
        )
        self.at += 1
        copy.start()
        return copy


def exchange_copy(src, dst, send, recv, step):
    me = lax.axis_index("expert")
    target = peer(step)
    return pltpu.make_async_remote_copy(
        src_ref=src.at[target[1]],
        dst_ref=dst.at[me],
        send_sem=send.at[step],
        recv_sem=recv.at[step],
        device_id=target,
        device_id_type=MESH,
    )


def exchange_start(src, dst, send, recv):
    me = lax.axis_index("expert")

    def begin(step, carry):
        exchange_copy(src, dst, send, recv, step).start()
        return carry

    lax.fori_loop(1, PEERS, begin, 0)
    pltpu.make_async_copy(src.at[me], dst.at[me], send.at[0]).start()


def exchange_recv(src, dst, send, recv):
    me = lax.axis_index("expert")

    def end(step, carry):
        exchange_copy(src, dst, send, recv, step).wait_recv()
        return carry

    lax.fori_loop(1, PEERS, end, 0)
    pltpu.make_async_copy(src.at[me], dst.at[me], send.at[0]).wait()


def exchange_sent(src, dst, send, recv):
    def end(step, carry):
        exchange_copy(src, dst, send, recv, step).wait_send()
        return carry

    lax.fori_loop(1, PEERS, end, 0)


def rows_of(ref):
    return ref[...].astype(F32).reshape(SLOTS, WIDE).astype(BF)


def store_rows(ref, rows):
    ref[...] = rows.reshape(PEERS, CAP, WIDE).astype(BF)


def slot_matrices(ids, weights):
    core = lax.axis_index("blk")
    expert = 2 * lax.broadcasted_iota(jnp.int32, (PEERS, TOKENS), 0) + core
    chosen = jnp.zeros((PEERS, TOKENS), F32)
    gate = jnp.zeros((PEERS, TOKENS), F32)
    for j in range(TOP):
        hit = jnp.where(ids[j : j + 1, :] == expert, 1.0, 0.0)
        chosen = chosen + hit
        gate = gate + hit * weights[j : j + 1, :]
    before = lax.broadcasted_iota(jnp.int32, (TOKENS, TOKENS), 0) < lax.broadcasted_iota(
        jnp.int32, (TOKENS, TOKENS), 1
    )
    rank = dot(chosen.astype(BF), jnp.where(before, 1.0, 0.0).astype(BF))
    rank = jnp.where(chosen > 0.0, rank, -1.0)
    shape = (PEERS, CAP, TOKENS)
    place = lax.broadcasted_iota(jnp.int32, shape, 1).astype(F32)
    onehot = jnp.where(jnp.broadcast_to(rank[:, None, :], shape) == place, 1.0, 0.0)
    weighted = onehot * jnp.broadcast_to(gate[:, None, :], shape)
    return onehot.reshape(SLOTS, TOKENS), weighted.reshape(SLOTS, TOKENS)


def halves(value):
    high = value.astype(BF)
    return high, (value - high.astype(F32)).astype(BF)


def combine(weighted, rows):
    high, low = halves(weighted)
    return dot(high, rows, 0, 0) + dot(low, rows, 0, 0)


def gain_rows(w_ref):
    unit = jnp.where(
        lax.broadcasted_iota(jnp.int32, (8, 128), 0) == lax.broadcasted_iota(jnp.int32, (8, 128), 1),
        1.0,
        0.0,
    ).astype(BF)
    rows = dot(unit, w_ref[:, QKV + OUT : COLS], 1, 1)
    return rows[0:1, :], rows[1:2, :]


def inverse_norm(u):
    return lax.rsqrt(jnp.mean(u * u, axis=-1, keepdims=True) + epsilon)


def norm_back(u, inverse, gain, upstream):
    scaled = upstream * gain
    inward = inverse * scaled - u * (inverse * inverse * inverse) * jnp.mean(
        u * scaled, axis=-1, keepdims=True
    )
    return inward, upstream * u * inverse


def rotate(u, cos, sin):
    return u * cos + pltpu.roll(u, HEAD // 2, 1) * sin


def unrotate(u, cos, sin):
    return u * cos - pltpu.roll(u, HEAD // 2, 1) * sin


def head_of(value, h):
    return value[:, h * HEAD : (h + 1) * HEAD]


def attention(x, gain, w_ref, cos, sin, allow, n_ref, qkv_ref, prob_ref, o_ref):
    n = (x * inverse_norm(x) * gain).astype(BF)
    n_ref[...] = n
    flat = dot(n, w_ref[:, 0:QKV])
    for h in range(HEADS + 1):
        qkv_ref[:, h * HEAD : (h + 1) * HEAD] = rotate(head_of(flat, h), cos, sin).astype(BF)
    qkv_ref[:, (HEADS + 1) * HEAD :] = flat[:, (HEADS + 1) * HEAD :].astype(BF)
    key = qkv_ref[:, HEADS * HEAD : (HEADS + 1) * HEAD]
    value = qkv_ref[:, (HEADS + 1) * HEAD :]
    for h in range(HEADS):
        scores = dot(qkv_ref[:, h * HEAD : (h + 1) * HEAD], key, 1, 1) * HEAD ** (-0.5)
        scores = jnp.where(allow > 0.0, scores, -1e30)
        weight = jnp.exp(scores - jnp.max(scores, axis=-1, keepdims=True))
        prob = weight / jnp.sum(weight, axis=-1, keepdims=True)
        prob_ref[h] = prob
        o_ref[:, h * HEAD : (h + 1) * HEAD] = dot(prob.astype(BF), value).astype(BF)
    return dot(o_ref[...], w_ref[:, QKV : QKV + OUT], 1, 1)


def expert_weight_copies(layer, r, local):
    core = lax.axis_index("blk")
    copies = []
    for name in ("gate", "up", "down"):
        held = getattr(r, "held_" + name)
        copies.append(local.start(getattr(r, name).at[layer, core], held.at[0]))
        copies.append(local.start(getattr(r, name + "_other").at[layer], held.at[1]))
    return copies


def expert_forward(rows, held, a_ref, b_ref):
    gate, up, down = held
    total = None
    for c in range(2):
        a = dot(rows, gate[c])
        b = dot(rows, up[c])
        a_ref[c] = a
        b_ref[c] = b
        z = (a / (1.0 + jnp.exp(-a)) * b).astype(BF)
        term = dot(z, down[c])
        total = term if total is None else total + term
    return total


def expert_backward(dy, held, a_ref, b_ref, z_ref, d_ref):
    gate, up, down = held
    total = None
    for c in range(2):
        a = a_ref[c]
        b = b_ref[c]
        sg = 1.0 / (1.0 + jnp.exp(-a))
        z_ref[:, c * HIDDEN : (c + 1) * HIDDEN] = (a * sg * b).astype(BF)
        dz = dot(dy, down[c], 1, 1)
        da = (dz * b * sg * (1.0 + a * (1.0 - sg))).astype(BF)
        db = (dz * a * sg).astype(BF)
        d_ref[:, 2 * c * HIDDEN : (2 * c + 1) * HIDDEN] = da
        d_ref[:, (2 * c + 1) * HIDDEN : (2 * c + 2) * HIDDEN] = db
        term = dot(da, gate[c], 1, 1) + dot(db, up[c], 1, 1)
        total = term if total is None else total + term
    return total


def expert_gradients(rows_ref, dy_ref, z_ref, d_ref, stage, grads, local):
    sent = []
    for q in range(4):
        if q >= 2:
            sent[q - 2].wait()
        columns = slice(q * HIDDEN, (q + 1) * HIDDEN)
        slot = q % 2
        both = dot(rows_ref[:, columns], d_ref[...], 0, 0)
        for c in range(2):
            for i in range(2):
                at = (2 * c + i) * HIDDEN
                stage[slot, 3 * c + i] = both[:, at : at + HIDDEN].astype(BF)
        low = dot(z_ref[...], dy_ref[:, columns], 0, 0)
        for c in range(2):
            stage[slot, 3 * c + 2] = low[c * HIDDEN : (c + 1) * HIDDEN].astype(BF)
        sent.append(local.start(stage.at[slot], grads.at[q]))
    return sent[2:]


def ring_devices(xyz, core, axis, steps=(1, 2, 3)):
    return [device_at(shifted(xyz, axis, by), core) for by in steps]


def arrive(copies):
    for copy in copies:
        copy.wait_recv()


class Gather:
    def __init__(self, sender, xyz, core):
        self.sender, self.xyz, self.core = sender, xyz, core

    def slab(self, job, stage, at, half=None):
        whole, lane, lanes, order = job
        index = list(at)
        for axis in order[:stage]:
            index[axis] = pl.ds(0, 4)
        if half is not None:
            index[order[0]] = pl.ds(2 * half, 2)
        return whole.at[index[0], index[1], index[2], :, pl.ds(lane, lanes)]

    def to(self, job, stage, by):
        return device_at(shifted(self.xyz, job[3][stage], by), self.core)

    def first(self, job, shard):
        source = shard.at[:, pl.ds(job[1], job[2])]
        target = self.slab(job, 0, self.xyz)
        return [self.sender.start(source, target, self.to(job, 0, by)) for by in (1, 3, 2)]

    def near(self, job, stage, steps=(1, 3)):
        block = self.slab(job, stage, self.xyz)
        return [self.sender.start(block, block, self.to(job, stage, by)) for by in steps]

    def relay(self, job, stage, near):
        copies = []
        for half, by in enumerate((1, 3)):
            near[half].wait_recv()
            at = shifted(self.xyz, job[3][stage], 4 - by)
            block = self.slab(job, stage, at, half)
            copies.append(self.sender.start(block, block, self.to(job, stage, by)))
        return copies

    def finish(self, near, relays):
        for copy in near:
            copy.wait_send()
        for copy in relays:
            copy.wait()


class ExpertSum:
    def __init__(self, r, layer, sender, local, xyz, core):
        self.r, self.sender, self.local, self.core = r, sender, local, core
        self.plus, self.minus = ring_devices(xyz, core, 0, (1, 3))
        self.grads, self.near, self.far, self.total = (
            getattr(r, f"{name}_{layer}") for name in ("grads", "near", "far", "total")
        )
        self.quarter = [shifted(xyz, 0, by)[0] for by in range(4)]

    def half(self, by, half):
        return self.grads.at[self.quarter[by], pl.ds(3 * half, 3)]

    def near_half(self, side, half):
        return self.near.at[side, pl.ds(3 * half, 3)]

    def start(self):
        go = self.sender.start
        self.passed = [
            go(self.half(2, 0), self.far.at[0], self.plus),
            go(self.half(2, 1), self.far.at[1], self.minus),
        ]
        self.plain = [
            go(self.half(1, 1), self.near_half(0, 1), self.plus),
            go(self.half(3, 0), self.near_half(1, 0), self.minus),
        ]

    def relay(self):
        r, load = self.r, self.local.start
        own = [load(self.half(by, side), r.own.at[side]) for side, by in enumerate((1, 3))]
        came = []
        for side in range(2):
            self.passed[side].wait_recv()
            came.append(load(self.far.at[side], r.work.at[side]))
        for side, target in enumerate((self.plus, self.minus)):
            own[side].wait()
            came[side].wait()
            for i in range(3):
                value = r.own[side, i].astype(F32) + r.work[side, i].astype(F32)
                r.work[side, i] = value.astype(BF)
            self.plain.append(
                self.sender.start(r.work.at[side], self.near_half(side, side), target)
            )

    def finish(self):
        r, load = self.r, self.local.start
        for copy in self.plain:
            copy.wait()
        for copy in self.passed:
            copy.wait_send()

        def bring(i, slot):
            return [
                load(self.grads.at[self.quarter[0], i], r.own.at[slot, 0]),
                load(self.near.at[0, i], r.own.at[slot, 1]),
                load(self.near.at[1, i], r.own.at[slot, 2]),
            ]

        order = (3, 4, 5, 0, 1, 2)
        loads = [bring(order[0], 0)]
        for k, i in enumerate(order):
            if k < 5:
                loads.append(bring(order[k + 1], (k + 1) % 2))
            for copy in loads[k]:
                copy.wait()
            slot = k % 2
            value = r.own[slot, 0].astype(F32) + r.own[slot, 1].astype(F32)
            r.ship[k] = (value + r.own[slot, 2].astype(F32)).astype(BF)
            if k == 2:
                across = self.sender.start(
                    r.ship.at[pl.ds(0, 3)], self.total.at[self.core], partner()
                )
        stay = load(r.ship.at[pl.ds(3, 3)], self.total.at[self.core])
        stay.wait()
        across.wait()


def tables(r):
    first = r.lengths[0, 0]
    second = first + r.lengths[0, 1]

    def place(index):
        segment = jnp.where(index >= first, 1, 0) + jnp.where(index >= second, 1, 0)
        start = jnp.where(segment == 0, 0, jnp.where(segment == 1, first, second))
        return segment, index - start

    shape = (TOKENS, TOKENS)
    lane = lax.broadcasted_iota(jnp.int32, shape, 1)
    row_segment, row_place = place(lax.broadcasted_iota(jnp.int32, shape, 0))
    key_segment, key_place = place(lane)
    allowed = (row_segment == key_segment) & (key_place <= row_place)
    r.allow[...] = jnp.where(allowed, 1.0, 0.0)
    half = jnp.where(lane < HEAD // 2, lane, lane - HEAD // 2).astype(F32)
    frequency = jnp.exp(half * (-2.0 / HEAD * math.log(rope_base)))
    angles = row_place.astype(F32) * frequency
    sign = jnp.where(lane < HEAD // 2, -1.0, 1.0)
    r.cos[...] = jnp.cos(angles)
    r.sin[...] = jnp.sin(angles) * sign


def assemble(r):
    square = (SHARD, SHARD)
    eye = lax.broadcasted_iota(jnp.int32, square, 0) == lax.broadcasted_iota(jnp.int32, square, 1)
    lane = lax.broadcasted_iota(jnp.int32, (SHARD, 128), 1)
    for l in range(LAYERS):
        r.shard[l, :, 0:768] = r.query[l]
        r.shard[l, :, 768:896] = r.key[l]
        r.shard[l, :, 896:QKV] = r.value[l]
        r.shard[l, :, QKV : QKV + OUT] = r.out[l]
        column = jnp.zeros((SHARD, 128), F32)
        for i, gain in enumerate((r.gain_a, r.gain_e)):
            spread = jnp.broadcast_to(gain[l : l + 1, :].astype(F32), square)
            spread = jnp.where(eye, spread, 0.0).astype(BF)
            column = column + dot(spread, jnp.where(lane == i, 1.0, 0.0).astype(BF))
        r.shard[l, :, QKV + OUT :] = column.astype(BF)


def gather_body(r):
    xyz, core = coords(), lax.axis_index("blk")
    count = hail([d for axis in range(3) for d in ring_devices(xyz, core, axis)] + [partner()])
    sender, local = Sender(r.send, r.recv), Local(r.local)
    mine = pl.ds(pl.multiple_of(core * HALF, HALF), HALF)
    here = [
        local.start(r.tok, r.tokens.at[:, mine]),
        local.start(r.cot_half, r.cot.at[:, mine]),
    ]
    assemble(r)
    here.append(local.start(r.shard.at[0], r.w0.at[xyz[0], xyz[1], xyz[2]]))
    here.append(local.start(r.shard.at[1], r.shard1))
    heard(count)
    gather = Gather(sender, xyz, core)
    now = [(r.w0, p * PART, PART, order) for p, order in enumerate(ORDERS)]
    first = [c for job in now for c in gather.first(job, r.shard.at[0])]
    others = [
        sender.start(r.tok, r.tokens.at[:, mine], partner()),
        sender.start(r.cot_half, r.cot.at[:, mine], partner()),
    ]
    for l in range(LAYERS):
        for name in ("gate", "up", "down"):
            ref = getattr(r, name).at[l, 1 - core]
            others.append(sender.start(ref, getattr(r, name + "_other").at[l], partner()))
    tables(r)
    for copy in here:
        copy.wait()
    arrive(first)
    near = [c for job in now for c in gather.near(job, 1, (1, 3, 2))]
    arrive(near)
    last = [gather.near(job, 2) for job in now]
    relays = [gather.relay(job, 2, n) for job, n in zip(now, last)]
    for n, relay in zip(last, relays):
        gather.finish(n, relay)
    for copy in others:
        copy.wait()
    for copy in first + near:
        copy.wait_send()


KEPT = dict(
    h=((TOKENS, WIDE), F32),
    n=((TOKENS, WIDE), BF),
    qkv=((TOKENS, QKV), BF),
    prob=((HEADS, TOKENS, TOKENS), F32),
    o=((TOKENS, OUT), BF),
    onehot=((SLOTS, TOKENS), BF),
    weighted=((SLOTS, TOKENS), F32),
)
KEPT_SPACE = {name: pltpu.VMEM(*spec) for name, spec in KEPT.items()}
HELD = dict(
    held_gate=pltpu.VMEM((2, WIDE, HIDDEN), BF),
    held_up=pltpu.VMEM((2, WIDE, HIDDEN), BF),
    held_down=pltpu.VMEM((2, HIDDEN, WIDE), BF),
)
ROWS = ((SLOTS, WIDE), BF)
INNER = ((2, SLOTS, HIDDEN), F32)
BLOCKS = ((PEERS, CAP, WIDE), BF)
PLANE = ((TOKENS, WIDE), F32)
GRADS = ((4, 6, HIDDEN, HIDDEN), BF)
BACKWARD = dict(
    z=pltpu.VMEM((SLOTS, 2 * HIDDEN), BF),
    d=pltpu.VMEM((SLOTS, 4 * HIDDEN), BF),
    dy=pltpu.VMEM(*ROWS),
    stage=pltpu.VMEM((2, 6, HIDDEN, HIDDEN), BF),
)


def sems(**counts):
    return {name: pltpu.SemaphoreType.DMA((n,)) for name, n in counts.items()}


def spaces(**specs):
    return {name: pltpu.VMEM(*spec) for name, spec in specs.items()}


def front(r, x, pair, local, then=None):
    gain_a, gain_e = gain_rows(r.w)
    r.part0[...] = attention(
        x, gain_a, r.w, r.cos[...], r.sin[...], r.allow[...], r.n, r.qkv, r.prob, r.o
    )
    copy = pair.start(r.part0, r.theirs0, partner())
    for name in ("n", "qkv", "prob", "o", "onehot", "weighted"):
        local.keep(getattr(r, name), getattr(r, name + "_out"))
    begun = then() if then else None
    copy.wait_recv()
    h = x + (r.part0[...] + r.theirs0[...])
    copy.wait_send()
    r.h[...] = h
    local.keep(r.h, r.h_out)
    return (h * inverse_norm(h) * gain_e).astype(BF), begun


def forward_body(layer, r):
    xyz, core = coords(), lax.axis_index("blk")
    local, pair = Local(r.local), Sender(r.pair_send, r.pair_recv)
    load = local.start(r.w_any, r.w)
    count = hail(peers() + ring_devices(xyz, core, 0))
    here = local.start(r.shard, r.w1.at[xyz[0], xyz[1], xyz[2]])
    loads = expert_weight_copies(layer, r, local)
    hot, heavy = slot_matrices(r.ids[layer], r.weights[layer])
    r.onehot[...] = hot.astype(BF)
    r.weighted[...] = heavy
    heard(count)
    gather = Gather(Sender(r.wide_send, r.wide_recv), xyz, core)
    jobs = [(r.w1, *job) for job in LATER]
    sent = [c for job in jobs for c in gather.first(job, r.shard)]
    load.wait()

    def second():
        here.wait()
        arrive(sent)
        return [c for job in jobs for c in gather.near(job, 1, (1, 3, 2))]

    m, middle = front(r, r.x[...].astype(F32), pair, local, second)
    store_rows(r.sent, dot(r.onehot[...], m))
    arrive(middle)
    near = [gather.near(job, 2) for job in jobs]
    exchange_start(r.sent, r.came, r.send0, r.recv0)
    for copy in loads:
        copy.wait()
    exchange_recv(r.sent, r.came, r.send0, r.recv0)
    relays = {i: gather.relay(jobs[i], 2, near[i]) for i in (2, 3)}
    r.rows[...] = rows_of(r.came)
    local.keep(r.rows, r.rows_out)
    held = (r.held_gate, r.held_up, r.held_down)
    result = expert_forward(r.rows[...], held, r.a, r.b)
    exchange_sent(r.sent, r.came, r.send0, r.recv0)
    store_rows(r.sent, result)
    exchange_start(r.sent, r.back, r.send1, r.recv1)
    for i in (0, 1):
        relays[i] = gather.relay(jobs[i], 2, near[i])
    local.keep(r.a, r.a_out)
    local.keep(r.b, r.b_out)
    exchange_recv(r.sent, r.back, r.send1, r.recv1)
    r.part1[...] = combine(r.weighted[...], rows_of(r.back))
    copy = pair.start(r.part1, r.theirs1, partner())
    copy.wait_recv()
    r.stream[...] = r.h[...] + (r.part1[...] + r.theirs1[...])
    copy.wait_send()
    exchange_sent(r.sent, r.back, r.send1, r.recv1)
    for i in range(4):
        gather.finish(near[i], relays[i])
    for c in sent + middle:
        c.wait_send()
    local.wait_kept()


def middle_body(layer, r):
    local, pair = Local(r.local), Sender(r.pair_send, r.pair_recv)
    load = local.start(r.w_any, r.w)
    count = hail(peers())
    loads = expert_weight_copies(layer, r, local)
    hot, heavy = slot_matrices(r.ids[layer], r.weights[layer])
    r.onehot[...] = hot.astype(BF)
    r.weighted[...] = heavy
    slot_weight = jnp.sum(heavy, axis=1, keepdims=True)
    store_rows(r.sent_g, dot(r.onehot[...], r.cot[...]) * slot_weight)
    heard(count)
    exchange_start(r.sent_g, r.came_g, r.send1, r.recv1)
    load.wait()
    m, _ = front(r, r.x[...], pair, local)
    store_rows(r.sent, dot(r.onehot[...], m))
    exchange_start(r.sent, r.came, r.send0, r.recv0)
    exchange_recv(r.sent_g, r.came_g, r.send1, r.recv1)
    r.dy[...] = rows_of(r.came_g)
    for copy in loads:
        copy.wait()
    exchange_recv(r.sent, r.came, r.send0, r.recv0)
    r.rows[...] = rows_of(r.came)
    held = (r.held_gate, r.held_up, r.held_down)
    result = expert_forward(r.rows[...], held, r.a, r.b)
    exchange_sent(r.sent, r.came, r.send0, r.recv0)
    store_rows(r.sent, result)
    local.keep(r.sent, r.y_rows)
    store_rows(r.turn, expert_backward(r.dy[...], held, r.a, r.b, r.z, r.d))
    local.keep(r.turn, r.m_back)
    local.kept += expert_gradients(r.rows, r.dy, r.z, r.d, r.stage, r.grads, local)
    exchange_sent(r.sent_g, r.came_g, r.send1, r.recv1)
    local.wait_kept()


def turned(value):
    return value.astype(F32).T.reshape(4, 4, 4, SHARD, TOKENS).astype(BF)


def own_part(ref, axis, index):
    return ref.at[:, index] if axis == 1 else ref.at[:, :, index]


def share_factor(ref, into, axis, sender, xyz, core):
    copies = []
    for by in (1, 3, 2):
        there = shifted(xyz, axis, by)
        copies.append(
            sender.start(own_part(ref, axis, there[axis]), into.at[by - 1], device_at(there, core))
        )
    return copies


def share_whole(ref, axis, sender, xyz, core):
    return [
        sender.start(
            ref.at[pl.ds(0, TOKENS)],
            ref.at[pl.ds(by * TOKENS, TOKENS)],
            device_at(shifted(xyz, axis, by), core),
        )
        for by in (1, 3, 2)
    ]


def quarter_sum(own, came, axis, xyz, right):
    first = own_part(own, axis, xyz[axis])[...]
    pieces = [first] + [came[i] for i in range(3)]
    left = [p.astype(F32).reshape(HIDDEN, TOKENS).astype(BF) for p in pieces]
    return dot(jnp.concatenate(left, axis=1), right[...])


def back_body(r):
    xyz, core = coords(), lax.axis_index("blk")
    local, pair = Local(r.local), Sender(r.pair_send, r.pair_recv)
    sender = Sender(r.wide_send, r.wide_recv)

    def load_layer(l):
        names = ("w", "h", "n", "qkv", "prob", "o")
        return [local.start(getattr(r, f"{name}_{l}"), getattr(r, name)) for name in names]

    loads = load_layer(1)
    count = hail(peers() + ring_devices(xyz, core, 0))
    sums = [ExpertSum(r, l, sender, local, xyz, core) for l in range(LAYERS)]
    heard(count)
    came_m, onehot, back_sems = (
        (r.came_0, r.came_1),
        (r.onehot_0, r.onehot_1),
        ((r.send2, r.recv2), (r.send0, r.recv0)),
    )
    m_rows = (r.turn, r.m_1)
    exchange_start(r.m_1, r.came_1, r.send0, r.recv0)
    sums[1].start()
    weights = expert_weight_copies(0, r, local)
    weights += [local.start(getattr(r, name + "_0"), getattr(r, name)) for name in ("rows", "a", "b")]
    for copy in loads:
        copy.wait()
    shared = [[], []]
    scale = HEAD ** (-0.5)
    row = lax.broadcasted_iota(jnp.int32, (8, WIDE), 0)
    r.gain_sum[1] = jnp.zeros((8, WIDE), F32)
    inner, across = [None] * 2, [None] * 2
    for l in (1, 0):
        x = (r.stream if l == 1 else r.tokens)[...].astype(F32)
        gain_a, gain_e = gain_rows(r.w)
        r.n_turned[l] = turned(r.n[...])
        r.o_all[l, 0:TOKENS] = r.o[...]
        exchange_recv(m_rows[l], came_m[l], *back_sems[l])
        r.part[0] = dot(onehot[l][...], rows_of(came_m[l]), 0, 0)
        inner[l] = pair.start(r.part.at[0], r.theirs.at[l, 0], partner())
        shared[l] += share_factor(r.n_turned.at[l], r.n_came.at[l], 1, sender, xyz, core)
        shared[l] += share_whole(r.o_all.at[l], 2, sender, xyz, core)
        if l == 0:
            shared[1] += share_whole(r.lin_all.at[1], 1, sender, xyz, core)
        inner[l].wait_recv()
        dm = r.part[0] + r.theirs[l, 0]
        hidden = r.h[...]
        inward, gain_grad_e = norm_back(hidden, inverse_norm(hidden), gain_e, dm)
        gh = (r.cot[...].astype(F32) if l == 1 else r.flow[...]) + inward
        r.flow[...] = gh
        da = gh.astype(BF)
        r.da_turned[l] = turned(gh)
        shared[l] += share_factor(r.da_turned.at[l], r.da_came.at[l], 2, sender, xyz, core)
        do = dot(da, r.w[:, QKV : QKV + OUT]).astype(BF)
        key = r.qkv[:, HEADS * HEAD : (HEADS + 1) * HEAD]
        value = r.qkv[:, (HEADS + 1) * HEAD :]
        key_grad, value_grad = None, None
        cosine, sine = r.cos[...], r.sin[...]
        lin = r.lin_all.at[l]
        for i in range(HEADS):
            prob_i = r.prob[i]
            do_i = head_of(do, i)
            q_i = r.qkv[:, i * HEAD : (i + 1) * HEAD]
            dprob = dot(do_i, value, 1, 1)
            centre = jnp.sum(prob_i * dprob, axis=-1, keepdims=True)
            ds = (prob_i * (dprob - centre)).astype(BF)
            dq = dot(ds, key) * scale
            lin[0:TOKENS, i * HEAD : (i + 1) * HEAD] = unrotate(dq, cosine, sine).astype(BF)
            dk = dot(ds, q_i, 0, 0)
            dv = dot(prob_i.astype(BF), do_i, 0, 0)
            key_grad = dk if key_grad is None else key_grad + dk
            value_grad = dv if value_grad is None else value_grad + dv
        lin[0:TOKENS, HEADS * HEAD : (HEADS + 1) * HEAD] = unrotate(
            key_grad * scale, cosine, sine
        ).astype(BF)
        lin[0:TOKENS, (HEADS + 1) * HEAD :] = value_grad.astype(BF)
        r.part[1] = dot(lin[0:TOKENS, :], r.w[:, 0:QKV], 1, 1)
        across[l] = pair.start(r.part.at[1], r.theirs.at[l, 1], partner())
        if l == 1:
            r.kept_half[...] = jnp.where(core == 1, r.h[:, HALF:], r.h[:, :HALF])
            loads = load_layer(0)
        else:
            shared[0] += share_whole(r.lin_all.at[0], 1, sender, xyz, core)
            exchange_start(r.y_1, r.came_1, r.send3, r.recv3)
        across[l].wait_recv()
        dn = r.part[1] + r.theirs[l, 1]
        inward, gain_grad_a = norm_back(x, inverse_norm(x), gain_a, dn)
        flow = r.flow[...] + inward
        gains = r.gain_sum[1]
        for i, grad in enumerate((gain_grad_a, gain_grad_e)):
            grad = jnp.sum(grad, axis=0, keepdims=True)
            gains = jnp.where(row == 2 * l + i, jnp.broadcast_to(grad, (8, WIDE)), gains)
        r.gain_sum[1] = gains
        inner[l].wait_send()
        across[l].wait_send()
        if l == 0:
            r.tokens_grad[...] = jnp.where(core == 1, flow[:, HALF:], flow[:, :HALF])
            continue
        r.flow[...] = flow
        slot_weight = jnp.sum(r.weighted_0[...], axis=1, keepdims=True)
        high, low = halves(flow)
        hot = r.onehot_0[...]
        store_rows(r.sent, (dot(hot, high) + dot(hot, low)) * slot_weight)
        exchange_start(r.sent, r.came_g, r.send1, r.recv1)
        sums[1].relay()
        for copy in weights:
            copy.wait()
        exchange_recv(r.sent, r.came_g, r.send1, r.recv1)
        r.dy[...] = rows_of(r.came_g)
        held = (r.held_gate, r.held_up, r.held_down)
        store_rows(r.turn, expert_backward(r.dy[...], held, r.a, r.b, r.z, r.d))
        exchange_start(r.turn, r.came_0, r.send2, r.recv2)
        for copy in expert_gradients(r.rows, r.dy, r.z, r.d, r.stage, r.grads_0, local):
            copy.wait()
        sums[0].start()
        sums[1].finish()
        for copy in loads:
            copy.wait()
    finish_sums(r, shared, sums[0], sender, xyz, core)
    exchange_recv(r.y_1, r.came_1, r.send3, r.recv3)
    mixed = combine(r.weighted_1[...], rows_of(r.came_1))
    r.half[...] = jnp.where(core == 1, mixed[:, :HALF], mixed[:, HALF:])
    third = pair.start(r.half, r.half_theirs, partner())
    own = jnp.where(core == 1, mixed[:, HALF:], mixed[:, :HALF])
    third.wait()
    r.block_out[...] = (r.kept_half[...] + (own + r.half_theirs[...])).astype(BF)
    sums[0].finish()
    exchange_sent(r.m_1, r.came_1, r.send0, r.recv0)
    exchange_sent(r.sent, r.came_g, r.send1, r.recv1)
    exchange_sent(r.turn, r.came_0, r.send2, r.recv2)
    exchange_sent(r.y_1, r.came_1, r.send3, r.recv3)


def late_start(r, l, sender, xyz, core):
    copies = []
    for ref, came, axis in ((r.sum_a, r.near_a, 2), (r.sum_b, r.near_b, 1)):
        for by in (1, 3, 2):
            there = shifted(xyz, axis, by)
            copies.append(
                sender.start(ref.at[l, :, there[axis]], came.at[l, by - 1], device_at(there, core))
            )
    return copies


def late_middle(r, l, sender, xyz, core, copies):
    arrive(copies)
    for ref, came, axis, lanes in (
        (r.sum_a, r.near_a, 2, slice(0, QKV)),
        (r.sum_b, r.near_b, 1, slice(QKV, QKV + OUT)),
    ):
        total = ref[l, :, xyz[axis]].astype(F32)
        for i in range(3):
            total = total + came[l, i].astype(F32)
        r.line[l, :, :, lanes] = total.astype(BF)
    copies = []
    for by in (1, 3, 2):
        there = shifted(xyz, 0, by)
        copies.append(
            sender.start(r.line.at[l, there[0]], r.line_came.at[l, by - 1], device_at(there, core))
        )
    return copies


def late_end(r, l, xyz, copies):
    for copy in copies:
        copy.wait()
    total = r.line[l, xyz[0]].astype(F32)
    for i in range(3):
        total = total + r.line_came[l, i].astype(F32)
    r.weight_grad[l] = total


def gains_along(r, axis, sender, xyz, core):
    return [
        sender.start(r.gain_sum.at[axis], r.gain_came.at[axis, by - 1], device_at(shifted(xyz, axis, by), core))
        for by in (1, 3, 2)
    ]


def gains_next(r, axis, copies):
    for copy in copies:
        copy.wait()
    total = r.gain_sum[axis]
    for i in range(3):
        total = total + r.gain_came[axis, i]
    return total


def finish_sums(r, shared, below, sender, xyz, core):
    along = gains_along(r, 1, sender, xyz, core)
    below.relay()
    begun = []
    for l in (1, 0):
        arrive(shared[l])
        wide = (4, 4, SHARD, QKV)
        total = quarter_sum(r.n_turned.at[l], r.n_came.at[l], 1, xyz, r.lin_all.at[l])
        r.sum_a[l] = total.reshape(wide).astype(BF)
        wide = (4, 4, SHARD, OUT)
        total = quarter_sum(r.da_turned.at[l], r.da_came.at[l], 2, xyz, r.o_all.at[l])
        r.sum_b[l] = total.reshape(wide).astype(BF)
        begun.append(late_start(r, l, sender, xyz, core))
    r.gain_sum[2] = gains_next(r, 1, along)
    along = gains_along(r, 2, sender, xyz, core)
    ended = [late_middle(r, l, sender, xyz, core, c) for l, c in zip((1, 0), begun)]
    r.gain_sum[0] = gains_next(r, 2, along)
    along = gains_along(r, 0, sender, xyz, core)
    for l, copies in zip((1, 0), ended):
        late_end(r, l, xyz, copies)
    r.gain_total[...] = gains_next(r, 0, along)
    for copy in shared[0] + shared[1] + begun[0] + begun[1]:
        copy.wait_send()


def finish_body(r):
    local = Local(r.local)
    loads = [
        [local.start(total.at[:, i], r.narrow.at[l, i]) for i in range(3)]
        for l, total in enumerate((r.total_below, r.total_above))
    ]
    r.block_out[...] = r.block_in[...]
    r.tokens_grad[...] = r.tokens_in[...]
    place = (lax.axis_index("dp") * PEERS + lax.axis_index("expert")) * SHARD
    near = pltpu.roll(r.gain_total[...], lax.rem(WIDE - place, WIDE), 1)
    for l in range(LAYERS):
        r.gain_a[l : l + 1, :] = near[2 * l : 2 * l + 1, :SHARD]
        r.gain_e[l : l + 1, :] = near[2 * l + 1 : 2 * l + 2, :SHARD]
        r.query[l] = r.weight_grad[l, :, :768]
        r.key[l] = r.weight_grad[l, :, 768:896]
        r.value[l] = r.weight_grad[l, :, 896:QKV]
        r.out[l] = r.weight_grad[l, :, QKV:]
    for l in range(LAYERS):
        for i, out in enumerate((r.gate, r.up, r.down)):
            loads[l][i].wait()
            r.broad[l, i] = r.narrow[l, i].astype(F32)
            local.keep(r.broad.at[l, i], out.at[l])
    local.wait_kept()


def kernel_call(body, name, cid, ins, outs, scratch, aliases=()):
    names = [*ins, *outs, *scratch]
    assert len(set(names)) == len(names)

    def kernel(*refs):
        body(types.SimpleNamespace(**dict(zip(names, refs))))

    results = pl.pallas_call(
        kernel,
        out_shape=[jax.ShapeDtypeStruct(shape, kind) for shape, kind, _ in outs.values()],
        in_specs=[space for _, space in ins.values()],
        out_specs=[space for _, _, space in outs.values()],
        scratch_shapes=list(scratch.values()),
        input_output_aliases={list(ins).index(a): list(outs).index(b) for a, b in aliases},
        compiler_params=pltpu.CompilerParams(
            collective_id=cid, has_side_effects=cid is not None, vmem_limit_bytes=LIMIT
        ),
        name=name,
    )(*[array for array, _ in ins.values()])
    return types.SimpleNamespace(**dict(zip(outs, results)))


def per_device(
    tokens_in,
    seq_lengths,
    expert_ids,
    gate_weights,
    attention_gain,
    query_weight,
    key_weight,
    value_weight,
    out_weight,
    expert_gain,
    gate_weight,
    up_weight,
    down_weight,
    cotangent,
):
    cube = (4, 4, 4, SHARD, COLS)
    own = dict(gate=(gate_weight, ANY), up=(up_weight, ANY), down=(down_weight, ANY))
    start = kernel_call(
        gather_body,
        "gather",
        1,
        dict(
            lengths=(seq_lengths, SMEM),
            query=(query_weight, VMEM),
            key=(key_weight, VMEM),
            value=(value_weight, VMEM),
            out=(jnp.swapaxes(out_weight, 1, 2), VMEM),
            gain_a=(attention_gain, VMEM),
            gain_e=(expert_gain, VMEM),
            tok=(tokens_in, VMEM),
            cot_half=(cotangent, VMEM),
            **own,
        ),
        dict(
            w0=(cube, BF, ANY),
            shard1=((SHARD, COLS), BF, ANY),
            tokens=((TOKENS, WIDE), BF, VMEM),
            cot=((TOKENS, WIDE), BF, VMEM),
            cos=((TOKENS, HEAD), F32, VMEM),
            sin=((TOKENS, HEAD), F32, VMEM),
            allow=((TOKENS, TOKENS), F32, VMEM),
            gate_other=((LAYERS, WIDE, HIDDEN), BF, ANY),
            up_other=((LAYERS, WIDE, HIDDEN), BF, ANY),
            down_other=((LAYERS, HIDDEN, WIDE), BF, ANY),
        ),
        dict(
            shard=pltpu.VMEM((LAYERS, SHARD, COLS), BF),
            **sems(send=72, recv=72, local=4),
        ),
    )
    experts = dict(
        own,
        gate_other=(start.gate_other, ANY),
        up_other=(start.up_other, ANY),
        down_other=(start.down_other, ANY),
    )
    trig = dict(cos=(start.cos, VMEM), sin=(start.sin, VMEM))
    routing = dict(
        ids=(jnp.swapaxes(expert_ids, 1, 2), VMEM), weights=(jnp.swapaxes(gate_weights, 1, 2), VMEM)
    )
    kept_out = {name + "_out": (*spec, ANY) for name, spec in KEPT.items()}
    w_space = dict(w=pltpu.VMEM((WIDE, COLS), BF))
    exchanges = sems(send0=PEERS, recv0=PEERS, send1=PEERS, recv1=PEERS, pair_send=5, pair_recv=5)
    w0 = start.w0.reshape(WIDE, COLS)
    below = kernel_call(
        functools.partial(forward_body, 0),
        "forward",
        2,
        dict(
            x=(start.tokens, VMEM),
            w_any=(w0, ANY),
            shard=(start.shard1, VMEM),
            allow=(start.allow, VMEM),
            **trig,
            **routing,
            **experts,
        ),
        dict(
            w1=(cube, BF, ANY),
            stream=(*PLANE, VMEM),
            rows_out=(*ROWS, ANY),
            a_out=(*INNER, ANY),
            b_out=(*INNER, ANY),
            **kept_out,
        ),
        dict(
            **w_space,
            **KEPT_SPACE,
            **HELD,
            **spaces(sent=BLOCKS, came=BLOCKS, back=BLOCKS, rows=ROWS, a=INNER, b=INNER),
            **spaces(part0=PLANE, theirs0=PLANE, part1=PLANE, theirs1=PLANE),
            **exchanges,
            **sems(wide_send=40, wide_recv=40, local=20),
        ),
    )
    w1 = below.w1.reshape(WIDE, COLS)
    above = kernel_call(
        functools.partial(middle_body, 1),
        "middle",
        3,
        dict(
            x=(below.stream, VMEM),
            cot=(start.cot, VMEM),
            w_any=(w1, ANY),
            allow=(start.allow, VMEM),
            **trig,
            **routing,
            **experts,
        ),
        dict(
            y_rows=(*BLOCKS, ANY),
            m_back=(*BLOCKS, ANY),
            grads=(*GRADS, ANY),
            **kept_out,
        ),
        dict(
            **w_space,
            **KEPT_SPACE,
            **HELD,
            **spaces(sent=BLOCKS, came=BLOCKS, sent_g=BLOCKS, came_g=BLOCKS, turn=BLOCKS),
            **spaces(rows=ROWS, a=INNER, b=INNER, part0=PLANE, theirs0=PLANE),
            **BACKWARD,
            **exchanges,
            **sems(local=20),
        ),
    )

    part_a, part_b = (4, 4, SHARD, QKV), (4, 4, SHARD, OUT)
    total = ((2, 3, HIDDEN, HIDDEN), BF, ANY)
    near, far = ((2, 6, HIDDEN, HIDDEN), BF, ANY), ((2, 3, HIDDEN, HIDDEN), BF, ANY)
    factor, quarter = (4, 4, 4, SHARD, TOKENS), (3, 4, 4, SHARD, TOKENS)
    by_layer = {}
    for l, of in enumerate((below, above)):
        for name in ("h", "n", "qkv", "prob", "o"):
            by_layer[f"{name}_{l}"] = (getattr(of, name + "_out"), ANY)
        for name in ("onehot", "weighted"):
            by_layer[f"{name}_{l}"] = (getattr(of, name + "_out"), VMEM)
    end = kernel_call(
        back_body,
        "backward",
        4,
        dict(
            stream=(below.stream, VMEM),
            tokens=(start.tokens, VMEM),
            cot=(start.cot, VMEM),
            w_0=(w0, ANY),
            w_1=(w1, ANY),
            **trig,
            **by_layer,
            m_1=(above.m_back, ANY),
            y_1=(above.y_rows, ANY),
            grads_1=(above.grads, ANY),
            rows_0=(below.rows_out, ANY),
            a_0=(below.a_out, ANY),
            b_0=(below.b_out, ANY),
            **experts,
        ),
        dict(
            block_out=((TOKENS, HALF), BF, VMEM),
            tokens_grad=((TOKENS, HALF), F32, VMEM),
            weight_grad=((LAYERS, SHARD, QKV + OUT), F32, VMEM),
            gain_total=((8, WIDE), F32, VMEM),
            total_0=total,
            total_1=total,
            grads_0=(*GRADS, ANY),
            near_0=near,
            near_1=near,
            far_0=far,
            far_1=far,
        ),
        dict(
            **w_space,
            **HELD,
            **BACKWARD,
            **{name: KEPT_SPACE[name] for name in ("h", "n", "qkv", "prob", "o")},
            **spaces(rows=ROWS, a=INNER, b=INNER, flow=PLANE),
            **spaces(sent=BLOCKS, turn=BLOCKS),
            **spaces(came_0=BLOCKS, came_1=BLOCKS, came_g=BLOCKS),
            part=pltpu.VMEM((2, TOKENS, WIDE), F32),
            theirs=pltpu.VMEM((LAYERS, 2, TOKENS, WIDE), F32),
            half=pltpu.VMEM((TOKENS, HALF), F32),
            half_theirs=pltpu.VMEM((TOKENS, HALF), F32),
            kept_half=pltpu.VMEM((TOKENS, HALF), F32),
            own=pltpu.VMEM((2, 3, HIDDEN, HIDDEN), BF),
            work=pltpu.VMEM((2, 3, HIDDEN, HIDDEN), BF),
            ship=pltpu.VMEM((6, HIDDEN, HIDDEN), BF),
            n_turned=pltpu.VMEM((LAYERS, *factor), BF),
            da_turned=pltpu.VMEM((LAYERS, *factor), BF),
            n_came=pltpu.VMEM((LAYERS, *quarter), BF),
            da_came=pltpu.VMEM((LAYERS, *quarter), BF),
            lin_all=pltpu.VMEM((LAYERS, 4 * TOKENS, QKV), BF),
            o_all=pltpu.VMEM((LAYERS, 4 * TOKENS, OUT), BF),
            sum_a=pltpu.VMEM((LAYERS, *part_a), BF),
            sum_b=pltpu.VMEM((LAYERS, *part_b), BF),
            near_a=pltpu.VMEM((LAYERS, 3, 4, SHARD, QKV), BF),
            near_b=pltpu.VMEM((LAYERS, 3, 4, SHARD, OUT), BF),
            line=pltpu.VMEM((LAYERS, 4, SHARD, QKV + OUT), BF),
            line_came=pltpu.VMEM((LAYERS, 3, SHARD, QKV + OUT), BF),
            gain_sum=pltpu.VMEM((3, 8, WIDE), F32),
            gain_came=pltpu.VMEM((3, 3, 8, WIDE), F32),
            **exchanges,
            **sems(send2=PEERS, recv2=PEERS, send3=PEERS, recv3=PEERS),
            **sems(wide_send=68, wide_recv=68, local=80),
        ),
    )
    expert_out = ((LAYERS, 2, HIDDEN, HIDDEN), F32, ANY)
    out = kernel_call(
        finish_body,
        "finish",
        None,
        dict(
            block_in=(end.block_out, VMEM),
            tokens_in=(end.tokens_grad, VMEM),
            total_above=(end.total_1, ANY),
            total_below=(end.total_0, ANY),
            weight_grad=(end.weight_grad, VMEM),
            gain_total=(end.gain_total, VMEM),
        ),
        dict(
            block_out=((TOKENS, HALF), BF, VMEM),
            tokens_grad=((TOKENS, HALF), F32, VMEM),
            gain_a=((LAYERS, SHARD), F32, VMEM),
            query=((LAYERS, SHARD, 768), F32, VMEM),
            key=((LAYERS, SHARD, 128), F32, VMEM),
            value=((LAYERS, SHARD, 128), F32, VMEM),
            out=((LAYERS, SHARD, OUT), F32, VMEM),
            gain_e=((LAYERS, SHARD), F32, VMEM),
            gate=expert_out,
            up=expert_out,
            down=expert_out,
        ),
        dict(
            narrow=pltpu.VMEM((LAYERS, 3, 2, HIDDEN, HIDDEN), BF),
            broad=pltpu.VMEM((LAYERS, 3, 2, HIDDEN, HIDDEN), F32),
            **sems(local=14),
        ),
    )
    return (
        out.block_out,
        out.tokens_grad,
        out.gain_a,
        out.query,
        out.key,
        out.value,
        jnp.swapaxes(out.out, 1, 2),
        out.gain_e,
        out.gate,
        out.up,
        out.down,
    )


def solution(mesh):
    placed = (
        P(("dp", "expert"), "blk"),
        P(("dp", "expert"), None),
        P(None, ("dp", "expert"), None),
        P(None, ("dp", "expert"), None),
        P(None, ("dp", "expert")),
        P(None, ("dp", "expert"), "blk"),
        P(None, ("dp", "expert"), "blk"),
        P(None, ("dp", "expert"), "blk"),
        P(None, "blk", ("dp", "expert")),
        P(None, ("dp", "expert")),
        P(None, "expert", None, "blk"),
        P(None, "expert", None, "blk"),
        P(None, "expert", "blk", None),
        P(("dp", "expert"), "blk"),
    )
    return jax.shard_map(
        per_device,
        mesh=mesh,
        in_specs=placed,
        out_specs=(
            P(("dp", "expert"), "blk"),
            P(("dp", "expert"), "blk"),
            P(None, ("dp", "expert")),
            P(None, ("dp", "expert"), "blk"),
            P(None, ("dp", "expert"), "blk"),
            P(None, ("dp", "expert"), "blk"),
            P(None, "blk", ("dp", "expert")),
            P(None, ("dp", "expert")),
            P(None, "expert", "dp", "blk"),
            P(None, "expert", "dp", "blk"),
            P(None, "expert", "blk", "dp"),
        ),
        check_vma=False,
    )
```

```python
import functools
import math
import types

import jax
import jax.numpy as jnp
from jax import lax
from jax.experimental import pallas as pl
from jax.experimental.pallas import tpu as pltpu
from jax.sharding import PartitionSpec as P

HEAD = 128
TOP = 4
LAYERS = 2
F32 = jnp.float32
BF = jnp.bfloat16
MESH = pl.DeviceIdType.MESH

epsilon = 1e-06
rope_base = 1000000.0

TOKENS = 128
WIDE = 1536
HALF = WIDE // 2
HEADS = 6
HIDDEN = 384
PEERS = 16
CAP = 24
SLOTS = PEERS * CAP
SHARD = 24
QKV = 1024
OUT = 768
COLS = QKV + OUT + 128
PART = COLS // 3
ORDERS = ((0, 1, 2), (1, 2, 0), (2, 0, 1))
LIMIT = 60 << 20
LATER = ((0, 768, (1, 2, 0)), (768, 768, (2, 1, 0)), (1536, 128, (0, 2, 1)), (1664, 256, (0, 1, 2)))

ANY = pl.BlockSpec(memory_space=pl.ANY)
VMEM = pl.BlockSpec(memory_space=pltpu.VMEM)
SMEM = pl.BlockSpec(memory_space=pltpu.SMEM)


def dot(a, b, ca=1, cb=0):
    return lax.dot_general(a, b, (((ca,), (cb,)), ((), ())), preferred_element_type=F32)


def coords():
    ex = lax.axis_index("expert")
    return [lax.axis_index("dp"), lax.div(ex, 4), lax.rem(ex, 4)]


def shifted(xyz, axis, by):
    moved = list(xyz)
    moved[axis] = lax.rem(xyz[axis] + by, 4)
    return moved


def device_at(xyz, core):
    return (xyz[0], xyz[1] * 4 + xyz[2], core)


def partner():
    return (lax.axis_index("dp"), lax.axis_index("expert"), 1 - lax.axis_index("blk"))


def hail(devices):
    barrier = pltpu.get_barrier_semaphore()
    for device in devices:
        pl.semaphore_signal(barrier, inc=1, device_id=device, device_id_type=MESH)
    return len(devices)


def heard(count):
    pl.semaphore_wait(pltpu.get_barrier_semaphore(), count)


def peer(step):
    dp, ex, core = (lax.axis_index(a) for a in ("dp", "expert", "blk"))
    return (dp, lax.rem(ex + step, PEERS), core)


def peers():
    return [peer(d) for d in range(1, PEERS)] + [partner()]


class Local:
    def __init__(self, sem):
        self.sem, self.at, self.kept = sem, 0, []

    def start(self, src, dst):
        assert self.at < self.sem.shape[0]
        copy = pltpu.make_async_copy(src, dst, self.sem.at[self.at])
        self.at += 1
        copy.start()
        return copy

    def keep(self, src, dst):
        self.kept.append(self.start(src, dst))

    def wait_kept(self):
        for copy in self.kept:
            copy.wait()


class Sender:
    def __init__(self, send, recv):
        self.send, self.recv, self.at = send, recv, 0

    def start(self, src, dst, device):
        assert self.at < self.send.shape[0]
        copy = pltpu.make_async_remote_copy(
            src_ref=src,
            dst_ref=dst,
            send_sem=self.send.at[self.at],
            recv_sem=self.recv.at[self.at],
            device_id=device,
            device_id_type=MESH,
        )
        self.at += 1
        copy.start()
        return copy


def step_of(k):
    row = lax.div(lax.rem(k, 8), 2)
    return 4 * row + 2 * lax.rem(k, 2) + lax.rem(row + lax.div(k, 8), 2)


class Exchange:
    def __init__(self, r, number, src, dst, back):
        self.send, self.recv = getattr(r, f"send{number}"), getattr(r, f"recv{number}")
        self.src, self.dst, self.back = src, dst, back
        self.me = lax.axis_index("expert")

    def copy(self, k):
        step = step_of(k)
        target = peer(PEERS - step if self.back else step)
        return pltpu.make_async_remote_copy(
            src_ref=self.src.at[k if self.back else target[1]],
            dst_ref=self.dst.at[self.me if self.back else k],
            send_sem=self.send.at[k],
            recv_sem=self.recv.at[k],
            device_id=target,
            device_id_type=MESH,
        )

    def own(self):
        src = self.src.at[0 if self.back else self.me]
        dst = self.dst.at[self.me if self.back else 0]
        return pltpu.make_async_copy(src, dst, self.send.at[0])

    def each(self, group, act):
        first, last = ((1, PEERS), (1, 8), (8, PEERS))[group + 1]

        def body(k, carry):
            act(self.copy(k))
            return carry

        lax.fori_loop(first, last, body, 0)

    def start(self, group=-1):
        if group <= 0:
            self.own().start()
        self.each(group, lambda copy: copy.start())

    def arrive(self, group=-1):
        if group <= 0:
            self.own().wait()
        self.each(group, lambda copy: copy.wait_recv())

    def sent(self):
        self.each(-1, lambda copy: copy.wait_send())


def rows_of(ref):
    value = ref[...]
    return value.astype(F32).reshape(value.shape[0] * CAP, WIDE).astype(BF)


def store_rows(ref, rows):
    ref[...] = rows.reshape(rows.shape[0] // CAP, CAP, WIDE).astype(BF)


def group_of(ref, group):
    return ref.at[pl.ds(8 * group, 8)]


def slot_matrices(ids, weights):
    core = lax.axis_index("blk")
    expert = 2 * lax.broadcasted_iota(jnp.int32, (PEERS, TOKENS), 0) + core
    chosen = jnp.zeros((PEERS, TOKENS), F32)
    gate = jnp.zeros((PEERS, TOKENS), F32)
    for j in range(TOP):
        hit = jnp.where(ids[j : j + 1, :] == expert, 1.0, 0.0)
        chosen = chosen + hit
        gate = gate + hit * weights[j : j + 1, :]
    before = lax.broadcasted_iota(jnp.int32, (TOKENS, TOKENS), 0) < lax.broadcasted_iota(
        jnp.int32, (TOKENS, TOKENS), 1
    )
    rank = dot(chosen.astype(BF), jnp.where(before, 1.0, 0.0).astype(BF))
    rank = jnp.where(chosen > 0.0, rank, -1.0)
    shape = (PEERS, CAP, TOKENS)
    place = lax.broadcasted_iota(jnp.int32, shape, 1).astype(F32)
    onehot = jnp.where(jnp.broadcast_to(rank[:, None, :], shape) == place, 1.0, 0.0)
    weighted = onehot * jnp.broadcast_to(gate[:, None, :], shape)
    return onehot.reshape(SLOTS, TOKENS), weighted.reshape(SLOTS, TOKENS)


def halves(value):
    high = value.astype(BF)
    return high, (value - high.astype(F32)).astype(BF)


def combine(weighted, rows):
    high, low = halves(weighted)
    return dot(high, rows, 0, 0) + dot(low, rows, 0, 0)


def gain_rows(w_ref):
    unit = jnp.where(
        lax.broadcasted_iota(jnp.int32, (8, 128), 0) == lax.broadcasted_iota(jnp.int32, (8, 128), 1),
        1.0,
        0.0,
    ).astype(BF)
    rows = dot(unit, w_ref[:, QKV + OUT : COLS], 1, 1)
    return rows[0:1, :], rows[1:2, :]


def inverse_norm(u):
    return lax.rsqrt(jnp.mean(u * u, axis=-1, keepdims=True) + epsilon)


def norm_back(u, inverse, gain, upstream):
    scaled = upstream * gain
    inward = inverse * scaled - u * (inverse * inverse * inverse) * jnp.mean(
        u * scaled, axis=-1, keepdims=True
    )
    return inward, upstream * u * inverse


def rotate(u, cos, sin):
    return u * cos + pltpu.roll(u, HEAD // 2, 1) * sin


def unrotate(u, cos, sin):
    return u * cos - pltpu.roll(u, HEAD // 2, 1) * sin


def head_of(value, h):
    return value[:, h * HEAD : (h + 1) * HEAD]


def attention(x, gain, w_ref, cos, sin, allow, n_ref, qkv_ref, prob_ref, o_ref):
    n = (x * inverse_norm(x) * gain).astype(BF)
    n_ref[...] = n
    flat = dot(n, w_ref[:, 0:QKV])
    for h in range(HEADS + 1):
        qkv_ref[:, h * HEAD : (h + 1) * HEAD] = rotate(head_of(flat, h), cos, sin).astype(BF)
    qkv_ref[:, (HEADS + 1) * HEAD :] = flat[:, (HEADS + 1) * HEAD :].astype(BF)
    key = qkv_ref[:, HEADS * HEAD : (HEADS + 1) * HEAD]
    value = qkv_ref[:, (HEADS + 1) * HEAD :]
    for h in range(HEADS):
        scores = dot(qkv_ref[:, h * HEAD : (h + 1) * HEAD], key, 1, 1) * HEAD ** (-0.5)
        scores = jnp.where(allow > 0.0, scores, -1e30)
        weight = jnp.exp(scores - jnp.max(scores, axis=-1, keepdims=True))
        prob = weight / jnp.sum(weight, axis=-1, keepdims=True)
        prob_ref[h] = prob
        o_ref[:, h * HEAD : (h + 1) * HEAD] = dot(prob.astype(BF), value).astype(BF)
    return dot(o_ref[...], w_ref[:, QKV : QKV + OUT], 1, 1)


def expert_weight_copies(layer, r, local):
    core = lax.axis_index("blk")
    copies = []
    for name in ("gate", "up", "down"):
        held = getattr(r, "held_" + name)
        copies.append(local.start(getattr(r, name).at[layer, core], held.at[0]))
        copies.append(local.start(getattr(r, name + "_other").at[layer], held.at[1]))
    return copies


GROUP = SLOTS // 2


def expert_forward(group, rows, held, a_ref, b_ref):
    gate, up, down = held
    at = pl.ds(GROUP * group, GROUP)
    total = None
    for c in range(2):
        a = dot(rows, gate[c])
        b = dot(rows, up[c])
        a_ref[c, at] = a
        b_ref[c, at] = b
        z = (a / (1.0 + jnp.exp(-a)) * b).astype(BF)
        term = dot(z, down[c])
        total = term if total is None else total + term
    return total


def expert_backward(group, dy, held, a_ref, b_ref, z_ref, d_ref):
    gate, up, down = held
    at = pl.ds(GROUP * group, GROUP)
    total = None
    for c in range(2):
        a = a_ref[c, at]
        b = b_ref[c, at]
        sg = 1.0 / (1.0 + jnp.exp(-a))
        z_ref[at, c * HIDDEN : (c + 1) * HIDDEN] = (a * sg * b).astype(BF)
        dz = dot(dy, down[c], 1, 1)
        da = (dz * b * sg * (1.0 + a * (1.0 - sg))).astype(BF)
        db = (dz * a * sg).astype(BF)
        d_ref[at, 2 * c * HIDDEN : (2 * c + 1) * HIDDEN] = da
        d_ref[at, (2 * c + 1) * HIDDEN : (2 * c + 2) * HIDDEN] = db
        term = dot(da, gate[c], 1, 1) + dot(db, up[c], 1, 1)
        total = term if total is None else total + term
    return total


def expert_gradients(rows_ref, dy_ref, z_ref, d_ref, stage, grads, local):
    sent = []
    for q in range(4):
        if q >= 2:
            sent[q - 2].wait()
        columns = slice(q * HIDDEN, (q + 1) * HIDDEN)
        slot = q % 2
        both = dot(rows_ref[:, columns], d_ref[...], 0, 0)
        for c in range(2):
            for i in range(2):
                at = (2 * c + i) * HIDDEN
                stage[slot, 3 * c + i] = both[:, at : at + HIDDEN].astype(BF)
        low = dot(z_ref[...], dy_ref[:, columns], 0, 0)
        for c in range(2):
            stage[slot, 3 * c + 2] = low[c * HIDDEN : (c + 1) * HIDDEN].astype(BF)
        sent.append(local.start(stage.at[slot], grads.at[q]))
    return sent[2:]


def ring_devices(xyz, core, axis, steps=(1, 2, 3)):
    return [device_at(shifted(xyz, axis, by), core) for by in steps]


def arrive(copies):
    for copy in copies:
        copy.wait_recv()


class Gather:
    def __init__(self, sender, xyz, core):
        self.sender, self.xyz, self.core = sender, xyz, core

    def slab(self, job, stage, at, half=None):
        whole, lane, lanes, order = job
        index = list(at)
        for axis in order[:stage]:
            index[axis] = pl.ds(0, 4)
        if half is not None:
            index[order[0]] = pl.ds(2 * half, 2)
        return whole.at[index[0], index[1], index[2], :, pl.ds(lane, lanes)]

    def to(self, job, stage, by):
        return device_at(shifted(self.xyz, job[3][stage], by), self.core)

    def first(self, job, shard):
        source = shard.at[:, pl.ds(job[1], job[2])]
        target = self.slab(job, 0, self.xyz)
        return [self.sender.start(source, target, self.to(job, 0, by)) for by in (1, 3, 2)]

    def near(self, job, stage, steps=(1, 3)):
        block = self.slab(job, stage, self.xyz)
        return [self.sender.start(block, block, self.to(job, stage, by)) for by in steps]

    def relay(self, job, stage, near):
        copies = []
        for half, by in enumerate((1, 3)):
            near[half].wait_recv()
            at = shifted(self.xyz, job[3][stage], 4 - by)
            block = self.slab(job, stage, at, half)
            copies.append(self.sender.start(block, block, self.to(job, stage, by)))
        return copies

    def finish(self, near, relays):
        for copy in near:
            copy.wait_send()
        for copy in relays:
            copy.wait()


class ExpertSum:
    def __init__(self, r, layer, sender, local, xyz, core):
        self.r, self.sender, self.local, self.core = r, sender, local, core
        self.plus, self.minus = ring_devices(xyz, core, 0, (1, 3))
        self.grads, self.near, self.far, self.total = (
            getattr(r, f"{name}_{layer}") for name in ("grads", "near", "far", "total")
        )
        self.quarter = [shifted(xyz, 0, by)[0] for by in range(4)]

    def half(self, by, half):
        return self.grads.at[self.quarter[by], pl.ds(3 * half, 3)]

    def near_half(self, side, half):
        return self.near.at[side, pl.ds(3 * half, 3)]

    def start(self):
        go = self.sender.start
        self.passed = [
            go(self.half(2, 0), self.far.at[0], self.plus),
            go(self.half(2, 1), self.far.at[1], self.minus),
        ]
        self.plain = [
            go(self.half(1, 1), self.near_half(0, 1), self.plus),
            go(self.half(3, 0), self.near_half(1, 0), self.minus),
        ]

    def relay(self):
        r, load = self.r, self.local.start
        own = [load(self.half(by, side), r.own.at[side]) for side, by in enumerate((1, 3))]
        came = []
        for side in range(2):
            self.passed[side].wait_recv()
            came.append(load(self.far.at[side], r.work.at[side]))
        for side, target in enumerate((self.plus, self.minus)):
            own[side].wait()
            came[side].wait()
            for i in range(3):
                value = r.own[side, i].astype(F32) + r.work[side, i].astype(F32)
                r.work[side, i] = value.astype(BF)
            self.plain.append(
                self.sender.start(r.work.at[side], self.near_half(side, side), target)
            )

    def finish(self):
        r, load = self.r, self.local.start
        for copy in self.plain:
            copy.wait()
        for copy in self.passed:
            copy.wait_send()

        def bring(i, slot):
            return [
                load(self.grads.at[self.quarter[0], i], r.own.at[slot, 0]),
                load(self.near.at[0, i], r.own.at[slot, 1]),
                load(self.near.at[1, i], r.own.at[slot, 2]),
            ]

        order = (3, 4, 5, 0, 1, 2)
        loads = [bring(order[0], 0)]
        for k, i in enumerate(order):
            if k < 5:
                loads.append(bring(order[k + 1], (k + 1) % 2))
            for copy in loads[k]:
                copy.wait()
            slot = k % 2
            value = r.own[slot, 0].astype(F32) + r.own[slot, 1].astype(F32)
            r.ship[k] = (value + r.own[slot, 2].astype(F32)).astype(BF)
            if k == 2:
                across = self.sender.start(
                    r.ship.at[pl.ds(0, 3)], self.total.at[self.core], partner()
                )
        stay = load(r.ship.at[pl.ds(3, 3)], self.total.at[self.core])
        stay.wait()
        across.wait()


def tables(r):
    first = r.lengths[0, 0]
    second = first + r.lengths[0, 1]

    def place(index):
        segment = jnp.where(index >= first, 1, 0) + jnp.where(index >= second, 1, 0)
        start = jnp.where(segment == 0, 0, jnp.where(segment == 1, first, second))
        return segment, index - start

    shape = (TOKENS, TOKENS)
    lane = lax.broadcasted_iota(jnp.int32, shape, 1)
    row_segment, row_place = place(lax.broadcasted_iota(jnp.int32, shape, 0))
    key_segment, key_place = place(lane)
    allowed = (row_segment == key_segment) & (key_place <= row_place)
    r.allow[...] = jnp.where(allowed, 1.0, 0.0)
    half = jnp.where(lane < HEAD // 2, lane, lane - HEAD // 2).astype(F32)
    frequency = jnp.exp(half * (-2.0 / HEAD * math.log(rope_base)))
    angles = row_place.astype(F32) * frequency
    sign = jnp.where(lane < HEAD // 2, -1.0, 1.0)
    r.cos[...] = jnp.cos(angles)
    r.sin[...] = jnp.sin(angles) * sign


def assemble(r):
    square = (SHARD, SHARD)
    eye = lax.broadcasted_iota(jnp.int32, square, 0) == lax.broadcasted_iota(jnp.int32, square, 1)
    lane = lax.broadcasted_iota(jnp.int32, (SHARD, 128), 1)
    for l in range(LAYERS):
        r.shard[l, :, 0:768] = r.query[l]
        r.shard[l, :, 768:896] = r.key[l]
        r.shard[l, :, 896:QKV] = r.value[l]
        r.shard[l, :, QKV : QKV + OUT] = r.out[l]
        column = jnp.zeros((SHARD, 128), F32)
        for i, gain in enumerate((r.gain_a, r.gain_e)):
            spread = jnp.broadcast_to(gain[l : l + 1, :].astype(F32), square)
            spread = jnp.where(eye, spread, 0.0).astype(BF)
            column = column + dot(spread, jnp.where(lane == i, 1.0, 0.0).astype(BF))
        r.shard[l, :, QKV + OUT :] = column.astype(BF)


KEPT = dict(
    h=((TOKENS, WIDE), F32),
    n=((TOKENS, WIDE), BF),
    qkv=((TOKENS, QKV), BF),
    prob=((HEADS, TOKENS, TOKENS), F32),
    o=((TOKENS, OUT), BF),
    onehot=((SLOTS, TOKENS), BF),
    weighted=((SLOTS, TOKENS), F32),
)
KEPT_SPACE = {name: pltpu.VMEM(*spec) for name, spec in KEPT.items()}
HELD = dict(
    held_gate=pltpu.VMEM((2, WIDE, HIDDEN), BF),
    held_up=pltpu.VMEM((2, WIDE, HIDDEN), BF),
    held_down=pltpu.VMEM((2, HIDDEN, WIDE), BF),
)
ROWS = ((SLOTS, WIDE), BF)
INNER = ((2, SLOTS, HIDDEN), F32)
BLOCKS = ((PEERS, CAP, WIDE), BF)
PLANE = ((TOKENS, WIDE), F32)
GRADS = ((4, 6, HIDDEN, HIDDEN), BF)
BACKWARD = dict(
    z=pltpu.VMEM((SLOTS, 2 * HIDDEN), BF),
    d=pltpu.VMEM((SLOTS, 4 * HIDDEN), BF),
    dy=pltpu.VMEM(*ROWS),
    stage=pltpu.VMEM((2, 6, HIDDEN, HIDDEN), BF),
)


def sems(**counts):
    return {name: pltpu.SemaphoreType.DMA((n,)) for name, n in counts.items()}


def spaces(**specs):
    return {name: pltpu.VMEM(*spec) for name, spec in specs.items()}


def attend(r, l, x, pair, local, then=None):
    gain_a, gain_e = gain_rows(r.w)
    r.part0[...] = attention(
        x, gain_a, r.w, r.cos[...], r.sin[...], r.allow[...], r.n, r.qkv, r.prob, r.o
    )
    copy = pair.start(r.part0, r.theirs0, partner())
    for name in ("n", "qkv", "prob", "o"):
        local.keep(getattr(r, name), getattr(r, f"{name}_{l}"))
    begun = then() if then else None
    copy.wait_recv()
    h = x + (r.part0[...] + r.theirs0[...])
    copy.wait_send()
    r.h[...] = h
    local.keep(r.h, getattr(r, f"h_{l}"))
    return (h * inverse_norm(h) * gain_e).astype(BF), begun


def front_body(r):
    xyz, core = coords(), lax.axis_index("blk")
    local, pair = Local(r.local), Sender(r.pair_send, r.pair_recv)
    sender = Sender(r.wide_send, r.wide_recv)
    gather = Gather(sender, xyz, core)
    held = (r.held_gate, r.held_up, r.held_down)
    count = hail(peers() + ring_devices(xyz, core, 0))
    mine = pl.ds(pl.multiple_of(core * HALF, HALF), HALF)
    here = [
        local.start(r.tok, r.tokens.at[:, mine]),
        local.start(r.cot_half, r.cot.at[:, mine]),
    ]
    assemble(r)
    here.append(local.start(r.shard.at[0], r.cube.at[xyz[0], xyz[1], xyz[2]]))
    here_later = local.start(r.shard.at[1], r.later.at[xyz[0], xyz[1], xyz[2]])
    heard(count)
    now = [(r.cube, p * PART, PART, order) for p, order in enumerate(ORDERS)]
    first = [c for job in now for c in gather.first(job, r.shard.at[0])]
    halves_sent = [
        sender.start(r.tok, r.tokens.at[:, mine], partner()),
        sender.start(r.cot_half, r.cot.at[:, mine], partner()),
    ]
    swaps = [[], []]
    for l in range(LAYERS):
        for name in ("gate", "up", "down"):
            ref = getattr(r, name).at[l, 1 - core]
            swaps[l].append(sender.start(ref, getattr(r, name + "_other").at[l], partner()))
    tables(r)
    for l, (onehot, weighted) in enumerate(((r.onehot_0, r.weighted_0), (r.onehot_1, r.weighted_1))):
        hot, heavy = slot_matrices(r.ids[l], r.weights[l])
        onehot[...] = hot.astype(BF)
        weighted[...] = heavy
    for copy in here:
        copy.wait()
    arrive(first)
    near = [c for job in now for c in gather.near(job, 1, (1, 3, 2))]
    arrive(halves_sent)
    slot_weight = jnp.sum(r.weighted_1[...], axis=1, keepdims=True)
    store_rows(r.sent_g, dot(r.onehot_1[...], r.cot[...]) * slot_weight)
    arrive(near)
    last = [gather.near(job, 2) for job in now]
    relays = [gather.relay(job, 2, n) for job, n in zip(now, last)]
    arrive(swaps[0])
    loads = expert_weight_copies(0, r, local)
    for relay in relays:
        arrive(relay)
    jobs = [(r.later, *job) for job in LATER]
    first_later = [c for job in jobs for c in gather.first(job, r.shard.at[1])]
    r.w[...] = r.cube[...].astype(F32).reshape(WIDE, COLS).astype(BF)
    w_kept = local.start(r.w, r.w_0)

    def second():
        here_later.wait()
        arrive(first_later)
        return [c for job in jobs for c in gather.near(job, 1, (1, 3, 2))]

    m, near_later = attend(r, 0, r.tokens[...].astype(F32), pair, local, second)
    store_rows(r.sent, dot(r.onehot_0[...], m))
    out0 = Exchange(r, 0, r.sent, r.came, False)
    out0.start()
    arrive(near_later)
    last_later = [gather.near(job, 2) for job in jobs]
    relays_later = {}
    for copy in loads:
        copy.wait()
    back0 = Exchange(r, 1, r.turn, r.back, True)
    for g in range(2):
        out0.arrive(g)
        at = pl.ds(GROUP * g, GROUP)
        r.rows[at] = rows_of(group_of(r.came, g))
        store_rows(group_of(r.turn, g), expert_forward(g, r.rows[at], held, r.a, r.b))
        back0.start(g)
    rows_kept = [local.start(r.rows, r.rows_0), local.start(r.a, r.a_0), local.start(r.b, r.b_0)]
    out0.sent()
    arrive(swaps[1])
    loads = expert_weight_copies(1, r, local)
    for i in range(4):
        relays_later[i] = gather.relay(jobs[i], 2, last_later[i])
    back0.arrive()
    out_g = Exchange(r, 3, r.sent_g, r.came_g, False)
    out_g.start()
    r.part1[...] = combine(r.weighted_0[...], rows_of(r.back))
    copy = pair.start(r.part1, r.theirs1, partner())
    w_kept.wait()
    local.wait_kept()
    local.kept = []
    copy.wait_recv()
    x = r.h[...] + (r.part1[...] + r.theirs1[...])
    r.stream[...] = x
    copy.wait_send()
    for i in range(4):
        arrive(relays_later[i])
    for copy in near + [c for n, relay in zip(last, relays) for c in n + relay]:
        copy.wait_send()
    load = local.start(r.later, r.cube)
    load.wait()
    r.w[...] = r.cube[...].astype(F32).reshape(WIDE, COLS).astype(BF)
    local.keep(r.w, r.w_1)
    m, _ = attend(r, 1, x, pair, local)
    store_rows(r.sent, dot(r.onehot_1[...], m))
    out1 = Exchange(r, 2, r.sent, r.came, False)
    out1.start()
    back0.sent()
    out_g.arrive()
    r.dy[...] = rows_of(r.came_g)
    for copy in loads + rows_kept:
        copy.wait()
    for g in range(2):
        out1.arrive(g)
        at = pl.ds(GROUP * g, GROUP)
        r.rows[at] = rows_of(group_of(r.came, g))
        store_rows(group_of(r.back, g), expert_forward(g, r.rows[at], held, r.a, r.b))
        result = expert_backward(g, r.dy[at], held, r.a, r.b, r.z, r.d)
        store_rows(group_of(r.turn, g), result)
    local.keep(r.back, r.y_1)
    local.keep(r.turn, r.m_1)
    local.kept += expert_gradients(r.rows, r.dy, r.z, r.d, r.stage, r.grads_1, local)
    out1.sent()
    out_g.sent()
    for copy in first + first_later + near_later + halves_sent + swaps[0] + swaps[1]:
        copy.wait_send()
    for i in range(4):
        for copy in last_later[i] + relays_later[i]:
            copy.wait_send()
    local.wait_kept()


def turned(value):
    return value.astype(F32).T.reshape(4, 4, 4, SHARD, TOKENS).astype(BF)


def own_part(ref, axis, index):
    return ref.at[:, index] if axis == 1 else ref.at[:, :, index]


def share_factor(ref, into, axis, sender, xyz, core):
    copies = []
    for by in (1, 3, 2):
        there = shifted(xyz, axis, by)
        copies.append(
            sender.start(own_part(ref, axis, there[axis]), into.at[by - 1], device_at(there, core))
        )
    return copies


def share_whole(ref, axis, sender, xyz, core):
    return [
        sender.start(
            ref.at[pl.ds(0, TOKENS)],
            ref.at[pl.ds(by * TOKENS, TOKENS)],
            device_at(shifted(xyz, axis, by), core),
        )
        for by in (1, 3, 2)
    ]


def quarter_sum(own, came, axis, xyz, right):
    first = own_part(own, axis, xyz[axis])[...]
    pieces = [first] + [came[i] for i in range(3)]
    left = [p.astype(F32).reshape(HIDDEN, TOKENS).astype(BF) for p in pieces]
    return dot(jnp.concatenate(left, axis=1), right[...])


def back_body(r):
    xyz, core = coords(), lax.axis_index("blk")
    local, pair = Local(r.local), Sender(r.pair_send, r.pair_recv)
    sender = Sender(r.wide_send, r.wide_recv)

    def load_layer(l):
        names = ("w", "h", "qkv", "prob", "o")
        return [local.start(getattr(r, f"{name}_{l}"), getattr(r, name)) for name in names]

    loads = load_layer(1)
    count = hail(peers() + ring_devices(xyz, core, 0))
    sums = [ExpertSum(r, l, sender, local, xyz, core) for l in range(LAYERS)]
    heard(count)
    came_m, onehot = (r.came_0, r.came_1), (r.onehot_0, r.onehot_1)
    back = [Exchange(r, 2, r.turn, r.came_0, True), Exchange(r, 0, r.m_1, r.came_1, True)]
    out_g = Exchange(r, 1, r.sent, r.came_g, False)
    y_back = Exchange(r, 3, r.y_1, r.came_1, True)
    back[1].start()
    sums[1].start()
    weights = expert_weight_copies(0, r, local)
    weights += [local.start(getattr(r, name + "_0"), getattr(r, name)) for name in ("rows", "a", "b")]
    r.n_turned[1] = turned(r.n_1[...])
    r.n_turned[0] = turned(r.n_0[...])
    for copy in loads:
        copy.wait()
    shared = [[], []]
    scale = HEAD ** (-0.5)
    row = lax.broadcasted_iota(jnp.int32, (8, WIDE), 0)
    r.gain_sum[1] = jnp.zeros((8, WIDE), F32)
    inner, across = [None] * 2, [None] * 2
    for l in (1, 0):
        x = (r.stream if l == 1 else r.tokens)[...].astype(F32)
        gain_a, gain_e = gain_rows(r.w)
        r.o_all[l, 0:TOKENS] = r.o[...]
        back[l].arrive()
        r.part[0] = dot(onehot[l][...], rows_of(came_m[l]), 0, 0)
        inner[l] = pair.start(r.part.at[0], r.theirs.at[l, 0], partner())
        if l == 1:
            for i in (1, 0):
                shared[i] += share_factor(r.n_turned.at[i], r.n_came.at[i], 1, sender, xyz, core)
        else:
            shared[1] += share_whole(r.lin_all.at[1], 1, sender, xyz, core)
        shared[l] += share_whole(r.o_all.at[l], 2, sender, xyz, core)
        inner[l].wait_recv()
        dm = r.part[0] + r.theirs[l, 0]
        hidden = r.h[...]
        inward, gain_grad_e = norm_back(hidden, inverse_norm(hidden), gain_e, dm)
        gh = (r.cot[...].astype(F32) if l == 1 else r.flow[...]) + inward
        r.flow[...] = gh
        da = gh.astype(BF)
        r.da_turned[l] = turned(gh)
        shared[l] += share_factor(r.da_turned.at[l], r.da_came.at[l], 2, sender, xyz, core)
        do = dot(da, r.w[:, QKV : QKV + OUT]).astype(BF)
        key = r.qkv[:, HEADS * HEAD : (HEADS + 1) * HEAD]
        value = r.qkv[:, (HEADS + 1) * HEAD :]
        key_grad, value_grad = None, None
        cosine, sine = r.cos[...], r.sin[...]
        lin = r.lin_all.at[l]
        for i in range(HEADS):
            prob_i = r.prob[i]
            do_i = head_of(do, i)
            q_i = r.qkv[:, i * HEAD : (i + 1) * HEAD]
            dprob = dot(do_i, value, 1, 1)
            centre = jnp.sum(prob_i * dprob, axis=-1, keepdims=True)
            ds = (prob_i * (dprob - centre)).astype(BF)
            dq = dot(ds, key) * scale
            lin[0:TOKENS, i * HEAD : (i + 1) * HEAD] = unrotate(dq, cosine, sine).astype(BF)
            dk = dot(ds, q_i, 0, 0)
            dv = dot(prob_i.astype(BF), do_i, 0, 0)
            key_grad = dk if key_grad is None else key_grad + dk
            value_grad = dv if value_grad is None else value_grad + dv
        lin[0:TOKENS, HEADS * HEAD : (HEADS + 1) * HEAD] = unrotate(
            key_grad * scale, cosine, sine
        ).astype(BF)
        lin[0:TOKENS, (HEADS + 1) * HEAD :] = value_grad.astype(BF)
        r.part[1] = dot(lin[0:TOKENS, :], r.w[:, 0:QKV], 1, 1)
        across[l] = pair.start(r.part.at[1], r.theirs.at[l, 1], partner())
        if l == 1:
            r.kept_half[...] = jnp.where(core == 1, r.h[:, HALF:], r.h[:, :HALF])
            loads = load_layer(0)
        else:
            shared[0] += share_whole(r.lin_all.at[0], 1, sender, xyz, core)
            sums[0].relay()
        across[l].wait_recv()
        dn = r.part[1] + r.theirs[l, 1]
        inward, gain_grad_a = norm_back(x, inverse_norm(x), gain_a, dn)
        flow = r.flow[...] + inward
        gains = r.gain_sum[1]
        for i, grad in enumerate((gain_grad_a, gain_grad_e)):
            grad = jnp.sum(grad, axis=0, keepdims=True)
            gains = jnp.where(row == 2 * l + i, jnp.broadcast_to(grad, (8, WIDE)), gains)
        r.gain_sum[1] = gains
        inner[l].wait_send()
        across[l].wait_send()
        if l == 0:
            r.tokens_grad[...] = jnp.where(core == 1, flow[:, HALF:], flow[:, :HALF])
            continue
        r.flow[...] = flow
        slot_weight = jnp.sum(r.weighted_0[...], axis=1, keepdims=True)
        high, low = halves(flow)
        hot = r.onehot_0[...]
        store_rows(r.sent, (dot(hot, high) + dot(hot, low)) * slot_weight)
        out_g.start()
        sums[1].relay()
        for copy in weights:
            copy.wait()
        held = (r.held_gate, r.held_up, r.held_down)
        for g in range(2):
            out_g.arrive(g)
            at = pl.ds(GROUP * g, GROUP)
            r.dy[at] = rows_of(group_of(r.came_g, g))
            result = expert_backward(g, r.dy[at], held, r.a, r.b, r.z, r.d)
            store_rows(group_of(r.turn, g), result)
            back[0].start(g)
        for copy in expert_gradients(r.rows, r.dy, r.z, r.d, r.stage, r.grads_0, local):
            copy.wait()
        sums[0].start()
        sums[1].finish()
        for copy in loads:
            copy.wait()
    finish_sums(r, shared, y_back, sender, xyz, core)
    y_back.arrive()
    mixed = combine(r.weighted_1[...], rows_of(r.came_1))
    r.half[...] = jnp.where(core == 1, mixed[:, :HALF], mixed[:, HALF:])
    third = pair.start(r.half, r.half_theirs, partner())
    own = jnp.where(core == 1, mixed[:, HALF:], mixed[:, :HALF])
    third.wait()
    r.block_out[...] = (r.kept_half[...] + (own + r.half_theirs[...])).astype(BF)
    sums[0].finish()
    for exchange in (*back, out_g, y_back):
        exchange.sent()


def late_start(r, l, sender, xyz, core):
    copies = []
    for ref, came, axis in ((r.sum_a, r.near_a, 2), (r.sum_b, r.near_b, 1)):
        for by in (1, 3, 2):
            there = shifted(xyz, axis, by)
            copies.append(
                sender.start(ref.at[l, :, there[axis]], came.at[l, by - 1], device_at(there, core))
            )
    return copies


def late_middle(r, l, sender, xyz, core, copies):
    arrive(copies)
    for ref, came, axis, lanes in (
        (r.sum_a, r.near_a, 2, slice(0, QKV)),
        (r.sum_b, r.near_b, 1, slice(QKV, QKV + OUT)),
    ):
        total = ref[l, :, xyz[axis]].astype(F32)
        for i in range(3):
            total = total + came[l, i].astype(F32)
        r.line[l, :, :, lanes] = total.astype(BF)
    copies = []
    for by in (1, 3, 2):
        there = shifted(xyz, 0, by)
        copies.append(
            sender.start(r.line.at[l, there[0]], r.line_came.at[l, by - 1], device_at(there, core))
        )
    return copies


def late_end(r, l, xyz, copies):
    for copy in copies:
        copy.wait()
    total = r.line[l, xyz[0]].astype(F32)
    for i in range(3):
        total = total + r.line_came[l, i].astype(F32)
    r.weight_grad[l] = total


def gains_along(r, axis, sender, xyz, core):
    return [
        sender.start(r.gain_sum.at[axis], r.gain_came.at[axis, by - 1], device_at(shifted(xyz, axis, by), core))
        for by in (1, 3, 2)
    ]


def gains_next(r, axis, copies):
    for copy in copies:
        copy.wait()
    total = r.gain_sum[axis]
    for i in range(3):
        total = total + r.gain_came[axis, i]
    return total


def finish_sums(r, shared, y_back, sender, xyz, core):
    def quarter(l):
        arrive(shared[l])
        wide = (4, 4, SHARD, QKV)
        total = quarter_sum(r.n_turned.at[l], r.n_came.at[l], 1, xyz, r.lin_all.at[l])
        r.sum_a[l] = total.reshape(wide).astype(BF)
        wide = (4, 4, SHARD, OUT)
        total = quarter_sum(r.da_turned.at[l], r.da_came.at[l], 2, xyz, r.o_all.at[l])
        r.sum_b[l] = total.reshape(wide).astype(BF)
        return late_start(r, l, sender, xyz, core)

    along = gains_along(r, 1, sender, xyz, core)
    above = quarter(1)
    y_back.start()
    r.gain_sum[2] = gains_next(r, 1, along)
    along = gains_along(r, 2, sender, xyz, core)
    above_last = late_middle(r, 1, sender, xyz, core, above)
    r.gain_sum[0] = gains_next(r, 2, along)
    along = gains_along(r, 0, sender, xyz, core)
    lower = quarter(0)
    late_end(r, 1, xyz, above_last)
    r.gain_total[...] = gains_next(r, 0, along)
    lower_last = late_middle(r, 0, sender, xyz, core, lower)
    late_end(r, 0, xyz, lower_last)
    for copy in shared[0] + shared[1] + above + lower:
        copy.wait_send()


def finish_body(r):
    local = Local(r.local)
    loads = [
        [local.start(total.at[:, i], r.narrow.at[l, i]) for i in range(3)]
        for l, total in enumerate((r.total_below, r.total_above))
    ]
    r.block_out[...] = r.block_in[...]
    r.tokens_grad[...] = r.tokens_in[...]
    place = (lax.axis_index("dp") * PEERS + lax.axis_index("expert")) * SHARD
    near = pltpu.roll(r.gain_total[...], lax.rem(WIDE - place, WIDE), 1)
    for l in range(LAYERS):
        r.gain_a[l : l + 1, :] = near[2 * l : 2 * l + 1, :SHARD]
        r.gain_e[l : l + 1, :] = near[2 * l + 1 : 2 * l + 2, :SHARD]
        r.query[l] = r.weight_grad[l, :, :768]
        r.key[l] = r.weight_grad[l, :, 768:896]
        r.value[l] = r.weight_grad[l, :, 896:QKV]
        r.out[l] = r.weight_grad[l, :, QKV:]
    for l in range(LAYERS):
        for i, out in enumerate((r.gate, r.up, r.down)):
            loads[l][i].wait()
            r.broad[l, i] = r.narrow[l, i].astype(F32)
            local.keep(r.broad.at[l, i], out.at[l])
    local.wait_kept()


def kernel_call(body, name, cid, ins, outs, scratch, aliases=()):
    names = [*ins, *outs, *scratch]
    assert len(set(names)) == len(names)

    def kernel(*refs):
        body(types.SimpleNamespace(**dict(zip(names, refs))))

    results = pl.pallas_call(
        kernel,
        out_shape=[jax.ShapeDtypeStruct(shape, kind) for shape, kind, _ in outs.values()],
        in_specs=[space for _, space in ins.values()],
        out_specs=[space for _, _, space in outs.values()],
        scratch_shapes=list(scratch.values()),
        input_output_aliases={list(ins).index(a): list(outs).index(b) for a, b in aliases},
        compiler_params=pltpu.CompilerParams(
            collective_id=cid, has_side_effects=cid is not None, vmem_limit_bytes=LIMIT
        ),
        name=name,
    )(*[array for array, _ in ins.values()])
    return types.SimpleNamespace(**dict(zip(outs, results)))


def per_device(
    tokens_in,
    seq_lengths,
    expert_ids,
    gate_weights,
    attention_gain,
    query_weight,
    key_weight,
    value_weight,
    out_weight,
    expert_gain,
    gate_weight,
    up_weight,
    down_weight,
    cotangent,
):
    cube = (4, 4, 4, SHARD, COLS)
    own = dict(gate=(gate_weight, ANY), up=(up_weight, ANY), down=(down_weight, ANY))
    exchanges = sems(
        **{f"{way}{i}": PEERS for way in ("send", "recv") for i in range(4)}, pair_send=5, pair_recv=5
    )
    kept = ("h", "n", "qkv", "prob", "o")
    w_space = dict(w=pltpu.VMEM((WIDE, COLS), BF))
    start = kernel_call(
        front_body,
        "front",
        1,
        dict(
            lengths=(seq_lengths, SMEM),
            query=(query_weight, VMEM),
            key=(key_weight, VMEM),
            value=(value_weight, VMEM),
            out=(jnp.swapaxes(out_weight, 1, 2), VMEM),
            gain_a=(attention_gain, VMEM),
            gain_e=(expert_gain, VMEM),
            tok=(tokens_in, VMEM),
            cot_half=(cotangent, VMEM),
            ids=(jnp.swapaxes(expert_ids, 1, 2), VMEM),
            weights=(jnp.swapaxes(gate_weights, 1, 2), VMEM),
            **own,
        ),
        dict(
            w_0=((WIDE, COLS), BF, ANY),
            w_1=((WIDE, COLS), BF, ANY),
            later=(cube, BF, ANY),
            tokens=((TOKENS, WIDE), BF, VMEM),
            cot=((TOKENS, WIDE), BF, VMEM),
            stream=(*PLANE, VMEM),
            cos=((TOKENS, HEAD), F32, VMEM),
            sin=((TOKENS, HEAD), F32, VMEM),
            gate_other=((LAYERS, WIDE, HIDDEN), BF, ANY),
            up_other=((LAYERS, WIDE, HIDDEN), BF, ANY),
            down_other=((LAYERS, HIDDEN, WIDE), BF, ANY),
            rows_0=(*ROWS, ANY),
            a_0=(*INNER, ANY),
            b_0=(*INNER, ANY),
            y_1=(*BLOCKS, ANY),
            m_1=(*BLOCKS, ANY),
            grads_1=(*GRADS, ANY),
            **{f"{name}_{l}": (*KEPT[name], ANY) for l in range(LAYERS) for name in kept},
            **{
                f"{name}_{l}": (*KEPT[name], VMEM)
                for l in range(LAYERS)
                for name in ("onehot", "weighted")
            },
        ),
        dict(
            shard=pltpu.VMEM((LAYERS, SHARD, COLS), BF),
            cube=pltpu.VMEM(cube, BF),
            allow=pltpu.VMEM((TOKENS, TOKENS), F32),
            **w_space,
            **{name: KEPT_SPACE[name] for name in kept},
            **HELD,
            **BACKWARD,
            **spaces(sent=BLOCKS, came=BLOCKS, back=BLOCKS, sent_g=BLOCKS, came_g=BLOCKS),
            **spaces(turn=BLOCKS, rows=ROWS, a=INNER, b=INNER),
            **spaces(part0=PLANE, theirs0=PLANE, part1=PLANE, theirs1=PLANE),
            **exchanges,
            **sems(wide_send=78, wide_recv=78, local=50),
        ),
    )
    experts = dict(
        own,
        gate_other=(start.gate_other, ANY),
        up_other=(start.up_other, ANY),
        down_other=(start.down_other, ANY),
    )
    part_a, part_b = (4, 4, SHARD, QKV), (4, 4, SHARD, OUT)
    total = ((2, 3, HIDDEN, HIDDEN), BF, ANY)
    near, far = ((2, 6, HIDDEN, HIDDEN), BF, ANY), ((2, 3, HIDDEN, HIDDEN), BF, ANY)
    factor, quarter = (4, 4, 4, SHARD, TOKENS), (3, 4, 4, SHARD, TOKENS)
    by_layer = {}
    for l in range(LAYERS):
        for name in ("h", "qkv", "prob", "o", "w"):
            by_layer[f"{name}_{l}"] = (getattr(start, f"{name}_{l}"), ANY)
        for name in ("n", "onehot", "weighted"):
            by_layer[f"{name}_{l}"] = (getattr(start, f"{name}_{l}"), VMEM)
    end = kernel_call(
        back_body,
        "backward",
        4,
        dict(
            stream=(start.stream, VMEM),
            tokens=(start.tokens, VMEM),
            cot=(start.cot, VMEM),
            cos=(start.cos, VMEM),
            sin=(start.sin, VMEM),
            **by_layer,
            **{
                name: (getattr(start, name), ANY)
                for name in ("m_1", "y_1", "grads_1", "rows_0", "a_0", "b_0")
            },
            **experts,
        ),
        dict(
            block_out=((TOKENS, HALF), BF, VMEM),
            tokens_grad=((TOKENS, HALF), F32, VMEM),
            weight_grad=((LAYERS, SHARD, QKV + OUT), F32, VMEM),
            gain_total=((8, WIDE), F32, VMEM),
            total_0=total,
            total_1=total,
            grads_0=(*GRADS, ANY),
            near_0=near,
            near_1=near,
            far_0=far,
            far_1=far,
        ),
        dict(
            **w_space,
            **HELD,
            **BACKWARD,
            **{name: KEPT_SPACE[name] for name in ("h", "qkv", "prob", "o")},
            **spaces(rows=ROWS, a=INNER, b=INNER, flow=PLANE),
            **spaces(sent=BLOCKS, turn=BLOCKS),
            **spaces(came_0=BLOCKS, came_1=BLOCKS, came_g=BLOCKS),
            part=pltpu.VMEM((2, TOKENS, WIDE), F32),
            theirs=pltpu.VMEM((LAYERS, 2, TOKENS, WIDE), F32),
            half=pltpu.VMEM((TOKENS, HALF), F32),
            half_theirs=pltpu.VMEM((TOKENS, HALF), F32),
            kept_half=pltpu.VMEM((TOKENS, HALF), F32),
            own=pltpu.VMEM((2, 3, HIDDEN, HIDDEN), BF),
            work=pltpu.VMEM((2, 3, HIDDEN, HIDDEN), BF),
            ship=pltpu.VMEM((6, HIDDEN, HIDDEN), BF),
            n_turned=pltpu.VMEM((LAYERS, *factor), BF),
            da_turned=pltpu.VMEM((LAYERS, *factor), BF),
            n_came=pltpu.VMEM((LAYERS, *quarter), BF),
            da_came=pltpu.VMEM((LAYERS, *quarter), BF),
            lin_all=pltpu.VMEM((LAYERS, 4 * TOKENS, QKV), BF),
            o_all=pltpu.VMEM((LAYERS, 4 * TOKENS, OUT), BF),
            sum_a=pltpu.VMEM((LAYERS, *part_a), BF),
            sum_b=pltpu.VMEM((LAYERS, *part_b), BF),
            near_a=pltpu.VMEM((LAYERS, 3, 4, SHARD, QKV), BF),
            near_b=pltpu.VMEM((LAYERS, 3, 4, SHARD, OUT), BF),
            line=pltpu.VMEM((LAYERS, 4, SHARD, QKV + OUT), BF),
            line_came=pltpu.VMEM((LAYERS, 3, SHARD, QKV + OUT), BF),
            gain_sum=pltpu.VMEM((3, 8, WIDE), F32),
            gain_came=pltpu.VMEM((3, 3, 8, WIDE), F32),
            **exchanges,
            **sems(wide_send=68, wide_recv=68, local=80),
        ),
    )
    expert_out = ((LAYERS, 2, HIDDEN, HIDDEN), F32, ANY)
    out = kernel_call(
        finish_body,
        "finish",
        None,
        dict(
            block_in=(end.block_out, VMEM),
            tokens_in=(end.tokens_grad, VMEM),
            total_above=(end.total_1, ANY),
            total_below=(end.total_0, ANY),
            weight_grad=(end.weight_grad, VMEM),
            gain_total=(end.gain_total, VMEM),
        ),
        dict(
            block_out=((TOKENS, HALF), BF, VMEM),
            tokens_grad=((TOKENS, HALF), F32, VMEM),
            gain_a=((LAYERS, SHARD), F32, VMEM),
            query=((LAYERS, SHARD, 768), F32, VMEM),
            key=((LAYERS, SHARD, 128), F32, VMEM),
            value=((LAYERS, SHARD, 128), F32, VMEM),
            out=((LAYERS, SHARD, OUT), F32, VMEM),
            gain_e=((LAYERS, SHARD), F32, VMEM),
            gate=expert_out,
            up=expert_out,
            down=expert_out,
        ),
        dict(
            narrow=pltpu.VMEM((LAYERS, 3, 2, HIDDEN, HIDDEN), BF),
            broad=pltpu.VMEM((LAYERS, 3, 2, HIDDEN, HIDDEN), F32),
            **sems(local=14),
        ),
    )
    return (
        out.block_out,
        out.tokens_grad,
        out.gain_a,
        out.query,
        out.key,
        out.value,
        jnp.swapaxes(out.out, 1, 2),
        out.gain_e,
        out.gate,
        out.up,
        out.down,
    )


def solution(mesh):
    placed = (
        P(("dp", "expert"), "blk"),
        P(("dp", "expert"), None),
        P(None, ("dp", "expert"), None),
        P(None, ("dp", "expert"), None),
        P(None, ("dp", "expert")),
        P(None, ("dp", "expert"), "blk"),
        P(None, ("dp", "expert"), "blk"),
        P(None, ("dp", "expert"), "blk"),
        P(None, "blk", ("dp", "expert")),
        P(None, ("dp", "expert")),
        P(None, "expert", None, "blk"),
        P(None, "expert", None, "blk"),
        P(None, "expert", "blk", None),
        P(("dp", "expert"), "blk"),
    )
    return jax.shard_map(
        per_device,
        mesh=mesh,
        in_specs=placed,
        out_specs=(
            P(("dp", "expert"), "blk"),
            P(("dp", "expert"), "blk"),
            P(None, ("dp", "expert")),
            P(None, ("dp", "expert"), "blk"),
            P(None, ("dp", "expert"), "blk"),
            P(None, ("dp", "expert"), "blk"),
            P(None, "blk", ("dp", "expert")),
            P(None, ("dp", "expert")),
            P(None, "expert", "dp", "blk"),
            P(None, "expert", "dp", "blk"),
            P(None, "expert", "blk", "dp"),
        ),
        check_vma=False,
    )
```

```python
import functools
import math
import types

import jax
import jax.numpy as jnp
from jax import lax
from jax.experimental import pallas as pl
from jax.experimental.pallas import tpu as pltpu
from jax.sharding import PartitionSpec as P

HEAD = 128
TOP = 4
LAYERS = 2
F32 = jnp.float32
BF = jnp.bfloat16
MESH = pl.DeviceIdType.MESH

epsilon = 1e-06
rope_base = 1000000.0

TOKENS = 128
WIDE = 1536
HALF = WIDE // 2
HEADS = 6
HIDDEN = 384
PEERS = 16
CAP = 24
SLOTS = PEERS * CAP
SHARD = 24
QKV = 1024
OUT = 768
COLS = QKV + OUT + 128
PART = COLS // 3
ORDERS = ((0, 1, 2), (1, 2, 0), (2, 0, 1))
LIMIT = 60 << 20
LATER = ((0, 768, (1, 2, 0)), (768, 768, (2, 1, 0)), (1536, 128, (0, 2, 1)), (1664, 256, (0, 1, 2)))

ANY = pl.BlockSpec(memory_space=pl.ANY)
VMEM = pl.BlockSpec(memory_space=pltpu.VMEM)
SMEM = pl.BlockSpec(memory_space=pltpu.SMEM)


def dot(a, b, ca=1, cb=0):
    return lax.dot_general(a, b, (((ca,), (cb,)), ((), ())), preferred_element_type=F32)


def coords():
    ex = lax.axis_index("expert")
    return [lax.axis_index("dp"), lax.div(ex, 4), lax.rem(ex, 4)]


def shifted(xyz, axis, by):
    moved = list(xyz)
    moved[axis] = lax.rem(xyz[axis] + by, 4)
    return moved


def device_at(xyz, core):
    return (xyz[0], xyz[1] * 4 + xyz[2], core)


def partner():
    return (lax.axis_index("dp"), lax.axis_index("expert"), 1 - lax.axis_index("blk"))


def hail(devices):
    barrier = pltpu.get_barrier_semaphore()
    for device in devices:
        pl.semaphore_signal(barrier, inc=1, device_id=device, device_id_type=MESH)
    return len(devices)


def heard(count):
    pl.semaphore_wait(pltpu.get_barrier_semaphore(), count)


def peer(step):
    dp, ex, core = (lax.axis_index(a) for a in ("dp", "expert", "blk"))
    return (dp, lax.rem(ex + step, PEERS), core)


def peers():
    return [peer(d) for d in range(1, PEERS)] + [partner()]


class Local:
    def __init__(self, sem):
        self.sem, self.at, self.kept = sem, 0, []

    def start(self, src, dst):
        assert self.at < self.sem.shape[0]
        copy = pltpu.make_async_copy(src, dst, self.sem.at[self.at])
        self.at += 1
        copy.start()
        return copy

    def keep(self, src, dst):
        self.kept.append(self.start(src, dst))

    def wait_kept(self):
        for copy in self.kept:
            copy.wait()


class Sender:
    def __init__(self, send, recv):
        self.send, self.recv, self.at = send, recv, 0

    def start(self, src, dst, device):
        assert self.at < self.send.shape[0]
        copy = pltpu.make_async_remote_copy(
            src_ref=src,
            dst_ref=dst,
            send_sem=self.send.at[self.at],
            recv_sem=self.recv.at[self.at],
            device_id=device,
            device_id_type=MESH,
        )
        self.at += 1
        copy.start()
        return copy


def step_of(k):
    row = lax.div(lax.rem(k, 8), 2)
    return 4 * row + 2 * lax.rem(k, 2) + lax.rem(row + lax.div(k, 8), 2)


class Exchange:
    def __init__(self, r, number, src, dst, back):
        self.send, self.recv = getattr(r, f"send{number}"), getattr(r, f"recv{number}")
        self.src, self.dst, self.back = src, dst, back
        self.me = lax.axis_index("expert")

    def copy(self, k):
        step = step_of(k)
        target = peer(PEERS - step if self.back else step)
        return pltpu.make_async_remote_copy(
            src_ref=self.src.at[k if self.back else target[1]],
            dst_ref=self.dst.at[self.me if self.back else k],
            send_sem=self.send.at[k],
            recv_sem=self.recv.at[k],
            device_id=target,
            device_id_type=MESH,
        )

    def own(self):
        src = self.src.at[0 if self.back else self.me]
        dst = self.dst.at[self.me if self.back else 0]
        return pltpu.make_async_copy(src, dst, self.send.at[0])

    def each(self, group, act):
        first, last = ((1, PEERS), (1, 8), (8, PEERS))[group + 1]

        def body(k, carry):
            act(self.copy(k))
            return carry

        lax.fori_loop(first, last, body, 0)

    def start(self, group=-1):
        if group <= 0:
            self.own().start()
        self.each(group, lambda copy: copy.start())

    def arrive(self, group=-1):
        if group <= 0:
            self.own().wait()
        self.each(group, lambda copy: copy.wait_recv())

    def sent(self):
        self.each(-1, lambda copy: copy.wait_send())


def rows_of(ref):
    value = ref[...]
    return value.astype(F32).reshape(value.shape[0] * CAP, WIDE).astype(BF)


def store_rows(ref, rows):
    ref[...] = rows.reshape(rows.shape[0] // CAP, CAP, WIDE).astype(BF)


def group_of(ref, group):
    return ref.at[pl.ds(8 * group, 8)]


def slot_matrices(ids, weights):
    core = lax.axis_index("blk")
    expert = 2 * lax.broadcasted_iota(jnp.int32, (PEERS, TOKENS), 0) + core
    chosen = jnp.zeros((PEERS, TOKENS), F32)
    gate = jnp.zeros((PEERS, TOKENS), F32)
    for j in range(TOP):
        hit = jnp.where(ids[j : j + 1, :] == expert, 1.0, 0.0)
        chosen = chosen + hit
        gate = gate + hit * weights[j : j + 1, :]
    before = lax.broadcasted_iota(jnp.int32, (TOKENS, TOKENS), 0) < lax.broadcasted_iota(
        jnp.int32, (TOKENS, TOKENS), 1
    )
    rank = dot(chosen.astype(BF), jnp.where(before, 1.0, 0.0).astype(BF))
    rank = jnp.where(chosen > 0.0, rank, -1.0)
    shape = (PEERS, CAP, TOKENS)
    place = lax.broadcasted_iota(jnp.int32, shape, 1).astype(F32)
    onehot = jnp.where(jnp.broadcast_to(rank[:, None, :], shape) == place, 1.0, 0.0)
    weighted = onehot * jnp.broadcast_to(gate[:, None, :], shape)
    return onehot.reshape(SLOTS, TOKENS), weighted.reshape(SLOTS, TOKENS)


def halves(value):
    high = value.astype(BF)
    return high, (value - high.astype(F32)).astype(BF)


def combine(weighted, rows):
    high, low = halves(weighted)
    return dot(high, rows, 0, 0) + dot(low, rows, 0, 0)


def gain_rows(w_ref):
    unit = jnp.where(
        lax.broadcasted_iota(jnp.int32, (8, 128), 0) == lax.broadcasted_iota(jnp.int32, (8, 128), 1),
        1.0,
        0.0,
    ).astype(BF)
    rows = dot(unit, w_ref[:, QKV + OUT : COLS], 1, 1)
    return rows[0:1, :], rows[1:2, :]


def inverse_norm(u):
    return lax.rsqrt(jnp.mean(u * u, axis=-1, keepdims=True) + epsilon)


def norm_back(u, inverse, gain, upstream):
    scaled = upstream * gain
    inward = inverse * scaled - u * (inverse * inverse * inverse) * jnp.mean(
        u * scaled, axis=-1, keepdims=True
    )
    return inward, upstream * u * inverse


def rotate(u, cos, sin):
    return u * cos + pltpu.roll(u, HEAD // 2, 1) * sin


def unrotate(u, cos, sin):
    return u * cos - pltpu.roll(u, HEAD // 2, 1) * sin


def head_of(value, h):
    return value[:, h * HEAD : (h + 1) * HEAD]


def attention(x, gain, w_ref, cos, sin, allow, n_ref, qkv_ref, prob_ref, o_ref):
    n = (x * inverse_norm(x) * gain).astype(BF)
    n_ref[...] = n
    flat = dot(n, w_ref[:, 0:QKV])
    for h in range(HEADS + 1):
        qkv_ref[:, h * HEAD : (h + 1) * HEAD] = rotate(head_of(flat, h), cos, sin).astype(BF)
    qkv_ref[:, (HEADS + 1) * HEAD :] = flat[:, (HEADS + 1) * HEAD :].astype(BF)
    key = qkv_ref[:, HEADS * HEAD : (HEADS + 1) * HEAD]
    value = qkv_ref[:, (HEADS + 1) * HEAD :]
    for h in range(HEADS):
        scores = dot(qkv_ref[:, h * HEAD : (h + 1) * HEAD], key, 1, 1) * HEAD ** (-0.5)
        scores = jnp.where(allow > 0.0, scores, -1e30)
        weight = jnp.exp(scores - jnp.max(scores, axis=-1, keepdims=True))
        prob = weight / jnp.sum(weight, axis=-1, keepdims=True)
        prob_ref[h] = prob
        o_ref[:, h * HEAD : (h + 1) * HEAD] = dot(prob.astype(BF), value).astype(BF)
    return dot(o_ref[...], w_ref[:, QKV : QKV + OUT], 1, 1)


def expert_weight_copies(layer, r, local):
    core = lax.axis_index("blk")
    copies = []
    for name in ("gate", "up", "down"):
        held = getattr(r, "held_" + name)
        copies.append(local.start(getattr(r, name).at[layer, core], held.at[0]))
        copies.append(local.start(getattr(r, name + "_other").at[layer], held.at[1]))
    return copies


GROUP = SLOTS // 2


def expert_forward(group, rows, held, a_ref, b_ref):
    gate, up, down = held
    at = pl.ds(GROUP * group, GROUP)
    total = None
    for c in range(2):
        a = dot(rows, gate[c])
        b = dot(rows, up[c])
        a_ref[c, at] = a
        b_ref[c, at] = b
        z = (a / (1.0 + jnp.exp(-a)) * b).astype(BF)
        term = dot(z, down[c])
        total = term if total is None else total + term
    return total


def expert_backward(group, dy, held, a_ref, b_ref, z_ref, d_ref):
    gate, up, down = held
    at = pl.ds(GROUP * group, GROUP)
    total = None
    for c in range(2):
        a = a_ref[c, at]
        b = b_ref[c, at]
        sg = 1.0 / (1.0 + jnp.exp(-a))
        z_ref[at, c * HIDDEN : (c + 1) * HIDDEN] = (a * sg * b).astype(BF)
        dz = dot(dy, down[c], 1, 1)
        da = (dz * b * sg * (1.0 + a * (1.0 - sg))).astype(BF)
        db = (dz * a * sg).astype(BF)
        d_ref[at, 2 * c * HIDDEN : (2 * c + 1) * HIDDEN] = da
        d_ref[at, (2 * c + 1) * HIDDEN : (2 * c + 2) * HIDDEN] = db
        term = dot(da, gate[c], 1, 1) + dot(db, up[c], 1, 1)
        total = term if total is None else total + term
    return total


def expert_gradients(rows_ref, dy_ref, z_ref, d_ref, stage, grads, local, xyz, ready=None):
    sent = []
    for k, by in enumerate((2, 1, 3, 0)):
        quarter = shifted(xyz, 0, by)[0]
        columns = pl.ds(pl.multiple_of(quarter * HIDDEN, 128), HIDDEN)
        slot = k % 2
        if k >= 2:
            sent[k - 2].wait()
            if ready:
                ready(k - 2)
        both = dot(rows_ref[:, columns], d_ref[...], 0, 0)
        for c in range(2):
            for i in range(2):
                at = (2 * c + i) * HIDDEN
                stage[slot, 3 * c + i] = both[:, at : at + HIDDEN].astype(BF)
        low = dot(z_ref[...], dy_ref[:, columns], 0, 0)
        for c in range(2):
            stage[slot, 3 * c + 2] = low[c * HIDDEN : (c + 1) * HIDDEN].astype(BF)
        sent.append(local.start(stage.at[slot], grads.at[quarter]))
    for k in (2, 3):
        sent[k].wait()
        if ready and k == 2:
            ready(k)


def ring_devices(xyz, core, axis, steps=(1, 2, 3)):
    return [device_at(shifted(xyz, axis, by), core) for by in steps]


def arrive(copies):
    for copy in copies:
        copy.wait_recv()


class Gather:
    def __init__(self, sender, xyz, core):
        self.sender, self.xyz, self.core = sender, xyz, core

    def slab(self, job, stage, at, half=None):
        whole, lane, lanes, order = job
        index = list(at)
        for axis in order[:stage]:
            index[axis] = pl.ds(0, 4)
        if half is not None:
            index[order[0]] = pl.ds(2 * half, 2)
        return whole.at[index[0], index[1], index[2], :, pl.ds(lane, lanes)]

    def to(self, job, stage, by):
        return device_at(shifted(self.xyz, job[3][stage], by), self.core)

    def first(self, job, shard):
        source = shard.at[:, pl.ds(job[1], job[2])]
        target = self.slab(job, 0, self.xyz)
        return [self.sender.start(source, target, self.to(job, 0, by)) for by in (1, 3, 2)]

    def near(self, job, stage, steps=(1, 3)):
        block = self.slab(job, stage, self.xyz)
        return [self.sender.start(block, block, self.to(job, stage, by)) for by in steps]

    def relay(self, job, stage, near):
        copies = []
        for half, by in enumerate((1, 3)):
            near[half].wait_recv()
            at = shifted(self.xyz, job[3][stage], 4 - by)
            block = self.slab(job, stage, at, half)
            copies.append(self.sender.start(block, block, self.to(job, stage, by)))
        return copies

    def finish(self, near, relays):
        for copy in near:
            copy.wait_send()
        for copy in relays:
            copy.wait()


class ExpertSum:
    def __init__(self, r, layer, sender, local, xyz, core):
        self.r, self.sender, self.local, self.core = r, sender, local, core
        self.plus, self.minus = ring_devices(xyz, core, 0, (1, 3))
        self.grads, self.near, self.far, self.total = (
            getattr(r, f"{name}_{layer}") for name in ("grads", "near", "far", "total")
        )
        self.quarter = [shifted(xyz, 0, by)[0] for by in range(4)]

    def half(self, by, half):
        return self.grads.at[self.quarter[by], pl.ds(3 * half, 3)]

    def near_half(self, side, half):
        return self.near.at[side, pl.ds(3 * half, 3)]

    def send(self, part):
        go = self.sender.start
        if part == 0:
            self.passed = [
                go(self.half(2, 0), self.far.at[0], self.plus),
                go(self.half(2, 1), self.far.at[1], self.minus),
            ]
        elif part == 1:
            self.plain = [go(self.half(1, 1), self.near_half(0, 1), self.plus)]
        else:
            self.plain.append(go(self.half(3, 0), self.near_half(1, 0), self.minus))

    def start(self):
        for part in range(3):
            self.send(part)

    def relay(self):
        r, load = self.r, self.local.start
        own = [load(self.half(by, side), r.own.at[side]) for side, by in enumerate((1, 3))]
        came = []
        for side in range(2):
            self.passed[side].wait_recv()
            came.append(load(self.far.at[side], r.work.at[side]))
        for side, target in enumerate((self.plus, self.minus)):
            own[side].wait()
            came[side].wait()
            for i in range(3):
                value = r.own[side, i].astype(F32) + r.work[side, i].astype(F32)
                r.work[side, i] = value.astype(BF)
            self.plain.append(
                self.sender.start(r.work.at[side], self.near_half(side, side), target)
            )

    def finish(self):
        r, load = self.r, self.local.start
        for copy in self.plain:
            copy.wait()
        for copy in self.passed:
            copy.wait_send()

        def bring(i, slot):
            return [
                load(self.grads.at[self.quarter[0], i], r.own.at[slot, 0]),
                load(self.near.at[0, i], r.own.at[slot, 1]),
                load(self.near.at[1, i], r.own.at[slot, 2]),
            ]

        order, out = (3, 4, 5, 0, 1, 2), []
        loads = [bring(order[0], 0)]
        for k, i in enumerate(order):
            if k < 5:
                loads.append(bring(order[k + 1], (k + 1) % 2))
            for copy in loads[k]:
                copy.wait()
            slot = k % 2
            value = r.own[slot, 0].astype(F32) + r.own[slot, 1].astype(F32)
            r.ship[k] = (value + r.own[slot, 2].astype(F32)).astype(BF)
            to = self.total.at[self.core, i % 3]
            if k < 3:
                out.append(self.sender.start(r.ship.at[k], to, partner()))
            else:
                out.append(load(r.ship.at[k], to))
        for copy in out:
            copy.wait()


def tables(r):
    first = r.lengths[0, 0]
    second = first + r.lengths[0, 1]

    def place(index):
        segment = jnp.where(index >= first, 1, 0) + jnp.where(index >= second, 1, 0)
        start = jnp.where(segment == 0, 0, jnp.where(segment == 1, first, second))
        return segment, index - start

    shape = (TOKENS, TOKENS)
    lane = lax.broadcasted_iota(jnp.int32, shape, 1)
    row_segment, row_place = place(lax.broadcasted_iota(jnp.int32, shape, 0))
    key_segment, key_place = place(lane)
    allowed = (row_segment == key_segment) & (key_place <= row_place)
    r.allow[...] = jnp.where(allowed, 1.0, 0.0)
    half = jnp.where(lane < HEAD // 2, lane, lane - HEAD // 2).astype(F32)
    frequency = jnp.exp(half * (-2.0 / HEAD * math.log(rope_base)))
    angles = row_place.astype(F32) * frequency
    sign = jnp.where(lane < HEAD // 2, -1.0, 1.0)
    r.cos[...] = jnp.cos(angles)
    r.sin[...] = jnp.sin(angles) * sign


def assemble(r):
    square = (SHARD, SHARD)
    eye = lax.broadcasted_iota(jnp.int32, square, 0) == lax.broadcasted_iota(jnp.int32, square, 1)
    lane = lax.broadcasted_iota(jnp.int32, (SHARD, 128), 1)
    for l in range(LAYERS):
        r.shard[l, :, 0:768] = r.query[l]
        r.shard[l, :, 768:896] = r.key[l]
        r.shard[l, :, 896:QKV] = r.value[l]
        r.shard[l, :, QKV : QKV + OUT] = r.out[l]
        column = jnp.zeros((SHARD, 128), F32)
        for i, gain in enumerate((r.gain_a, r.gain_e)):
            spread = jnp.broadcast_to(gain[l : l + 1, :].astype(F32), square)
            spread = jnp.where(eye, spread, 0.0).astype(BF)
            column = column + dot(spread, jnp.where(lane == i, 1.0, 0.0).astype(BF))
        r.shard[l, :, QKV + OUT :] = column.astype(BF)


KEPT = dict(
    h=((TOKENS, WIDE), F32),
    n=((TOKENS, WIDE), BF),
    qkv=((TOKENS, QKV), BF),
    prob=((HEADS, TOKENS, TOKENS), F32),
    o=((TOKENS, OUT), BF),
    onehot=((SLOTS, TOKENS), BF),
    weighted=((SLOTS, TOKENS), F32),
)
KEPT_SPACE = {name: pltpu.VMEM(*spec) for name, spec in KEPT.items()}
HELD = dict(
    held_gate=pltpu.VMEM((2, WIDE, HIDDEN), BF),
    held_up=pltpu.VMEM((2, WIDE, HIDDEN), BF),
    held_down=pltpu.VMEM((2, HIDDEN, WIDE), BF),
)
ROWS = ((SLOTS, WIDE), BF)
INNER = ((2, SLOTS, HIDDEN), F32)
BLOCKS = ((PEERS, CAP, WIDE), BF)
PLANE = ((TOKENS, WIDE), F32)
FLAT = ((TOKENS, WIDE), BF)
GRADS = ((4, 6, HIDDEN, HIDDEN), BF)
BACKWARD = dict(
    z=pltpu.VMEM((SLOTS, 2 * HIDDEN), BF),
    d=pltpu.VMEM((SLOTS, 4 * HIDDEN), BF),
    dy=pltpu.VMEM(*ROWS),
    stage=pltpu.VMEM((2, 6, HIDDEN, HIDDEN), BF),
)


def sems(**counts):
    return {name: pltpu.SemaphoreType.DMA((n,)) for name, n in counts.items()}


def spaces(**specs):
    return {name: pltpu.VMEM(*spec) for name, spec in specs.items()}


def attend(r, l, x, pair, local, then=None):
    gain_a, gain_e = gain_rows(r.w)
    r.part0[...] = attention(
        x, gain_a, r.w, r.cos[...], r.sin[...], r.allow[...], r.n, r.qkv, r.prob, r.o
    ).astype(BF)
    copy = pair.start(r.part0, r.theirs0, partner())
    for name in ("n", "qkv", "prob", "o"):
        local.keep(getattr(r, name), getattr(r, f"{name}_{l}"))
    begun = then() if then else None
    copy.wait_recv()
    h = x + (r.part0[...].astype(F32) + r.theirs0[...].astype(F32))
    copy.wait_send()
    r.h[...] = h
    local.keep(r.h, getattr(r, f"h_{l}"))
    return (h * inverse_norm(h) * gain_e).astype(BF), begun


def front_body(r):
    xyz, core = coords(), lax.axis_index("blk")
    local, pair = Local(r.local), Sender(r.pair_send, r.pair_recv)
    sender = Sender(r.wide_send, r.wide_recv)
    gather = Gather(sender, xyz, core)
    held = (r.held_gate, r.held_up, r.held_down)
    count = hail(peers() + ring_devices(xyz, core, 0))
    mine = pl.ds(pl.multiple_of(core * HALF, HALF), HALF)
    here = [
        local.start(r.tok, r.tokens.at[:, mine]),
        local.start(r.cot_half, r.cot.at[:, mine]),
    ]
    assemble(r)
    here.append(local.start(r.shard.at[0], r.cube.at[xyz[0], xyz[1], xyz[2]]))
    here_later = local.start(r.shard.at[1], r.later.at[xyz[0], xyz[1], xyz[2]])
    heard(count)
    now = [(r.cube, p * PART, PART, order) for p, order in enumerate(ORDERS)]
    first = [c for job in now for c in gather.first(job, r.shard.at[0])]
    halves_sent = [
        sender.start(r.tok, r.tokens.at[:, mine], partner()),
        sender.start(r.cot_half, r.cot.at[:, mine], partner()),
    ]
    swaps = [[], []]
    for l in range(LAYERS):
        for name in ("gate", "up", "down"):
            ref = getattr(r, name).at[l, 1 - core]
            swaps[l].append(sender.start(ref, getattr(r, name + "_other").at[l], partner()))
    tables(r)
    for l, (onehot, weighted) in enumerate(((r.onehot_0, r.weighted_0), (r.onehot_1, r.weighted_1))):
        hot, heavy = slot_matrices(r.ids[l], r.weights[l])
        onehot[...] = hot.astype(BF)
        weighted[...] = heavy
    for copy in here:
        copy.wait()
    arrive(first)
    near = [gather.near(job, 1, (1, 3, 2)) for job in now]

    def onward(job, at):
        block = gather.slab(job, 1, at)
        return at, [sender.start(block, block, gather.to(job, 2, by)) for by in (1, 3)]

    last = [[onward(job, xyz)] for job in now]
    arrive(halves_sent)
    slot_weight = jnp.sum(r.weighted_1[...], axis=1, keepdims=True)
    store_rows(r.sent_g, dot(r.onehot_1[...], r.cot[...]) * slot_weight)
    for n, by in enumerate((1, 3, 2)):
        for p, job in enumerate(now):
            near[p][n].wait_recv()
            last[p].append(onward(job, shifted(xyz, job[3][1], 4 - by)))
    relays = []
    for m in range(4):
        for p, job in enumerate(now):
            at, copies = last[p][m]
            for half, by in enumerate((1, 3)):
                copies[half].wait_recv()
                block = gather.slab(job, 1, shifted(at, job[3][2], 4 - by), half)
                relays.append(sender.start(block, block, gather.to(job, 2, by)))
    arrive(swaps[0])
    loads = expert_weight_copies(0, r, local)
    arrive(relays)
    jobs = [(r.later, *job) for job in LATER]
    first_later = [c for job in jobs for c in gather.first(job, r.shard.at[1])]
    r.w[...] = r.cube[...].astype(F32).reshape(WIDE, COLS).astype(BF)
    w_kept = local.start(r.w, r.w_0)

    def second():
        here_later.wait()
        arrive(first_later)
        return [c for job in jobs for c in gather.near(job, 1, (1, 3, 2))]

    m, near_later = attend(r, 0, r.tokens[...].astype(F32), pair, local, second)
    store_rows(r.sent, dot(r.onehot_0[...], m))
    out0 = Exchange(r, 0, r.sent, r.came, False)
    out0.start()
    arrive(near_later)
    last_later = [gather.near(job, 2) for job in jobs]
    relays_later = {}
    for copy in loads:
        copy.wait()
    back0 = Exchange(r, 1, r.turn, r.back, True)
    for g in range(2):
        out0.arrive(g)
        at = pl.ds(GROUP * g, GROUP)
        r.rows[at] = rows_of(group_of(r.came, g))
        store_rows(group_of(r.turn, g), expert_forward(g, r.rows[at], held, r.a, r.b))
        back0.start(g)
    rows_kept = [local.start(r.rows, r.rows_0), local.start(r.a, r.a_0), local.start(r.b, r.b_0)]
    out0.sent()
    arrive(swaps[1])
    loads = expert_weight_copies(1, r, local)
    for i in range(4):
        relays_later[i] = gather.relay(jobs[i], 2, last_later[i])
    back0.arrive()
    out_g = Exchange(r, 3, r.sent_g, r.came_g, False)
    out_g.start()
    r.part1[...] = combine(r.weighted_0[...], rows_of(r.back)).astype(BF)
    copy = pair.start(r.part1, r.theirs1, partner())
    w_kept.wait()
    local.wait_kept()
    local.kept = []
    copy.wait_recv()
    x = r.h[...] + (r.part1[...].astype(F32) + r.theirs1[...].astype(F32))
    r.stream[...] = x
    copy.wait_send()
    for i in range(4):
        arrive(relays_later[i])
    for copy in relays + [c for n in near for c in n] + [c for n in last for _, two in n for c in two]:
        copy.wait_send()
    load = local.start(r.later, r.cube)
    load.wait()
    r.w[...] = r.cube[...].astype(F32).reshape(WIDE, COLS).astype(BF)
    local.keep(r.w, r.w_1)
    m, _ = attend(r, 1, x, pair, local)
    store_rows(r.sent, dot(r.onehot_1[...], m))
    out1 = Exchange(r, 2, r.sent, r.came, False)
    out1.start()
    back0.sent()
    out_g.arrive()
    r.dy[...] = rows_of(r.came_g)
    for copy in loads + rows_kept:
        copy.wait()
    for g in range(2):
        out1.arrive(g)
        at = pl.ds(GROUP * g, GROUP)
        r.rows[at] = rows_of(group_of(r.came, g))
        store_rows(group_of(r.back, g), expert_forward(g, r.rows[at], held, r.a, r.b))
        result = expert_backward(g, r.dy[at], held, r.a, r.b, r.z, r.d)
        store_rows(group_of(r.turn, g), result)
    local.keep(r.back, r.y_1)
    local.keep(r.turn, r.m_1)
    expert_gradients(r.rows, r.dy, r.z, r.d, r.stage, r.grads_1, local, xyz)
    out1.sent()
    out_g.sent()
    for copy in first + first_later + near_later + halves_sent + swaps[0] + swaps[1]:
        copy.wait_send()
    for i in range(4):
        for copy in last_later[i] + relays_later[i]:
            copy.wait_send()
    local.wait_kept()


def turned(value):
    return value.astype(F32).T.reshape(4, 4, 4, SHARD, TOKENS).astype(BF)


def own_part(ref, axis, index):
    return ref.at[:, index] if axis == 1 else ref.at[:, :, index]


def share_factor(ref, into, axis, sender, xyz, core):
    copies = []
    for by in (1, 3, 2):
        there = shifted(xyz, axis, by)
        copies.append(
            sender.start(own_part(ref, axis, there[axis]), into.at[by - 1], device_at(there, core))
        )
    return copies


def share_whole(ref, axis, sender, xyz, core):
    return [
        sender.start(
            ref.at[pl.ds(0, TOKENS)],
            ref.at[pl.ds(by * TOKENS, TOKENS)],
            device_at(shifted(xyz, axis, by), core),
        )
        for by in (1, 3, 2)
    ]


def quarter_sum(own, came, axis, xyz, right):
    first = own_part(own, axis, xyz[axis])[...]
    pieces = [first] + [came[i] for i in range(3)]
    left = [p.astype(F32).reshape(HIDDEN, TOKENS).astype(BF) for p in pieces]
    return dot(jnp.concatenate(left, axis=1), right[...])


def back_body(r):
    xyz, core = coords(), lax.axis_index("blk")
    local, pair = Local(r.local), Sender(r.pair_send, r.pair_recv)
    sender = Sender(r.wide_send, r.wide_recv)

    def load_layer(l):
        names = ("w", "h", "qkv", "prob", "o")
        return [local.start(getattr(r, f"{name}_{l}"), getattr(r, name)) for name in names]

    loads = load_layer(1)
    count = hail(peers() + ring_devices(xyz, core, 0))
    sums = [ExpertSum(r, l, sender, local, xyz, core) for l in range(LAYERS)]
    heard(count)
    came_m, onehot = (r.came_0, r.came_1), (r.onehot_0, r.onehot_1)
    back = [Exchange(r, 2, r.turn, r.came_0, True), Exchange(r, 0, r.m_1, r.came_1, True)]
    out_g = Exchange(r, 1, r.sent, r.came_g, False)
    y_back = Exchange(r, 3, r.y_1, r.came_1, True)
    back[1].start()
    sums[1].start()
    weights = expert_weight_copies(0, r, local)
    weights += [local.start(getattr(r, name + "_0"), getattr(r, name)) for name in ("rows", "a", "b")]
    r.n_turned[1] = turned(r.n_1[...])
    r.n_turned[0] = turned(r.n_0[...])
    for copy in loads:
        copy.wait()
    shared = [[], []]
    scale = HEAD ** (-0.5)
    row = lax.broadcasted_iota(jnp.int32, (8, WIDE), 0)
    r.gain_sum[1] = jnp.zeros((8, WIDE), F32)
    inner, across = [None] * 2, [None] * 2
    for l in (1, 0):
        x = (r.stream if l == 1 else r.tokens)[...].astype(F32)
        gain_a, gain_e = gain_rows(r.w)
        r.o_all[l, 0:TOKENS] = r.o[...]
        back[l].arrive()
        r.part[0] = dot(onehot[l][...], rows_of(came_m[l]), 0, 0)
        inner[l] = pair.start(r.part.at[0], r.theirs.at[l, 0], partner())
        if l == 1:
            for i in (1, 0):
                shared[i] += share_factor(r.n_turned.at[i], r.n_came.at[i], 1, sender, xyz, core)
        else:
            shared[1] += share_whole(r.lin_all.at[1], 1, sender, xyz, core)
        shared[l] += share_whole(r.o_all.at[l], 2, sender, xyz, core)
        inner[l].wait_recv()
        dm = r.part[0] + r.theirs[l, 0]
        hidden = r.h[...]
        inward, gain_grad_e = norm_back(hidden, inverse_norm(hidden), gain_e, dm)
        gh = (r.cot[...].astype(F32) if l == 1 else r.flow[...]) + inward
        r.flow[...] = gh
        da = gh.astype(BF)
        r.da_turned[l] = turned(gh)
        shared[l] += share_factor(r.da_turned.at[l], r.da_came.at[l], 2, sender, xyz, core)
        do = dot(da, r.w[:, QKV : QKV + OUT]).astype(BF)
        key = r.qkv[:, HEADS * HEAD : (HEADS + 1) * HEAD]
        value = r.qkv[:, (HEADS + 1) * HEAD :]
        key_grad, value_grad = None, None
        cosine, sine = r.cos[...], r.sin[...]
        lin = r.lin_all.at[l]
        for i in range(HEADS):
            prob_i = r.prob[i]
            do_i = head_of(do, i)
            q_i = r.qkv[:, i * HEAD : (i + 1) * HEAD]
            dprob = dot(do_i, value, 1, 1)
            centre = jnp.sum(prob_i * dprob, axis=-1, keepdims=True)
            ds = (prob_i * (dprob - centre)).astype(BF)
            dq = dot(ds, key) * scale
            lin[0:TOKENS, i * HEAD : (i + 1) * HEAD] = unrotate(dq, cosine, sine).astype(BF)
            dk = dot(ds, q_i, 0, 0)
            dv = dot(prob_i.astype(BF), do_i, 0, 0)
            key_grad = dk if key_grad is None else key_grad + dk
            value_grad = dv if value_grad is None else value_grad + dv
        lin[0:TOKENS, HEADS * HEAD : (HEADS + 1) * HEAD] = unrotate(
            key_grad * scale, cosine, sine
        ).astype(BF)
        lin[0:TOKENS, (HEADS + 1) * HEAD :] = value_grad.astype(BF)
        r.part[1] = dot(lin[0:TOKENS, :], r.w[:, 0:QKV], 1, 1)
        across[l] = pair.start(r.part.at[1], r.theirs.at[l, 1], partner())
        if l == 1:
            r.kept_half[...] = jnp.where(core == 1, r.h[:, HALF:], r.h[:, :HALF])
            loads = load_layer(0)
        else:
            shared[0] += share_whole(r.lin_all.at[0], 1, sender, xyz, core)
            sums[0].relay()
        across[l].wait_recv()
        dn = r.part[1] + r.theirs[l, 1]
        inward, gain_grad_a = norm_back(x, inverse_norm(x), gain_a, dn)
        flow = r.flow[...] + inward
        gains = r.gain_sum[1]
        for i, grad in enumerate((gain_grad_a, gain_grad_e)):
            grad = jnp.sum(grad, axis=0, keepdims=True)
            gains = jnp.where(row == 2 * l + i, jnp.broadcast_to(grad, (8, WIDE)), gains)
        r.gain_sum[1] = gains
        inner[l].wait_send()
        across[l].wait_send()
        if l == 0:
            r.tokens_grad[...] = jnp.where(core == 1, flow[:, HALF:], flow[:, :HALF])
            continue
        r.flow[...] = flow
        slot_weight = jnp.sum(r.weighted_0[...], axis=1, keepdims=True)
        high, low = halves(flow)
        hot = r.onehot_0[...]
        store_rows(r.sent, (dot(hot, high) + dot(hot, low)) * slot_weight)
        out_g.start()
        sums[1].relay()
        for copy in weights:
            copy.wait()
        held = (r.held_gate, r.held_up, r.held_down)
        for g in range(2):
            out_g.arrive(g)
            at = pl.ds(GROUP * g, GROUP)
            r.dy[at] = rows_of(group_of(r.came_g, g))
            result = expert_backward(g, r.dy[at], held, r.a, r.b, r.z, r.d)
            store_rows(group_of(r.turn, g), result)
            back[0].start(g)
        expert_gradients(
            r.rows, r.dy, r.z, r.d, r.stage, r.grads_0, local, xyz, sums[0].send
        )
        sums[1].finish()
        for copy in loads:
            copy.wait()
    finish_sums(r, shared, y_back, sender, xyz, core)
    y_back.arrive()
    mixed = combine(r.weighted_1[...], rows_of(r.came_1))
    r.half[...] = jnp.where(core == 1, mixed[:, :HALF], mixed[:, HALF:])
    third = pair.start(r.half, r.half_theirs, partner())
    own = jnp.where(core == 1, mixed[:, HALF:], mixed[:, :HALF])
    third.wait()
    r.block_out[...] = (r.kept_half[...] + (own + r.half_theirs[...])).astype(BF)
    sums[0].finish()
    for exchange in (*back, out_g, y_back):
        exchange.sent()


def late_start(r, l, sender, xyz, core):
    copies = []
    for ref, came, axis in ((r.sum_a, r.near_a, 2), (r.sum_b, r.near_b, 1)):
        for by in (1, 3, 2):
            there = shifted(xyz, axis, by)
            copies.append(
                sender.start(ref.at[l, :, there[axis]], came.at[l, by - 1], device_at(there, core))
            )
    return copies


def late_middle(r, l, sender, xyz, core, copies):
    arrive(copies)
    for ref, came, axis, lanes in (
        (r.sum_a, r.near_a, 2, slice(0, QKV)),
        (r.sum_b, r.near_b, 1, slice(QKV, QKV + OUT)),
    ):
        total = ref[l, :, xyz[axis]].astype(F32)
        for i in range(3):
            total = total + came[l, i].astype(F32)
        r.line[l, :, :, lanes] = total.astype(BF)
    copies = []
    for by in (1, 3, 2):
        there = shifted(xyz, 0, by)
        copies.append(
            sender.start(r.line.at[l, there[0]], r.line_came.at[l, by - 1], device_at(there, core))
        )
    return copies


def late_end(r, l, xyz, copies):
    for copy in copies:
        copy.wait()
    total = r.line[l, xyz[0]].astype(F32)
    for i in range(3):
        total = total + r.line_came[l, i].astype(F32)
    r.weight_grad[l] = total


def gains_along(r, axis, sender, xyz, core):
    copies = []
    for by in (1, 3, 2):
        there = shifted(xyz, axis, by)
        if axis == 0:
            quarter = pl.ds(pl.multiple_of(there[0] * HIDDEN, 128), HIDDEN)
            src, dst = r.gain_sum.at[0, :, quarter], r.gain_last.at[by - 1]
        else:
            src, dst = r.gain_sum.at[axis], r.gain_came.at[axis - 1, by - 1]
        copies.append(sender.start(src, dst, device_at(there, core)))
    return copies


def gains_next(r, axis, xyz, copies):
    for copy in copies:
        copy.wait()
    if axis == 0:
        total = r.gain_sum[0, :, pl.ds(pl.multiple_of(xyz[0] * HIDDEN, 128), HIDDEN)]
        for i in range(3):
            total = total + r.gain_last[i]
        return total
    total = r.gain_sum[axis]
    for i in range(3):
        total = total + r.gain_came[axis - 1, i]
    return total


def finish_sums(r, shared, y_back, sender, xyz, core):
    def quarter(l):
        arrive(shared[l])
        wide = (4, 4, SHARD, QKV)
        total = quarter_sum(r.n_turned.at[l], r.n_came.at[l], 1, xyz, r.lin_all.at[l])
        r.sum_a[l] = total.reshape(wide).astype(BF)
        wide = (4, 4, SHARD, OUT)
        total = quarter_sum(r.da_turned.at[l], r.da_came.at[l], 2, xyz, r.o_all.at[l])
        r.sum_b[l] = total.reshape(wide).astype(BF)
        return late_start(r, l, sender, xyz, core)

    along = gains_along(r, 1, sender, xyz, core)
    above = quarter(1)
    y_back.start()
    r.gain_sum[2] = gains_next(r, 1, xyz, along)
    along = gains_along(r, 2, sender, xyz, core)
    above_last = late_middle(r, 1, sender, xyz, core, above)
    r.gain_sum[0] = gains_next(r, 2, xyz, along)
    along = gains_along(r, 0, sender, xyz, core)
    lower = quarter(0)
    late_end(r, 1, xyz, above_last)
    r.gain_total[...] = gains_next(r, 0, xyz, along)
    lower_last = late_middle(r, 0, sender, xyz, core, lower)
    late_end(r, 0, xyz, lower_last)
    for copy in shared[0] + shared[1] + above + lower:
        copy.wait_send()


def finish_body(r):
    local = Local(r.local)
    loads = [
        [local.start(total.at[:, i], r.narrow.at[l, i]) for i in range(3)]
        for l, total in enumerate((r.total_below, r.total_above))
    ]
    r.block_out[...] = r.block_in[...]
    r.tokens_grad[...] = r.tokens_in[...]
    place = lax.axis_index("expert") * SHARD
    near = pltpu.roll(r.gain_total[...], lax.rem(HIDDEN - place, HIDDEN), 1)
    for l in range(LAYERS):
        r.gain_a[l : l + 1, :] = near[2 * l : 2 * l + 1, :SHARD]
        r.gain_e[l : l + 1, :] = near[2 * l + 1 : 2 * l + 2, :SHARD]
        r.query[l] = r.weight_grad[l, :, :768]
        r.key[l] = r.weight_grad[l, :, 768:896]
        r.value[l] = r.weight_grad[l, :, 896:QKV]
        r.out[l] = r.weight_grad[l, :, QKV:]
    for l in range(LAYERS):
        for i, out in enumerate((r.gate, r.up, r.down)):
            loads[l][i].wait()
            r.broad[l, i] = r.narrow[l, i].astype(F32)
            local.keep(r.broad.at[l, i], out.at[l])
    local.wait_kept()


def kernel_call(body, name, cid, ins, outs, scratch, aliases=()):
    names = [*ins, *outs, *scratch]
    assert len(set(names)) == len(names)

    def kernel(*refs):
        body(types.SimpleNamespace(**dict(zip(names, refs))))

    results = pl.pallas_call(
        kernel,
        out_shape=[jax.ShapeDtypeStruct(shape, kind) for shape, kind, _ in outs.values()],
        in_specs=[space for _, space in ins.values()],
        out_specs=[space for _, _, space in outs.values()],
        scratch_shapes=list(scratch.values()),
        input_output_aliases={list(ins).index(a): list(outs).index(b) for a, b in aliases},
        compiler_params=pltpu.CompilerParams(
            collective_id=cid, has_side_effects=cid is not None, vmem_limit_bytes=LIMIT
        ),
        name=name,
    )(*[array for array, _ in ins.values()])
    return types.SimpleNamespace(**dict(zip(outs, results)))


def per_device(
    tokens_in,
    seq_lengths,
    expert_ids,
    gate_weights,
    attention_gain,
    query_weight,
    key_weight,
    value_weight,
    out_weight,
    expert_gain,
    gate_weight,
    up_weight,
    down_weight,
    cotangent,
):
    cube = (4, 4, 4, SHARD, COLS)
    own = dict(gate=(gate_weight, ANY), up=(up_weight, ANY), down=(down_weight, ANY))
    exchanges = sems(
        **{f"{way}{i}": PEERS for way in ("send", "recv") for i in range(4)}, pair_send=5, pair_recv=5
    )
    kept = ("h", "n", "qkv", "prob", "o")
    w_space = dict(w=pltpu.VMEM((WIDE, COLS), BF))
    start = kernel_call(
        front_body,
        "front",
        1,
        dict(
            lengths=(seq_lengths, SMEM),
            query=(query_weight, VMEM),
            key=(key_weight, VMEM),
            value=(value_weight, VMEM),
            out=(jnp.swapaxes(out_weight, 1, 2), VMEM),
            gain_a=(attention_gain, VMEM),
            gain_e=(expert_gain, VMEM),
            tok=(tokens_in, VMEM),
            cot_half=(cotangent, VMEM),
            ids=(jnp.swapaxes(expert_ids, 1, 2), VMEM),
            weights=(jnp.swapaxes(gate_weights, 1, 2), VMEM),
            **own,
        ),
        dict(
            w_0=((WIDE, COLS), BF, ANY),
            w_1=((WIDE, COLS), BF, ANY),
            later=(cube, BF, ANY),
            tokens=((TOKENS, WIDE), BF, VMEM),
            cot=((TOKENS, WIDE), BF, VMEM),
            stream=(*PLANE, VMEM),
            cos=((TOKENS, HEAD), F32, VMEM),
            sin=((TOKENS, HEAD), F32, VMEM),
            gate_other=((LAYERS, WIDE, HIDDEN), BF, ANY),
            up_other=((LAYERS, WIDE, HIDDEN), BF, ANY),
            down_other=((LAYERS, HIDDEN, WIDE), BF, ANY),
            rows_0=(*ROWS, ANY),
            a_0=(*INNER, ANY),
            b_0=(*INNER, ANY),
            y_1=(*BLOCKS, ANY),
            m_1=(*BLOCKS, ANY),
            grads_1=(*GRADS, ANY),
            **{f"{name}_{l}": (*KEPT[name], ANY) for l in range(LAYERS) for name in kept},
            **{
                f"{name}_{l}": (*KEPT[name], VMEM)
                for l in range(LAYERS)
                for name in ("onehot", "weighted")
            },
        ),
        dict(
            shard=pltpu.VMEM((LAYERS, SHARD, COLS), BF),
            cube=pltpu.VMEM(cube, BF),
            allow=pltpu.VMEM((TOKENS, TOKENS), F32),
            **w_space,
            **{name: KEPT_SPACE[name] for name in kept},
            **HELD,
            **BACKWARD,
            **spaces(sent=BLOCKS, came=BLOCKS, back=BLOCKS, sent_g=BLOCKS, came_g=BLOCKS),
            **spaces(turn=BLOCKS, rows=ROWS, a=INNER, b=INNER),
            **spaces(part0=FLAT, theirs0=FLAT, part1=FLAT, theirs1=FLAT),
            **exchanges,
            **sems(wide_send=114, wide_recv=114, local=50),
        ),
    )
    experts = dict(
        own,
        gate_other=(start.gate_other, ANY),
        up_other=(start.up_other, ANY),
        down_other=(start.down_other, ANY),
    )
    part_a, part_b = (4, 4, SHARD, QKV), (4, 4, SHARD, OUT)
    total = ((2, 3, HIDDEN, HIDDEN), BF, ANY)
    near, far = ((2, 6, HIDDEN, HIDDEN), BF, ANY), ((2, 3, HIDDEN, HIDDEN), BF, ANY)
    factor, quarter = (4, 4, 4, SHARD, TOKENS), (3, 4, 4, SHARD, TOKENS)
    by_layer = {}
    for l in range(LAYERS):
        for name in ("h", "qkv", "prob", "o", "w"):
            by_layer[f"{name}_{l}"] = (getattr(start, f"{name}_{l}"), ANY)
        for name in ("n", "onehot", "weighted"):
            by_layer[f"{name}_{l}"] = (getattr(start, f"{name}_{l}"), VMEM)
    end = kernel_call(
        back_body,
        "backward",
        4,
        dict(
            stream=(start.stream, VMEM),
            tokens=(start.tokens, VMEM),
            cot=(start.cot, VMEM),
            cos=(start.cos, VMEM),
            sin=(start.sin, VMEM),
            **by_layer,
            **{
                name: (getattr(start, name), ANY)
                for name in ("m_1", "y_1", "grads_1", "rows_0", "a_0", "b_0")
            },
            **experts,
        ),
        dict(
            block_out=((TOKENS, HALF), BF, VMEM),
            tokens_grad=((TOKENS, HALF), F32, VMEM),
            weight_grad=((LAYERS, SHARD, QKV + OUT), F32, VMEM),
            gain_total=((8, HIDDEN), F32, VMEM),
            total_0=total,
            total_1=total,
            grads_0=(*GRADS, ANY),
            near_0=near,
            near_1=near,
            far_0=far,
            far_1=far,
        ),
        dict(
            **w_space,
            **HELD,
            **BACKWARD,
            **{name: KEPT_SPACE[name] for name in ("h", "qkv", "prob", "o")},
            **spaces(rows=ROWS, a=INNER, b=INNER, flow=PLANE),
            **spaces(sent=BLOCKS, turn=BLOCKS),
            **spaces(came_0=BLOCKS, came_1=BLOCKS, came_g=BLOCKS),
            part=pltpu.VMEM((2, TOKENS, WIDE), F32),
            theirs=pltpu.VMEM((LAYERS, 2, TOKENS, WIDE), F32),
            half=pltpu.VMEM((TOKENS, HALF), F32),
            half_theirs=pltpu.VMEM((TOKENS, HALF), F32),
            kept_half=pltpu.VMEM((TOKENS, HALF), F32),
            own=pltpu.VMEM((2, 3, HIDDEN, HIDDEN), BF),
            work=pltpu.VMEM((2, 3, HIDDEN, HIDDEN), BF),
            ship=pltpu.VMEM((6, HIDDEN, HIDDEN), BF),
            n_turned=pltpu.VMEM((LAYERS, *factor), BF),
            da_turned=pltpu.VMEM((LAYERS, *factor), BF),
            n_came=pltpu.VMEM((LAYERS, *quarter), BF),
            da_came=pltpu.VMEM((LAYERS, *quarter), BF),
            lin_all=pltpu.VMEM((LAYERS, 4 * TOKENS, QKV), BF),
            o_all=pltpu.VMEM((LAYERS, 4 * TOKENS, OUT), BF),
            sum_a=pltpu.VMEM((LAYERS, *part_a), BF),
            sum_b=pltpu.VMEM((LAYERS, *part_b), BF),
            near_a=pltpu.VMEM((LAYERS, 3, 4, SHARD, QKV), BF),
            near_b=pltpu.VMEM((LAYERS, 3, 4, SHARD, OUT), BF),
            line=pltpu.VMEM((LAYERS, 4, SHARD, QKV + OUT), BF),
            line_came=pltpu.VMEM((LAYERS, 3, SHARD, QKV + OUT), BF),
            gain_sum=pltpu.VMEM((3, 8, WIDE), F32),
            gain_came=pltpu.VMEM((2, 3, 8, WIDE), F32),
            gain_last=pltpu.VMEM((3, 8, HIDDEN), F32),
            **exchanges,
            **sems(wide_send=72, wide_recv=72, local=84),
        ),
    )
    expert_out = ((LAYERS, 2, HIDDEN, HIDDEN), F32, ANY)
    out = kernel_call(
        finish_body,
        "finish",
        None,
        dict(
            block_in=(end.block_out, VMEM),
            tokens_in=(end.tokens_grad, VMEM),
            total_above=(end.total_1, ANY),
            total_below=(end.total_0, ANY),
            weight_grad=(end.weight_grad, VMEM),
            gain_total=(end.gain_total, VMEM),
        ),
        dict(
            block_out=((TOKENS, HALF), BF, VMEM),
            tokens_grad=((TOKENS, HALF), F32, VMEM),
            gain_a=((LAYERS, SHARD), F32, VMEM),
            query=((LAYERS, SHARD, 768), F32, VMEM),
            key=((LAYERS, SHARD, 128), F32, VMEM),
            value=((LAYERS, SHARD, 128), F32, VMEM),
            out=((LAYERS, SHARD, OUT), F32, VMEM),
            gain_e=((LAYERS, SHARD), F32, VMEM),
            gate=expert_out,
            up=expert_out,
            down=expert_out,
        ),
        dict(
            narrow=pltpu.VMEM((LAYERS, 3, 2, HIDDEN, HIDDEN), BF),
            broad=pltpu.VMEM((LAYERS, 3, 2, HIDDEN, HIDDEN), F32),
            **sems(local=14),
        ),
    )
    return (
        out.block_out,
        out.tokens_grad,
        out.gain_a,
        out.query,
        out.key,
        out.value,
        jnp.swapaxes(out.out, 1, 2),
        out.gain_e,
        out.gate,
        out.up,
        out.down,
    )


def solution(mesh):
    placed = (
        P(("dp", "expert"), "blk"),
        P(("dp", "expert"), None),
        P(None, ("dp", "expert"), None),
        P(None, ("dp", "expert"), None),
        P(None, ("dp", "expert")),
        P(None, ("dp", "expert"), "blk"),
        P(None, ("dp", "expert"), "blk"),
        P(None, ("dp", "expert"), "blk"),
        P(None, "blk", ("dp", "expert")),
        P(None, ("dp", "expert")),
        P(None, "expert", None, "blk"),
        P(None, "expert", None, "blk"),
        P(None, "expert", "blk", None),
        P(("dp", "expert"), "blk"),
    )
    return jax.shard_map(
        per_device,
        mesh=mesh,
        in_specs=placed,
        out_specs=(
            P(("dp", "expert"), "blk"),
            P(("dp", "expert"), "blk"),
            P(None, ("dp", "expert")),
            P(None, ("dp", "expert"), "blk"),
            P(None, ("dp", "expert"), "blk"),
            P(None, ("dp", "expert"), "blk"),
            P(None, "blk", ("dp", "expert")),
            P(None, ("dp", "expert")),
            P(None, "expert", "dp", "blk"),
            P(None, "expert", "dp", "blk"),
            P(None, "expert", "blk", "dp"),
        ),
        check_vma=False,
    )
```

```python
import functools
import math
import types

import jax
import jax.numpy as jnp
from jax import lax
from jax.experimental import pallas as pl
from jax.experimental.pallas import tpu as pltpu
from jax.sharding import PartitionSpec as P

HEAD = 128
TOP = 4
LAYERS = 2
F32 = jnp.float32
BF = jnp.bfloat16
MESH = pl.DeviceIdType.MESH

epsilon = 1e-06
rope_base = 1000000.0

TOKENS = 128
WIDE = 1536
HALF = WIDE // 2
HEADS = 6
HIDDEN = 384
PEERS = 16
CAP = 24
SLOTS = PEERS * CAP
SHARD = 24
QKV = 1024
OUT = 768
COLS = QKV + OUT + 128
PART = COLS // 3
ORDERS = ((0, 1, 2), (1, 2, 0), (2, 0, 1))
LIMIT = 60 << 20
LATER = ((0, 768, (1, 2, 0)), (768, 768, (2, 1, 0)), (1536, 128, (0, 2, 1)), (1664, 256, (0, 1, 2)))

ANY = pl.BlockSpec(memory_space=pl.ANY)
VMEM = pl.BlockSpec(memory_space=pltpu.VMEM)
SMEM = pl.BlockSpec(memory_space=pltpu.SMEM)


def dot(a, b, ca=1, cb=0):
    return lax.dot_general(a, b, (((ca,), (cb,)), ((), ())), preferred_element_type=F32)


def coords():
    ex = lax.axis_index("expert")
    return [lax.axis_index("dp"), lax.div(ex, 4), lax.rem(ex, 4)]


def shifted(xyz, axis, by):
    moved = list(xyz)
    moved[axis] = lax.rem(xyz[axis] + by, 4)
    return moved


def device_at(xyz, core):
    return (xyz[0], xyz[1] * 4 + xyz[2], core)


def partner():
    return (lax.axis_index("dp"), lax.axis_index("expert"), 1 - lax.axis_index("blk"))


def hail(devices):
    barrier = pltpu.get_barrier_semaphore()
    for device in devices:
        pl.semaphore_signal(barrier, inc=1, device_id=device, device_id_type=MESH)
    return len(devices)


def heard(count):
    pl.semaphore_wait(pltpu.get_barrier_semaphore(), count)


def peer(step):
    dp, ex, core = (lax.axis_index(a) for a in ("dp", "expert", "blk"))
    return (dp, lax.rem(ex + step, PEERS), core)


def peers():
    return [peer(d) for d in range(1, PEERS)] + [partner()]


class Local:
    def __init__(self, sem):
        self.sem, self.at, self.kept = sem, 0, []

    def start(self, src, dst):
        assert self.at < self.sem.shape[0]
        copy = pltpu.make_async_copy(src, dst, self.sem.at[self.at])
        self.at += 1
        copy.start()
        return copy

    def keep(self, src, dst):
        self.kept.append(self.start(src, dst))

    def wait_kept(self):
        for copy in self.kept:
            copy.wait()


class Sender:
    def __init__(self, send, recv):
        self.send, self.recv, self.at = send, recv, 0

    def start(self, src, dst, device):
        assert self.at < self.send.shape[0]
        copy = pltpu.make_async_remote_copy(
            src_ref=src,
            dst_ref=dst,
            send_sem=self.send.at[self.at],
            recv_sem=self.recv.at[self.at],
            device_id=device,
            device_id_type=MESH,
        )
        self.at += 1
        copy.start()
        return copy


def step_of(k):
    row = lax.div(lax.rem(k, 8), 2)
    return 4 * row + 2 * lax.rem(k, 2) + lax.rem(row + lax.div(k, 8), 2)


class Exchange:
    def __init__(self, r, number, src, dst, back):
        self.send, self.recv = getattr(r, f"send{number}"), getattr(r, f"recv{number}")
        self.src, self.dst, self.back = src, dst, back
        self.me = lax.axis_index("expert")

    def copy(self, k):
        step = step_of(k)
        target = peer(PEERS - step if self.back else step)
        return pltpu.make_async_remote_copy(
            src_ref=self.src.at[k if self.back else target[1]],
            dst_ref=self.dst.at[self.me if self.back else k],
            send_sem=self.send.at[k],
            recv_sem=self.recv.at[k],
            device_id=target,
            device_id_type=MESH,
        )

    def own(self):
        src = self.src.at[0 if self.back else self.me]
        dst = self.dst.at[self.me if self.back else 0]
        return pltpu.make_async_copy(src, dst, self.send.at[0])

    def each(self, group, act):
        first, last = ((1, PEERS), (1, 8), (8, PEERS))[group + 1]

        def body(k, carry):
            act(self.copy(k))
            return carry

        lax.fori_loop(first, last, body, 0)

    def start(self, group=-1):
        if group <= 0:
            self.own().start()
        self.each(group, lambda copy: copy.start())

    def arrive(self, group=-1):
        if group <= 0:
            self.own().wait()
        self.each(group, lambda copy: copy.wait_recv())

    def sent(self):
        self.each(-1, lambda copy: copy.wait_send())


def rows_of(ref):
    value = ref[...]
    return value.astype(F32).reshape(value.shape[0] * CAP, WIDE).astype(BF)


def store_rows(ref, rows):
    ref[...] = rows.reshape(rows.shape[0] // CAP, CAP, WIDE).astype(BF)


def group_of(ref, group):
    return ref.at[pl.ds(8 * group, 8)]


def slot_matrices(ids, weights):
    core = lax.axis_index("blk")
    expert = 2 * lax.broadcasted_iota(jnp.int32, (PEERS, TOKENS), 0) + core
    chosen = jnp.zeros((PEERS, TOKENS), F32)
    gate = jnp.zeros((PEERS, TOKENS), F32)
    for j in range(TOP):
        hit = jnp.where(ids[j : j + 1, :] == expert, 1.0, 0.0)
        chosen = chosen + hit
        gate = gate + hit * weights[j : j + 1, :]
    before = lax.broadcasted_iota(jnp.int32, (TOKENS, TOKENS), 0) < lax.broadcasted_iota(
        jnp.int32, (TOKENS, TOKENS), 1
    )
    rank = dot(chosen.astype(BF), jnp.where(before, 1.0, 0.0).astype(BF))
    rank = jnp.where(chosen > 0.0, rank, -1.0)
    shape = (PEERS, CAP, TOKENS)
    place = lax.broadcasted_iota(jnp.int32, shape, 1).astype(F32)
    onehot = jnp.where(jnp.broadcast_to(rank[:, None, :], shape) == place, 1.0, 0.0)
    weighted = onehot * jnp.broadcast_to(gate[:, None, :], shape)
    return onehot.reshape(SLOTS, TOKENS), weighted.reshape(SLOTS, TOKENS)


def halves(value):
    high = value.astype(BF)
    return high, (value - high.astype(F32)).astype(BF)


def combine(weighted, rows):
    high, low = halves(weighted)
    return dot(high, rows, 0, 0) + dot(low, rows, 0, 0)


def gain_rows(w_ref):
    unit = jnp.where(
        lax.broadcasted_iota(jnp.int32, (8, 128), 0) == lax.broadcasted_iota(jnp.int32, (8, 128), 1),
        1.0,
        0.0,
    ).astype(BF)
    rows = dot(unit, w_ref[:, QKV + OUT : COLS], 1, 1)
    return rows[0:1, :], rows[1:2, :]


def inverse_norm(u):
    return lax.rsqrt(jnp.mean(u * u, axis=-1, keepdims=True) + epsilon)


def norm_back(u, inverse, gain, upstream):
    scaled = upstream * gain
    inward = inverse * scaled - u * (inverse * inverse * inverse) * jnp.mean(
        u * scaled, axis=-1, keepdims=True
    )
    return inward, upstream * u * inverse


def rotate(u, cos, sin):
    return u * cos + pltpu.roll(u, HEAD // 2, 1) * sin


def unrotate(u, cos, sin):
    return u * cos - pltpu.roll(u, HEAD // 2, 1) * sin


def head_of(value, h):
    return value[:, h * HEAD : (h + 1) * HEAD]


def attention(x, gain, w_ref, cos, sin, allow, n_ref, qkv_ref, prob_ref, o_ref):
    n = (x * inverse_norm(x) * gain).astype(BF)
    n_ref[...] = n
    flat = dot(n, w_ref[:, 0:QKV])
    for h in range(HEADS + 1):
        qkv_ref[:, h * HEAD : (h + 1) * HEAD] = rotate(head_of(flat, h), cos, sin).astype(BF)
    qkv_ref[:, (HEADS + 1) * HEAD :] = flat[:, (HEADS + 1) * HEAD :].astype(BF)
    key = qkv_ref[:, HEADS * HEAD : (HEADS + 1) * HEAD]
    value = qkv_ref[:, (HEADS + 1) * HEAD :]
    for h in range(HEADS):
        scores = dot(qkv_ref[:, h * HEAD : (h + 1) * HEAD], key, 1, 1) * HEAD ** (-0.5)
        scores = jnp.where(allow > 0.0, scores, -1e30)
        weight = jnp.exp(scores - jnp.max(scores, axis=-1, keepdims=True))
        prob = weight / jnp.sum(weight, axis=-1, keepdims=True)
        prob_ref[h] = prob
        o_ref[:, h * HEAD : (h + 1) * HEAD] = dot(prob.astype(BF), value).astype(BF)
    return dot(o_ref[...], w_ref[:, QKV : QKV + OUT], 1, 1)


def expert_weight_copies(layer, r, local):
    core = lax.axis_index("blk")
    copies = []
    for name in ("gate", "up", "down"):
        held = getattr(r, "held_" + name)
        copies.append(local.start(getattr(r, name).at[layer, core], held.at[0]))
        copies.append(local.start(getattr(r, name + "_other").at[layer], held.at[1]))
    return copies


GROUP = SLOTS // 2


def expert_forward(group, rows, held, a_ref, b_ref):
    gate, up, down = held
    at = pl.ds(GROUP * group, GROUP)
    total = None
    for c in range(2):
        a = dot(rows, gate[c])
        b = dot(rows, up[c])
        a_ref[c, at] = a
        b_ref[c, at] = b
        z = (a / (1.0 + jnp.exp(-a)) * b).astype(BF)
        term = dot(z, down[c])
        total = term if total is None else total + term
    return total


def expert_backward(group, dy, held, a_ref, b_ref, z_ref, d_ref):
    gate, up, down = held
    at = pl.ds(GROUP * group, GROUP)
    total = None
    for c in range(2):
        a = a_ref[c, at]
        b = b_ref[c, at]
        sg = 1.0 / (1.0 + jnp.exp(-a))
        z_ref[at, c * HIDDEN : (c + 1) * HIDDEN] = (a * sg * b).astype(BF)
        dz = dot(dy, down[c], 1, 1)
        da = (dz * b * sg * (1.0 + a * (1.0 - sg))).astype(BF)
        db = (dz * a * sg).astype(BF)
        d_ref[at, 2 * c * HIDDEN : (2 * c + 1) * HIDDEN] = da
        d_ref[at, (2 * c + 1) * HIDDEN : (2 * c + 2) * HIDDEN] = db
        term = dot(da, gate[c], 1, 1) + dot(db, up[c], 1, 1)
        total = term if total is None else total + term
    return total


def expert_gradients(rows_ref, dy_ref, z_ref, d_ref, stage, grads, local, xyz, ready=None):
    sent = []
    for k, by in enumerate((2, 1, 3, 0)):
        quarter = shifted(xyz, 0, by)[0]
        columns = pl.ds(pl.multiple_of(quarter * HIDDEN, 128), HIDDEN)
        slot = k % 2
        if k >= 2:
            sent[k - 2].wait()
            if ready:
                ready(k - 2)
        both = dot(rows_ref[:, columns], d_ref[...], 0, 0)
        for c in range(2):
            for i in range(2):
                at = (2 * c + i) * HIDDEN
                stage[slot, 3 * c + i] = both[:, at : at + HIDDEN].astype(BF)
        low = dot(z_ref[...], dy_ref[:, columns], 0, 0)
        for c in range(2):
            stage[slot, 3 * c + 2] = low[c * HIDDEN : (c + 1) * HIDDEN].astype(BF)
        sent.append(local.start(stage.at[slot], grads.at[quarter]))
    for k in (2, 3):
        sent[k].wait()
        if ready and k == 2:
            ready(k)


def ring_devices(xyz, core, axis, steps=(1, 2, 3)):
    return [device_at(shifted(xyz, axis, by), core) for by in steps]


def arrive(copies):
    for copy in copies:
        copy.wait_recv()


class Gather:
    def __init__(self, sender, xyz, core):
        self.sender, self.xyz, self.core = sender, xyz, core

    def slab(self, job, stage, at, half=None):
        whole, lane, lanes, order = job
        index = list(at)
        for axis in order[:stage]:
            index[axis] = pl.ds(0, 4)
        if half is not None:
            index[order[0]] = pl.ds(2 * half, 2)
        return whole.at[index[0], index[1], index[2], :, pl.ds(lane, lanes)]

    def to(self, job, stage, by):
        return device_at(shifted(self.xyz, job[3][stage], by), self.core)

    def first(self, job, shard):
        source = shard.at[:, pl.ds(job[1], job[2])]
        target = self.slab(job, 0, self.xyz)
        return [self.sender.start(source, target, self.to(job, 0, by)) for by in (1, 3, 2)]

    def near(self, job, stage, steps=(1, 3)):
        block = self.slab(job, stage, self.xyz)
        return [self.sender.start(block, block, self.to(job, stage, by)) for by in steps]

    def relay(self, job, stage, near):
        copies = []
        for half, by in enumerate((1, 3)):
            near[half].wait_recv()
            at = shifted(self.xyz, job[3][stage], 4 - by)
            block = self.slab(job, stage, at, half)
            copies.append(self.sender.start(block, block, self.to(job, stage, by)))
        return copies

    def finish(self, near, relays):
        for copy in near:
            copy.wait_send()
        for copy in relays:
            copy.wait()


class ExpertSum:
    def __init__(self, r, layer, sender, local, xyz, core):
        self.r, self.sender, self.local, self.core = r, sender, local, core
        self.plus, self.minus = ring_devices(xyz, core, 0, (1, 3))
        self.grads, self.near, self.far, self.total = (
            getattr(r, f"{name}_{layer}") for name in ("grads", "near", "far", "total")
        )
        self.quarter = [shifted(xyz, 0, by)[0] for by in range(4)]

    def half(self, by, half):
        return self.grads.at[self.quarter[by], pl.ds(3 * half, 3)]

    def near_half(self, side, half):
        return self.near.at[side, pl.ds(3 * half, 3)]

    def send(self, part):
        go = self.sender.start
        if part == 0:
            self.passed = [
                go(self.half(2, 0), self.far.at[0], self.plus),
                go(self.half(2, 1), self.far.at[1], self.minus),
            ]
        elif part == 1:
            self.plain = [go(self.half(1, 1), self.near_half(0, 1), self.plus)]
        else:
            self.plain.append(go(self.half(3, 0), self.near_half(1, 0), self.minus))

    def start(self):
        for part in range(3):
            self.send(part)

    def relay(self):
        r, load = self.r, self.local.start
        own = [load(self.half(by, side), r.own.at[side]) for side, by in enumerate((1, 3))]
        came = []
        for side in range(2):
            self.passed[side].wait_recv()
            came.append(load(self.far.at[side], r.work.at[side]))
        for side, target in enumerate((self.plus, self.minus)):
            own[side].wait()
            came[side].wait()
            for i in range(3):
                value = r.own[side, i].astype(F32) + r.work[side, i].astype(F32)
                r.work[side, i] = value.astype(BF)
            self.plain.append(
                self.sender.start(r.work.at[side], self.near_half(side, side), target)
            )

    def finish(self):
        r, load = self.r, self.local.start
        for copy in self.plain:
            copy.wait()
        for copy in self.passed:
            copy.wait_send()

        def bring(i, slot):
            return [
                load(self.grads.at[self.quarter[0], i], r.own.at[slot, 0]),
                load(self.near.at[0, i], r.own.at[slot, 1]),
                load(self.near.at[1, i], r.own.at[slot, 2]),
            ]

        order, out = (3, 4, 5, 0, 1, 2), []
        loads = [bring(order[0], 0)]
        for k, i in enumerate(order):
            if k < 5:
                loads.append(bring(order[k + 1], (k + 1) % 2))
            for copy in loads[k]:
                copy.wait()
            slot = k % 2
            value = r.own[slot, 0].astype(F32) + r.own[slot, 1].astype(F32)
            r.ship[k] = (value + r.own[slot, 2].astype(F32)).astype(BF)
            to = self.total.at[self.core, i % 3]
            if k < 3:
                out.append(self.sender.start(r.ship.at[k], to, partner()))
            else:
                out.append(load(r.ship.at[k], to))
        for copy in out:
            copy.wait()


def tables(r):
    first = r.lengths[0, 0]
    second = first + r.lengths[0, 1]

    def place(index):
        segment = jnp.where(index >= first, 1, 0) + jnp.where(index >= second, 1, 0)
        start = jnp.where(segment == 0, 0, jnp.where(segment == 1, first, second))
        return segment, index - start

    shape = (TOKENS, TOKENS)
    lane = lax.broadcasted_iota(jnp.int32, shape, 1)
    row_segment, row_place = place(lax.broadcasted_iota(jnp.int32, shape, 0))
    key_segment, key_place = place(lane)
    allowed = (row_segment == key_segment) & (key_place <= row_place)
    r.allow[...] = jnp.where(allowed, 1.0, 0.0)
    half = jnp.where(lane < HEAD // 2, lane, lane - HEAD // 2).astype(F32)
    frequency = jnp.exp(half * (-2.0 / HEAD * math.log(rope_base)))
    angles = row_place.astype(F32) * frequency
    sign = jnp.where(lane < HEAD // 2, -1.0, 1.0)
    r.cos[...] = jnp.cos(angles)
    r.sin[...] = jnp.sin(angles) * sign


def assemble(r):
    square = (SHARD, SHARD)
    eye = lax.broadcasted_iota(jnp.int32, square, 0) == lax.broadcasted_iota(jnp.int32, square, 1)
    lane = lax.broadcasted_iota(jnp.int32, (SHARD, 128), 1)
    for l in range(LAYERS):
        r.shard[l, :, 0:768] = r.query[l]
        r.shard[l, :, 768:896] = r.key[l]
        r.shard[l, :, 896:QKV] = r.value[l]
        r.shard[l, :, QKV : QKV + OUT] = r.out[l]
        column = jnp.zeros((SHARD, 128), F32)
        for i, gain in enumerate((r.gain_a, r.gain_e)):
            spread = jnp.broadcast_to(gain[l : l + 1, :].astype(F32), square)
            spread = jnp.where(eye, spread, 0.0).astype(BF)
            column = column + dot(spread, jnp.where(lane == i, 1.0, 0.0).astype(BF))
        r.shard[l, :, QKV + OUT :] = column.astype(BF)


KEPT = dict(
    h=((TOKENS, WIDE), F32),
    n=((TOKENS, WIDE), BF),
    qkv=((TOKENS, QKV), BF),
    prob=((HEADS, TOKENS, TOKENS), F32),
    o=((TOKENS, OUT), BF),
    onehot=((SLOTS, TOKENS), BF),
    weighted=((SLOTS, TOKENS), F32),
)
KEPT_SPACE = {name: pltpu.VMEM(*spec) for name, spec in KEPT.items()}
HELD = dict(
    held_gate=pltpu.VMEM((2, WIDE, HIDDEN), BF),
    held_up=pltpu.VMEM((2, WIDE, HIDDEN), BF),
    held_down=pltpu.VMEM((2, HIDDEN, WIDE), BF),
)
ROWS = ((SLOTS, WIDE), BF)
INNER = ((2, SLOTS, HIDDEN), F32)
BLOCKS = ((PEERS, CAP, WIDE), BF)
PLANE = ((TOKENS, WIDE), F32)
FLAT = ((TOKENS, WIDE), BF)
GRADS = ((4, 6, HIDDEN, HIDDEN), BF)
BACKWARD = dict(
    z=pltpu.VMEM((SLOTS, 2 * HIDDEN), BF),
    d=pltpu.VMEM((SLOTS, 4 * HIDDEN), BF),
    dy=pltpu.VMEM(*ROWS),
    stage=pltpu.VMEM((2, 6, HIDDEN, HIDDEN), BF),
)


def sems(**counts):
    return {name: pltpu.SemaphoreType.DMA((n,)) for name, n in counts.items()}


def spaces(**specs):
    return {name: pltpu.VMEM(*spec) for name, spec in specs.items()}


def attend(r, l, x, pair, local, then=None):
    gain_a, gain_e = gain_rows(r.w)
    r.part0[...] = attention(
        x, gain_a, r.w, r.cos[...], r.sin[...], r.allow[...], r.n, r.qkv, r.prob, r.o
    ).astype(BF)
    copy = pair.start(r.part0, r.theirs0, partner())
    for name in ("n", "qkv", "prob", "o"):
        local.keep(getattr(r, name), getattr(r, f"{name}_{l}"))
    begun = then() if then else None
    copy.wait_recv()
    h = x + (r.part0[...].astype(F32) + r.theirs0[...].astype(F32))
    copy.wait_send()
    r.h[...] = h
    local.keep(r.h, getattr(r, f"h_{l}"))
    return (h * inverse_norm(h) * gain_e).astype(BF), begun


def front_body(r):
    xyz, core = coords(), lax.axis_index("blk")
    local, pair = Local(r.local), Sender(r.pair_send, r.pair_recv)
    sender = Sender(r.wide_send, r.wide_recv)
    gather = Gather(sender, xyz, core)
    held = (r.held_gate, r.held_up, r.held_down)
    count = hail(peers() + ring_devices(xyz, core, 0))
    mine = pl.ds(pl.multiple_of(core * HALF, HALF), HALF)
    here = [
        local.start(r.tok, r.tokens.at[:, mine]),
        local.start(r.cot_half, r.cot.at[:, mine]),
    ]
    assemble(r)
    here.append(local.start(r.shard.at[0], r.cube.at[xyz[0], xyz[1], xyz[2]]))
    here_later = local.start(r.shard.at[1], r.later.at[xyz[0], xyz[1], xyz[2]])
    heard(count)
    now = [(r.cube, p * PART, PART, order) for p, order in enumerate(ORDERS)]
    first = [c for job in now for c in gather.first(job, r.shard.at[0])]
    halves_sent = [
        sender.start(r.tok, r.tokens.at[:, mine], partner()),
        sender.start(r.cot_half, r.cot.at[:, mine], partner()),
    ]
    swaps = [[], []]
    for l in range(LAYERS):
        for name in ("gate", "up", "down"):
            ref = getattr(r, name).at[l, 1 - core]
            swaps[l].append(sender.start(ref, getattr(r, name + "_other").at[l], partner()))
    tables(r)
    for l, (onehot, weighted) in enumerate(((r.onehot_0, r.weighted_0), (r.onehot_1, r.weighted_1))):
        hot, heavy = slot_matrices(r.ids[l], r.weights[l])
        onehot[...] = hot.astype(BF)
        weighted[...] = heavy
    for copy in here:
        copy.wait()
    arrive(first)
    near = [gather.near(job, 1, (1, 3, 2)) for job in now]

    def onward(job, at):
        block = gather.slab(job, 1, at)
        return at, [sender.start(block, block, gather.to(job, 2, by)) for by in (1, 3)]

    last = [[onward(job, xyz)] for job in now]
    arrive(halves_sent)
    slot_weight = jnp.sum(r.weighted_1[...], axis=1, keepdims=True)
    store_rows(r.sent_g, dot(r.onehot_1[...], r.cot[...]) * slot_weight)
    for n, by in enumerate((1, 3, 2)):
        for p, job in enumerate(now):
            near[p][n].wait_recv()
            last[p].append(onward(job, shifted(xyz, job[3][1], 4 - by)))
    relays = []
    for m in range(4):
        for p, job in enumerate(now):
            at, copies = last[p][m]
            for half, by in enumerate((1, 3)):
                copies[half].wait_recv()
                block = gather.slab(job, 1, shifted(at, job[3][2], 4 - by), half)
                relays.append(sender.start(block, block, gather.to(job, 2, by)))
    arrive(swaps[0])
    loads = expert_weight_copies(0, r, local)
    arrive(relays)
    jobs = [(r.later, *job) for job in LATER]
    first_later = [c for job in jobs for c in gather.first(job, r.shard.at[1])]
    r.w[...] = r.cube[...].astype(F32).reshape(WIDE, COLS).astype(BF)
    w_kept = local.start(r.w, r.w_0)

    def second():
        here_later.wait()
        arrive(first_later)
        return [c for job in jobs for c in gather.near(job, 1, (1, 3, 2))]

    m, near_later = attend(r, 0, r.tokens[...].astype(F32), pair, local, second)
    store_rows(r.sent, dot(r.onehot_0[...], m))
    out0 = Exchange(r, 0, r.sent, r.came, False)
    out0.start()
    arrive(near_later)
    last_later = [gather.near(job, 2) for job in jobs]
    relays_later = {}
    for copy in loads:
        copy.wait()
    back0 = Exchange(r, 1, r.turn, r.back, True)
    for g in range(2):
        out0.arrive(g)
        at = pl.ds(GROUP * g, GROUP)
        r.rows[at] = rows_of(group_of(r.came, g))
        store_rows(group_of(r.turn, g), expert_forward(g, r.rows[at], held, r.a, r.b))
        back0.start(g)
    rows_kept = [local.start(r.rows, r.rows_0), local.start(r.a, r.a_0), local.start(r.b, r.b_0)]
    out0.sent()
    arrive(swaps[1])
    loads = expert_weight_copies(1, r, local)
    for i in range(4):
        relays_later[i] = gather.relay(jobs[i], 2, last_later[i])
    back0.arrive()
    out_g = Exchange(r, 3, r.sent_g, r.came_g, False)
    out_g.start()
    r.part1[...] = combine(r.weighted_0[...], rows_of(r.back)).astype(BF)
    copy = pair.start(r.part1, r.theirs1, partner())
    w_kept.wait()
    local.wait_kept()
    local.kept = []
    copy.wait_recv()
    x = r.h[...] + (r.part1[...].astype(F32) + r.theirs1[...].astype(F32))
    r.stream[...] = x
    copy.wait_send()
    for i in range(4):
        arrive(relays_later[i])
    for copy in relays + [c for n in near for c in n] + [c for n in last for _, two in n for c in two]:
        copy.wait_send()
    load = local.start(r.later, r.cube)
    load.wait()
    r.w[...] = r.cube[...].astype(F32).reshape(WIDE, COLS).astype(BF)
    local.keep(r.w, r.w_1)
    m, _ = attend(r, 1, x, pair, local)
    store_rows(r.sent, dot(r.onehot_1[...], m))
    out1 = Exchange(r, 2, r.sent, r.came, False)
    out1.start()
    back0.sent()
    out_g.arrive()
    r.dy[...] = rows_of(r.came_g)
    for copy in loads + rows_kept:
        copy.wait()
    for g in range(2):
        out1.arrive(g)
        at = pl.ds(GROUP * g, GROUP)
        r.rows[at] = rows_of(group_of(r.came, g))
        store_rows(group_of(r.back, g), expert_forward(g, r.rows[at], held, r.a, r.b))
        result = expert_backward(g, r.dy[at], held, r.a, r.b, r.z, r.d)
        store_rows(group_of(r.turn, g), result)
    local.keep(r.back, r.y_1)
    local.keep(r.turn, r.m_1)
    expert_gradients(r.rows, r.dy, r.z, r.d, r.stage, r.grads_1, local, xyz)
    out1.sent()
    out_g.sent()
    for copy in first + first_later + near_later + halves_sent + swaps[0] + swaps[1]:
        copy.wait_send()
    for i in range(4):
        for copy in last_later[i] + relays_later[i]:
            copy.wait_send()
    local.wait_kept()


def turned(value):
    return value.astype(F32).T.reshape(4, 4, 4, SHARD, TOKENS).astype(BF)


def own_part(ref, axis, index):
    return ref.at[:, index] if axis == 1 else ref.at[:, :, index]


def share_factor(ref, into, axis, sender, xyz, core):
    copies = []
    for by in (1, 3, 2):
        there = shifted(xyz, axis, by)
        copies.append(
            sender.start(own_part(ref, axis, there[axis]), into.at[by - 1], device_at(there, core))
        )
    return copies


def share_whole(ref, axis, sender, xyz, core):
    return [
        sender.start(
            ref.at[pl.ds(0, TOKENS)],
            ref.at[pl.ds(by * TOKENS, TOKENS)],
            device_at(shifted(xyz, axis, by), core),
        )
        for by in (1, 3, 2)
    ]


def quarter_sum(own, came, axis, xyz, right):
    first = own_part(own, axis, xyz[axis])[...]
    pieces = [first] + [came[i] for i in range(3)]
    left = [p.astype(F32).reshape(HIDDEN, TOKENS).astype(BF) for p in pieces]
    return dot(jnp.concatenate(left, axis=1), right[...])


def back_body(r):
    xyz, core = coords(), lax.axis_index("blk")
    local, pair = Local(r.local), Sender(r.pair_send, r.pair_recv)
    sender = Sender(r.wide_send, r.wide_recv)

    def load_layer(l):
        names = ("w", "h", "qkv", "prob", "o")
        return [local.start(getattr(r, f"{name}_{l}"), getattr(r, name)) for name in names]

    loads = load_layer(1)
    count = hail(peers() + ring_devices(xyz, core, 0))
    sums = [ExpertSum(r, l, sender, local, xyz, core) for l in range(LAYERS)]
    heard(count)
    came_m, onehot = (r.came_0, r.came_1), (r.onehot_0, r.onehot_1)
    back = [Exchange(r, 2, r.turn, r.came_0, True), Exchange(r, 0, r.m_1, r.came_1, True)]
    out_g = Exchange(r, 1, r.sent, r.came_g, False)
    y_back = Exchange(r, 3, r.y_1, r.came_1, True)
    back[1].start()
    sums[1].start()
    weights = expert_weight_copies(0, r, local)
    weights += [local.start(getattr(r, name + "_0"), getattr(r, name)) for name in ("rows", "a", "b")]
    r.n_turned[1] = turned(r.n_1[...])
    r.n_turned[0] = turned(r.n_0[...])
    for copy in loads:
        copy.wait()
    shared = [[], []]
    scale = HEAD ** (-0.5)
    row = lax.broadcasted_iota(jnp.int32, (8, WIDE), 0)
    r.gain_sum[1] = jnp.zeros((8, WIDE), F32)
    inner, across = [None] * 2, [None] * 2
    for l in (1, 0):
        x = (r.stream if l == 1 else r.tokens)[...].astype(F32)
        gain_a, gain_e = gain_rows(r.w)
        r.o_all[l, 0:TOKENS] = r.o[...]
        back[l].arrive()
        r.part[0] = dot(onehot[l][...], rows_of(came_m[l]), 0, 0)
        inner[l] = pair.start(r.part.at[0], r.theirs.at[l, 0], partner())
        if l == 1:
            for i in (1, 0):
                shared[i] += share_factor(r.n_turned.at[i], r.n_came.at[i], 1, sender, xyz, core)
        shared[l] += share_whole(r.o_all.at[l], 2, sender, xyz, core)
        inner[l].wait_recv()
        dm = r.part[0] + r.theirs[l, 0]
        hidden = r.h[...]
        inward, gain_grad_e = norm_back(hidden, inverse_norm(hidden), gain_e, dm)
        gh = (r.cot[...].astype(F32) if l == 1 else r.flow[...]) + inward
        r.flow[...] = gh
        da = gh.astype(BF)
        r.da_turned[l] = turned(gh)
        shared[l] += share_factor(r.da_turned.at[l], r.da_came.at[l], 2, sender, xyz, core)
        do = dot(da, r.w[:, QKV : QKV + OUT]).astype(BF)
        key = r.qkv[:, HEADS * HEAD : (HEADS + 1) * HEAD]
        value = r.qkv[:, (HEADS + 1) * HEAD :]
        key_grad, value_grad = None, None
        cosine, sine = r.cos[...], r.sin[...]
        lin = r.lin_all.at[l]
        for i in range(HEADS):
            prob_i = r.prob[i]
            do_i = head_of(do, i)
            q_i = r.qkv[:, i * HEAD : (i + 1) * HEAD]
            dprob = dot(do_i, value, 1, 1)
            centre = jnp.sum(prob_i * dprob, axis=-1, keepdims=True)
            ds = (prob_i * (dprob - centre)).astype(BF)
            dq = dot(ds, key) * scale
            lin[0:TOKENS, i * HEAD : (i + 1) * HEAD] = unrotate(dq, cosine, sine).astype(BF)
            dk = dot(ds, q_i, 0, 0)
            dv = dot(prob_i.astype(BF), do_i, 0, 0)
            key_grad = dk if key_grad is None else key_grad + dk
            value_grad = dv if value_grad is None else value_grad + dv
        lin[0:TOKENS, HEADS * HEAD : (HEADS + 1) * HEAD] = unrotate(
            key_grad * scale, cosine, sine
        ).astype(BF)
        lin[0:TOKENS, (HEADS + 1) * HEAD :] = value_grad.astype(BF)
        r.part[1] = dot(lin[0:TOKENS, :], r.w[:, 0:QKV], 1, 1)
        across[l] = pair.start(r.part.at[1], r.theirs.at[l, 1], partner())
        if l == 1:
            r.kept_half[...] = jnp.where(core == 1, r.h[:, HALF:], r.h[:, :HALF])
            loads = load_layer(0)
        else:
            shared[0] += share_whole(r.lin_all.at[0], 1, sender, xyz, core)
            sums[0].relay()
        across[l].wait_recv()
        dn = r.part[1] + r.theirs[l, 1]
        inward, gain_grad_a = norm_back(x, inverse_norm(x), gain_a, dn)
        flow = r.flow[...] + inward
        gains = r.gain_sum[1]
        for i, grad in enumerate((gain_grad_a, gain_grad_e)):
            grad = jnp.sum(grad, axis=0, keepdims=True)
            gains = jnp.where(row == 2 * l + i, jnp.broadcast_to(grad, (8, WIDE)), gains)
        r.gain_sum[1] = gains
        inner[l].wait_send()
        across[l].wait_send()
        if l == 0:
            r.tokens_grad[...] = jnp.where(core == 1, flow[:, HALF:], flow[:, :HALF])
            continue
        r.flow[...] = flow
        slot_weight = jnp.sum(r.weighted_0[...], axis=1, keepdims=True)
        high, low = halves(flow)
        hot = r.onehot_0[...]
        store_rows(r.sent, (dot(hot, high) + dot(hot, low)) * slot_weight)
        out_g.start()
        sums[1].relay()
        for copy in weights:
            copy.wait()
        held = (r.held_gate, r.held_up, r.held_down)
        for g in range(2):
            out_g.arrive(g)
            at = pl.ds(GROUP * g, GROUP)
            r.dy[at] = rows_of(group_of(r.came_g, g))
            result = expert_backward(g, r.dy[at], held, r.a, r.b, r.z, r.d)
            store_rows(group_of(r.turn, g), result)
            back[0].start(g)
        shared[1] += share_whole(r.lin_all.at[1], 1, sender, xyz, core)
        expert_gradients(
            r.rows, r.dy, r.z, r.d, r.stage, r.grads_0, local, xyz, sums[0].send
        )
        sums[1].finish()
        for copy in loads:
            copy.wait()
    last_sums = finish_sums(r, shared, y_back, sender, xyz, core)
    y_back.arrive()
    mixed = combine(r.weighted_1[...], rows_of(r.came_1))
    r.half[...] = jnp.where(core == 1, mixed[:, :HALF], mixed[:, HALF:])
    third = pair.start(r.half, r.half_theirs, partner())
    own = jnp.where(core == 1, mixed[:, HALF:], mixed[:, :HALF])
    third.wait()
    r.block_out[...] = (r.kept_half[...] + (own + r.half_theirs[...])).astype(BF)
    sums[0].finish()
    last_sums()
    for exchange in (*back, out_g, y_back):
        exchange.sent()


def late_start(r, l, sender, xyz, core):
    copies = []
    for ref, came, axis in ((r.sum_a, r.near_a, 2), (r.sum_b, r.near_b, 1)):
        for by in (1, 3, 2):
            there = shifted(xyz, axis, by)
            copies.append(
                sender.start(ref.at[l, :, there[axis]], came.at[l, by - 1], device_at(there, core))
            )
    return copies


def late_middle(r, l, sender, xyz, core, copies):
    arrive(copies)
    for ref, came, axis, lanes in (
        (r.sum_a, r.near_a, 2, slice(0, QKV)),
        (r.sum_b, r.near_b, 1, slice(QKV, QKV + OUT)),
    ):
        total = ref[l, :, xyz[axis]].astype(F32)
        for i in range(3):
            total = total + came[l, i].astype(F32)
        r.line[l, :, :, lanes] = total.astype(BF)
    copies = []
    for by in (1, 3, 2):
        there = shifted(xyz, 0, by)
        copies.append(
            sender.start(r.line.at[l, there[0]], r.line_came.at[l, by - 1], device_at(there, core))
        )
    return copies


def late_end(r, l, xyz, copies):
    for copy in copies:
        copy.wait()
    total = r.line[l, xyz[0]].astype(F32)
    for i in range(3):
        total = total + r.line_came[l, i].astype(F32)
    r.weight_grad[l] = total


def gains_along(r, axis, sender, xyz, core):
    copies = []
    for by in (1, 3, 2):
        there = shifted(xyz, axis, by)
        if axis == 0:
            quarter = pl.ds(pl.multiple_of(there[0] * HIDDEN, 128), HIDDEN)
            src, dst = r.gain_sum.at[0, :, quarter], r.gain_last.at[by - 1]
        else:
            src, dst = r.gain_sum.at[axis], r.gain_came.at[axis - 1, by - 1]
        copies.append(sender.start(src, dst, device_at(there, core)))
    return copies


def gains_next(r, axis, xyz, copies):
    for copy in copies:
        copy.wait()
    if axis == 0:
        total = r.gain_sum[0, :, pl.ds(pl.multiple_of(xyz[0] * HIDDEN, 128), HIDDEN)]
        for i in range(3):
            total = total + r.gain_last[i]
        return total
    total = r.gain_sum[axis]
    for i in range(3):
        total = total + r.gain_came[axis - 1, i]
    return total


def finish_sums(r, shared, y_back, sender, xyz, core):
    def quarter(l):
        arrive(shared[l])
        wide = (4, 4, SHARD, QKV)
        total = quarter_sum(r.n_turned.at[l], r.n_came.at[l], 1, xyz, r.lin_all.at[l])
        r.sum_a[l] = total.reshape(wide).astype(BF)
        wide = (4, 4, SHARD, OUT)
        total = quarter_sum(r.da_turned.at[l], r.da_came.at[l], 2, xyz, r.o_all.at[l])
        r.sum_b[l] = total.reshape(wide).astype(BF)
        return late_start(r, l, sender, xyz, core)

    along = gains_along(r, 1, sender, xyz, core)
    above = quarter(1)
    r.gain_sum[2] = gains_next(r, 1, xyz, along)
    along = gains_along(r, 2, sender, xyz, core)
    above_last = late_middle(r, 1, sender, xyz, core, above)
    y_back.start()
    r.gain_sum[0] = gains_next(r, 2, xyz, along)
    along = gains_along(r, 0, sender, xyz, core)
    lower = quarter(0)
    lower_last = late_middle(r, 0, sender, xyz, core, lower)

    def end():
        late_end(r, 1, xyz, above_last)
        r.gain_total[...] = gains_next(r, 0, xyz, along)
        late_end(r, 0, xyz, lower_last)
        for copy in shared[0] + shared[1] + above + lower:
            copy.wait_send()

    return end


def finish_body(r):
    local = Local(r.local)
    loads = [
        [local.start(total.at[:, i], r.narrow.at[l, i]) for i in range(3)]
        for l, total in enumerate((r.total_below, r.total_above))
    ]
    r.block_out[...] = r.block_in[...]
    r.tokens_grad[...] = r.tokens_in[...]
    place = lax.axis_index("expert") * SHARD
    near = pltpu.roll(r.gain_total[...], lax.rem(HIDDEN - place, HIDDEN), 1)
    for l in range(LAYERS):
        r.gain_a[l : l + 1, :] = near[2 * l : 2 * l + 1, :SHARD]
        r.gain_e[l : l + 1, :] = near[2 * l + 1 : 2 * l + 2, :SHARD]
        r.query[l] = r.weight_grad[l, :, :768]
        r.key[l] = r.weight_grad[l, :, 768:896]
        r.value[l] = r.weight_grad[l, :, 896:QKV]
        r.out[l] = r.weight_grad[l, :, QKV:]
    for l in range(LAYERS):
        for i, out in enumerate((r.gate, r.up, r.down)):
            loads[l][i].wait()
            r.broad[l, i] = r.narrow[l, i].astype(F32)
            local.keep(r.broad.at[l, i], out.at[l])
    local.wait_kept()


def kernel_call(body, name, cid, ins, outs, scratch, aliases=()):
    names = [*ins, *outs, *scratch]
    assert len(set(names)) == len(names)

    def kernel(*refs):
        body(types.SimpleNamespace(**dict(zip(names, refs))))

    results = pl.pallas_call(
        kernel,
        out_shape=[jax.ShapeDtypeStruct(shape, kind) for shape, kind, _ in outs.values()],
        in_specs=[space for _, space in ins.values()],
        out_specs=[space for _, _, space in outs.values()],
        scratch_shapes=list(scratch.values()),
        input_output_aliases={list(ins).index(a): list(outs).index(b) for a, b in aliases},
        compiler_params=pltpu.CompilerParams(
            collective_id=cid, has_side_effects=cid is not None, vmem_limit_bytes=LIMIT
        ),
        name=name,
    )(*[array for array, _ in ins.values()])
    return types.SimpleNamespace(**dict(zip(outs, results)))


def per_device(
    tokens_in,
    seq_lengths,
    expert_ids,
    gate_weights,
    attention_gain,
    query_weight,
    key_weight,
    value_weight,
    out_weight,
    expert_gain,
    gate_weight,
    up_weight,
    down_weight,
    cotangent,
):
    cube = (4, 4, 4, SHARD, COLS)
    own = dict(gate=(gate_weight, ANY), up=(up_weight, ANY), down=(down_weight, ANY))
    exchanges = sems(
        **{f"{way}{i}": PEERS for way in ("send", "recv") for i in range(4)}, pair_send=5, pair_recv=5
    )
    kept = ("h", "n", "qkv", "prob", "o")
    w_space = dict(w=pltpu.VMEM((WIDE, COLS), BF))
    start = kernel_call(
        front_body,
        "front",
        1,
        dict(
            lengths=(seq_lengths, SMEM),
            query=(query_weight, VMEM),
            key=(key_weight, VMEM),
            value=(value_weight, VMEM),
            out=(jnp.swapaxes(out_weight, 1, 2), VMEM),
            gain_a=(attention_gain, VMEM),
            gain_e=(expert_gain, VMEM),
            tok=(tokens_in, VMEM),
            cot_half=(cotangent, VMEM),
            ids=(jnp.swapaxes(expert_ids, 1, 2), VMEM),
            weights=(jnp.swapaxes(gate_weights, 1, 2), VMEM),
            **own,
        ),
        dict(
            w_0=((WIDE, COLS), BF, ANY),
            w_1=((WIDE, COLS), BF, ANY),
            later=(cube, BF, ANY),
            tokens=((TOKENS, WIDE), BF, VMEM),
            cot=((TOKENS, WIDE), BF, VMEM),
            stream=(*PLANE, VMEM),
            cos=((TOKENS, HEAD), F32, VMEM),
            sin=((TOKENS, HEAD), F32, VMEM),
            gate_other=((LAYERS, WIDE, HIDDEN), BF, ANY),
            up_other=((LAYERS, WIDE, HIDDEN), BF, ANY),
            down_other=((LAYERS, HIDDEN, WIDE), BF, ANY),
            rows_0=(*ROWS, ANY),
            a_0=(*INNER, ANY),
            b_0=(*INNER, ANY),
            y_1=(*BLOCKS, ANY),
            m_1=(*BLOCKS, ANY),
            grads_1=(*GRADS, ANY),
            **{f"{name}_{l}": (*KEPT[name], ANY) for l in range(LAYERS) for name in kept},
            **{
                f"{name}_{l}": (*KEPT[name], VMEM)
                for l in range(LAYERS)
                for name in ("onehot", "weighted")
            },
        ),
        dict(
            shard=pltpu.VMEM((LAYERS, SHARD, COLS), BF),
            cube=pltpu.VMEM(cube, BF),
            allow=pltpu.VMEM((TOKENS, TOKENS), F32),
            **w_space,
            **{name: KEPT_SPACE[name] for name in kept},
            **HELD,
            **BACKWARD,
            **spaces(sent=BLOCKS, came=BLOCKS, back=BLOCKS, sent_g=BLOCKS, came_g=BLOCKS),
            **spaces(turn=BLOCKS, rows=ROWS, a=INNER, b=INNER),
            **spaces(part0=FLAT, theirs0=FLAT, part1=FLAT, theirs1=FLAT),
            **exchanges,
            **sems(wide_send=114, wide_recv=114, local=50),
        ),
    )
    experts = dict(
        own,
        gate_other=(start.gate_other, ANY),
        up_other=(start.up_other, ANY),
        down_other=(start.down_other, ANY),
    )
    part_a, part_b = (4, 4, SHARD, QKV), (4, 4, SHARD, OUT)
    total = ((2, 3, HIDDEN, HIDDEN), BF, ANY)
    near, far = ((2, 6, HIDDEN, HIDDEN), BF, ANY), ((2, 3, HIDDEN, HIDDEN), BF, ANY)
    factor, quarter = (4, 4, 4, SHARD, TOKENS), (3, 4, 4, SHARD, TOKENS)
    by_layer = {}
    for l in range(LAYERS):
        for name in ("h", "qkv", "prob", "o", "w"):
            by_layer[f"{name}_{l}"] = (getattr(start, f"{name}_{l}"), ANY)
        for name in ("n", "onehot", "weighted"):
            by_layer[f"{name}_{l}"] = (getattr(start, f"{name}_{l}"), VMEM)
    end = kernel_call(
        back_body,
        "backward",
        4,
        dict(
            stream=(start.stream, VMEM),
            tokens=(start.tokens, VMEM),
            cot=(start.cot, VMEM),
            cos=(start.cos, VMEM),
            sin=(start.sin, VMEM),
            **by_layer,
            **{
                name: (getattr(start, name), ANY)
                for name in ("m_1", "y_1", "grads_1", "rows_0", "a_0", "b_0")
            },
            **experts,
        ),
        dict(
            block_out=((TOKENS, HALF), BF, VMEM),
            tokens_grad=((TOKENS, HALF), F32, VMEM),
            weight_grad=((LAYERS, SHARD, QKV + OUT), F32, VMEM),
            gain_total=((8, HIDDEN), F32, VMEM),
            total_0=total,
            total_1=total,
            grads_0=(*GRADS, ANY),
            near_0=near,
            near_1=near,
            far_0=far,
            far_1=far,
        ),
        dict(
            **w_space,
            **HELD,
            **BACKWARD,
            **{name: KEPT_SPACE[name] for name in ("h", "qkv", "prob", "o")},
            **spaces(rows=ROWS, a=INNER, b=INNER, flow=PLANE),
            **spaces(sent=BLOCKS, turn=BLOCKS),
            **spaces(came_0=BLOCKS, came_1=BLOCKS, came_g=BLOCKS),
            part=pltpu.VMEM((2, TOKENS, WIDE), F32),
            theirs=pltpu.VMEM((LAYERS, 2, TOKENS, WIDE), F32),
            half=pltpu.VMEM((TOKENS, HALF), F32),
            half_theirs=pltpu.VMEM((TOKENS, HALF), F32),
            kept_half=pltpu.VMEM((TOKENS, HALF), F32),
            own=pltpu.VMEM((2, 3, HIDDEN, HIDDEN), BF),
            work=pltpu.VMEM((2, 3, HIDDEN, HIDDEN), BF),
            ship=pltpu.VMEM((6, HIDDEN, HIDDEN), BF),
            n_turned=pltpu.VMEM((LAYERS, *factor), BF),
            da_turned=pltpu.VMEM((LAYERS, *factor), BF),
            n_came=pltpu.VMEM((LAYERS, *quarter), BF),
            da_came=pltpu.VMEM((LAYERS, *quarter), BF),
            lin_all=pltpu.VMEM((LAYERS, 4 * TOKENS, QKV), BF),
            o_all=pltpu.VMEM((LAYERS, 4 * TOKENS, OUT), BF),
            sum_a=pltpu.VMEM((LAYERS, *part_a), BF),
            sum_b=pltpu.VMEM((LAYERS, *part_b), BF),
            near_a=pltpu.VMEM((LAYERS, 3, 4, SHARD, QKV), BF),
            near_b=pltpu.VMEM((LAYERS, 3, 4, SHARD, OUT), BF),
            line=pltpu.VMEM((LAYERS, 4, SHARD, QKV + OUT), BF),
            line_came=pltpu.VMEM((LAYERS, 3, SHARD, QKV + OUT), BF),
            gain_sum=pltpu.VMEM((3, 8, WIDE), F32),
            gain_came=pltpu.VMEM((2, 3, 8, WIDE), F32),
            gain_last=pltpu.VMEM((3, 8, HIDDEN), F32),
            **exchanges,
            **sems(wide_send=72, wide_recv=72, local=84),
        ),
    )
    expert_out = ((LAYERS, 2, HIDDEN, HIDDEN), F32, ANY)
    out = kernel_call(
        finish_body,
        "finish",
        None,
        dict(
            block_in=(end.block_out, VMEM),
            tokens_in=(end.tokens_grad, VMEM),
            total_above=(end.total_1, ANY),
            total_below=(end.total_0, ANY),
            weight_grad=(end.weight_grad, VMEM),
            gain_total=(end.gain_total, VMEM),
        ),
        dict(
            block_out=((TOKENS, HALF), BF, VMEM),
            tokens_grad=((TOKENS, HALF), F32, VMEM),
            gain_a=((LAYERS, SHARD), F32, VMEM),
            query=((LAYERS, SHARD, 768), F32, VMEM),
            key=((LAYERS, SHARD, 128), F32, VMEM),
            value=((LAYERS, SHARD, 128), F32, VMEM),
            out=((LAYERS, SHARD, OUT), F32, VMEM),
            gain_e=((LAYERS, SHARD), F32, VMEM),
            gate=expert_out,
            up=expert_out,
            down=expert_out,
        ),
        dict(
            narrow=pltpu.VMEM((LAYERS, 3, 2, HIDDEN, HIDDEN), BF),
            broad=pltpu.VMEM((LAYERS, 3, 2, HIDDEN, HIDDEN), F32),
            **sems(local=14),
        ),
    )
    return (
        out.block_out,
        out.tokens_grad,
        out.gain_a,
        out.query,
        out.key,
        out.value,
        jnp.swapaxes(out.out, 1, 2),
        out.gain_e,
        out.gate,
        out.up,
        out.down,
    )


def solution(mesh):
    placed = (
        P(("dp", "expert"), "blk"),
        P(("dp", "expert"), None),
        P(None, ("dp", "expert"), None),
        P(None, ("dp", "expert"), None),
        P(None, ("dp", "expert")),
        P(None, ("dp", "expert"), "blk"),
        P(None, ("dp", "expert"), "blk"),
        P(None, ("dp", "expert"), "blk"),
        P(None, "blk", ("dp", "expert")),
        P(None, ("dp", "expert")),
        P(None, "expert", None, "blk"),
        P(None, "expert", None, "blk"),
        P(None, "expert", "blk", None),
        P(("dp", "expert"), "blk"),
    )
    return jax.shard_map(
        per_device,
        mesh=mesh,
        in_specs=placed,
        out_specs=(
            P(("dp", "expert"), "blk"),
            P(("dp", "expert"), "blk"),
            P(None, ("dp", "expert")),
            P(None, ("dp", "expert"), "blk"),
            P(None, ("dp", "expert"), "blk"),
            P(None, ("dp", "expert"), "blk"),
            P(None, "blk", ("dp", "expert")),
            P(None, ("dp", "expert")),
            P(None, "expert", "dp", "blk"),
            P(None, "expert", "dp", "blk"),
            P(None, "expert", "blk", "dp"),
        ),
        check_vma=False,
    )
```

```python
import functools
import math
import types

import jax
import jax.numpy as jnp
from jax import lax
from jax.experimental import pallas as pl
from jax.experimental.pallas import tpu as pltpu
from jax.sharding import PartitionSpec as P

HEAD = 128
TOP = 4
LAYERS = 2
F32 = jnp.float32
BF = jnp.bfloat16
MESH = pl.DeviceIdType.MESH

epsilon = 1e-06
rope_base = 1000000.0

TOKENS = 128
WIDE = 1536
HALF = WIDE // 2
HEADS = 6
HIDDEN = 384
PEERS = 16
CAP = 24
SLOTS = PEERS * CAP
SHARD = 24
QKV = 1024
OUT = 768
COLS = QKV + OUT + 128
PART = COLS // 3
ORDERS = ((0, 1, 2), (1, 2, 0), (2, 0, 1))
LIMIT = 60 << 20
LATER = ((0, 896, (1, 2, 0)), (896, 896, (2, 1, 0)), (1792, 128, (0, 1, 2)))

ANY = pl.BlockSpec(memory_space=pl.ANY)
VMEM = pl.BlockSpec(memory_space=pltpu.VMEM)
SMEM = pl.BlockSpec(memory_space=pltpu.SMEM)


def dot(a, b, ca=1, cb=0):
    return lax.dot_general(a, b, (((ca,), (cb,)), ((), ())), preferred_element_type=F32)


def coords():
    ex = lax.axis_index("expert")
    return [lax.axis_index("dp"), lax.div(ex, 4), lax.rem(ex, 4)]


def shifted(xyz, axis, by):
    moved = list(xyz)
    moved[axis] = lax.rem(xyz[axis] + by, 4)
    return moved


def device_at(xyz, core):
    return (xyz[0], xyz[1] * 4 + xyz[2], core)


def partner():
    return (lax.axis_index("dp"), lax.axis_index("expert"), 1 - lax.axis_index("blk"))


def hail(devices):
    barrier = pltpu.get_barrier_semaphore()
    for device in devices:
        pl.semaphore_signal(barrier, inc=1, device_id=device, device_id_type=MESH)
    return len(devices)


def heard(count):
    pl.semaphore_wait(pltpu.get_barrier_semaphore(), count)


def peer(step):
    dp, ex, core = (lax.axis_index(a) for a in ("dp", "expert", "blk"))
    return (dp, lax.rem(ex + step, PEERS), core)


def peers():
    return [peer(d) for d in range(1, PEERS)] + [partner()]


class Local:
    def __init__(self, sem):
        self.sem, self.at, self.kept = sem, 0, []

    def start(self, src, dst):
        assert self.at < self.sem.shape[0]
        copy = pltpu.make_async_copy(src, dst, self.sem.at[self.at])
        self.at += 1
        copy.start()
        return copy

    def keep(self, src, dst):
        self.kept.append(self.start(src, dst))

    def wait_kept(self):
        for copy in self.kept:
            copy.wait()


class Sender:
    def __init__(self, send, recv):
        self.send, self.recv, self.at = send, recv, 0

    def start(self, src, dst, device):
        assert self.at < self.send.shape[0]
        copy = pltpu.make_async_remote_copy(
            src_ref=src,
            dst_ref=dst,
            send_sem=self.send.at[self.at],
            recv_sem=self.recv.at[self.at],
            device_id=device,
            device_id_type=MESH,
        )
        self.at += 1
        copy.start()
        return copy


def step_of(k):
    row = lax.div(lax.rem(k, 8), 2)
    return 4 * row + 2 * lax.rem(k, 2) + lax.rem(row + lax.div(k, 8), 2)


class Exchange:
    def __init__(self, r, number, src, dst, back):
        self.send, self.recv = getattr(r, f"send{number}"), getattr(r, f"recv{number}")
        self.src, self.dst, self.back = src, dst, back
        self.me = lax.axis_index("expert")

    def copy(self, k):
        step = step_of(k)
        target = peer(PEERS - step if self.back else step)
        return pltpu.make_async_remote_copy(
            src_ref=self.src.at[k if self.back else target[1]],
            dst_ref=self.dst.at[self.me if self.back else k],
            send_sem=self.send.at[k],
            recv_sem=self.recv.at[k],
            device_id=target,
            device_id_type=MESH,
        )

    def own(self):
        src = self.src.at[0 if self.back else self.me]
        dst = self.dst.at[self.me if self.back else 0]
        return pltpu.make_async_copy(src, dst, self.send.at[0])

    def each(self, group, act):
        first, last = ((1, PEERS), (1, 8), (8, PEERS))[group + 1]

        def body(k, carry):
            act(self.copy(k))
            return carry

        lax.fori_loop(first, last, body, 0)

    def start(self, group=-1):
        if group <= 0:
            self.own().start()
        self.each(group, lambda copy: copy.start())

    def arrive(self, group=-1):
        if group <= 0:
            self.own().wait()
        self.each(group, lambda copy: copy.wait_recv())

    def sent(self):
        self.each(-1, lambda copy: copy.wait_send())


def rows_of(ref):
    value = ref[...]
    return value.astype(F32).reshape(value.shape[0] * CAP, WIDE).astype(BF)


def store_rows(ref, rows):
    ref[...] = rows.reshape(rows.shape[0] // CAP, CAP, WIDE).astype(BF)


def group_of(ref, group):
    return ref.at[pl.ds(8 * group, 8)]


def slot_matrices(ids, weights):
    core = lax.axis_index("blk")
    expert = 2 * lax.broadcasted_iota(jnp.int32, (PEERS, TOKENS), 0) + core
    chosen = jnp.zeros((PEERS, TOKENS), F32)
    gate = jnp.zeros((PEERS, TOKENS), F32)
    for j in range(TOP):
        hit = jnp.where(ids[j : j + 1, :] == expert, 1.0, 0.0)
        chosen = chosen + hit
        gate = gate + hit * weights[j : j + 1, :]
    before = lax.broadcasted_iota(jnp.int32, (TOKENS, TOKENS), 0) < lax.broadcasted_iota(
        jnp.int32, (TOKENS, TOKENS), 1
    )
    rank = dot(chosen.astype(BF), jnp.where(before, 1.0, 0.0).astype(BF))
    rank = jnp.where(chosen > 0.0, rank, -1.0)
    shape = (PEERS, CAP, TOKENS)
    place = lax.broadcasted_iota(jnp.int32, shape, 1).astype(F32)
    onehot = jnp.where(jnp.broadcast_to(rank[:, None, :], shape) == place, 1.0, 0.0)
    weighted = onehot * jnp.broadcast_to(gate[:, None, :], shape)
    return onehot.reshape(SLOTS, TOKENS), weighted.reshape(SLOTS, TOKENS)


def halves(value):
    high = value.astype(BF)
    return high, (value - high.astype(F32)).astype(BF)


def combine(weighted, rows):
    high, low = halves(weighted)
    return dot(high, rows, 0, 0) + dot(low, rows, 0, 0)


def gain_rows(w_ref):
    unit = jnp.where(
        lax.broadcasted_iota(jnp.int32, (8, 128), 0) == lax.broadcasted_iota(jnp.int32, (8, 128), 1),
        1.0,
        0.0,
    ).astype(BF)
    rows = dot(unit, w_ref[:, QKV + OUT : COLS], 1, 1)
    return rows[0:1, :], rows[1:2, :]


def inverse_norm(u):
    return lax.rsqrt(jnp.mean(u * u, axis=-1, keepdims=True) + epsilon)


def norm_back(u, inverse, gain, upstream):
    scaled = upstream * gain
    inward = inverse * scaled - u * (inverse * inverse * inverse) * jnp.mean(
        u * scaled, axis=-1, keepdims=True
    )
    return inward, upstream * u * inverse


def rotate(u, cos, sin):
    return u * cos + pltpu.roll(u, HEAD // 2, 1) * sin


def unrotate(u, cos, sin):
    return u * cos - pltpu.roll(u, HEAD // 2, 1) * sin


def head_of(value, h):
    return value[:, h * HEAD : (h + 1) * HEAD]


def attention(x, gain, w_ref, cos, sin, allow, n_ref, qkv_ref, prob_ref, o_ref):
    n = (x * inverse_norm(x) * gain).astype(BF)
    n_ref[...] = n
    flat = dot(n, w_ref[:, 0:QKV])
    for h in range(HEADS + 1):
        qkv_ref[:, h * HEAD : (h + 1) * HEAD] = rotate(head_of(flat, h), cos, sin).astype(BF)
    qkv_ref[:, (HEADS + 1) * HEAD :] = flat[:, (HEADS + 1) * HEAD :].astype(BF)
    key = qkv_ref[:, HEADS * HEAD : (HEADS + 1) * HEAD]
    value = qkv_ref[:, (HEADS + 1) * HEAD :]
    for h in range(HEADS):
        scores = dot(qkv_ref[:, h * HEAD : (h + 1) * HEAD], key, 1, 1) * HEAD ** (-0.5)
        scores = jnp.where(allow > 0.0, scores, -1e30)
        weight = jnp.exp(scores - jnp.max(scores, axis=-1, keepdims=True))
        prob = weight / jnp.sum(weight, axis=-1, keepdims=True)
        prob_ref[h] = prob
        o_ref[:, h * HEAD : (h + 1) * HEAD] = dot(prob.astype(BF), value).astype(BF)
    return dot(o_ref[...], w_ref[:, QKV : QKV + OUT], 1, 1)


def expert_weight_copies(layer, r, local):
    core = lax.axis_index("blk")
    copies = []
    for name in ("gate", "up", "down"):
        held = getattr(r, "held_" + name)
        copies.append(local.start(getattr(r, name).at[layer, core], held.at[0]))
        copies.append(local.start(getattr(r, name + "_other").at[layer], held.at[1]))
    return copies


GROUP = SLOTS // 2


def expert_forward(group, rows, held, a_ref, b_ref):
    gate, up, down = held
    at = pl.ds(GROUP * group, GROUP)
    total = None
    for c in range(2):
        a = dot(rows, gate[c])
        b = dot(rows, up[c])
        a_ref[c, at] = a
        b_ref[c, at] = b
        z = (a / (1.0 + jnp.exp(-a)) * b).astype(BF)
        term = dot(z, down[c])
        total = term if total is None else total + term
    return total


def expert_backward(group, dy, held, a_ref, b_ref, z_ref, d_ref):
    gate, up, down = held
    at = pl.ds(GROUP * group, GROUP)
    total = None
    for c in range(2):
        a = a_ref[c, at]
        b = b_ref[c, at]
        sg = 1.0 / (1.0 + jnp.exp(-a))
        z_ref[at, c * HIDDEN : (c + 1) * HIDDEN] = (a * sg * b).astype(BF)
        dz = dot(dy, down[c], 1, 1)
        da = (dz * b * sg * (1.0 + a * (1.0 - sg))).astype(BF)
        db = (dz * a * sg).astype(BF)
        d_ref[at, 2 * c * HIDDEN : (2 * c + 1) * HIDDEN] = da
        d_ref[at, (2 * c + 1) * HIDDEN : (2 * c + 2) * HIDDEN] = db
        term = dot(da, gate[c], 1, 1) + dot(db, up[c], 1, 1)
        total = term if total is None else total + term
    return total


def expert_gradients(rows_ref, dy_ref, z_ref, d_ref, stage, grads, local, xyz, ready=None):
    sent = []
    for k, by in enumerate((2, 1, 3, 0)):
        quarter = shifted(xyz, 0, by)[0]
        columns = pl.ds(pl.multiple_of(quarter * HIDDEN, 128), HIDDEN)
        slot = k % 2
        if k >= 2:
            sent[k - 2].wait()
            if ready:
                ready(k - 2)
        both = dot(rows_ref[:, columns], d_ref[...], 0, 0)
        for c in range(2):
            for i in range(2):
                at = (2 * c + i) * HIDDEN
                stage[slot, 3 * c + i] = both[:, at : at + HIDDEN].astype(BF)
        low = dot(z_ref[...], dy_ref[:, columns], 0, 0)
        for c in range(2):
            stage[slot, 3 * c + 2] = low[c * HIDDEN : (c + 1) * HIDDEN].astype(BF)
        sent.append(local.start(stage.at[slot], grads.at[quarter]))
    for k in (2, 3):
        sent[k].wait()
        if ready and k == 2:
            ready(k)


def ring_devices(xyz, core, axis, steps=(1, 2, 3)):
    return [device_at(shifted(xyz, axis, by), core) for by in steps]


def arrive(copies):
    for copy in copies:
        copy.wait_recv()


class Gather:
    def __init__(self, sender, xyz, core):
        self.sender, self.xyz, self.core = sender, xyz, core

    def slab(self, job, stage, at, half=None):
        whole, lane, lanes, order = job
        index = list(at)
        for axis in order[:stage]:
            index[axis] = pl.ds(0, 4)
        if half is not None:
            index[order[0]] = pl.ds(2 * half, 2)
        return whole.at[index[0], index[1], index[2], :, pl.ds(lane, lanes)]

    def to(self, job, stage, by):
        return device_at(shifted(self.xyz, job[3][stage], by), self.core)

    def first(self, job, shard):
        source = shard.at[:, pl.ds(job[1], job[2])]
        target = self.slab(job, 0, self.xyz)
        return [self.sender.start(source, target, self.to(job, 0, by)) for by in (1, 3, 2)]

    def near(self, job, stage, steps=(1, 3)):
        block = self.slab(job, stage, self.xyz)
        return [self.sender.start(block, block, self.to(job, stage, by)) for by in steps]

    def relay(self, job, stage, near):
        copies = []
        for half, by in enumerate((1, 3)):
            near[half].wait_recv()
            at = shifted(self.xyz, job[3][stage], 4 - by)
            block = self.slab(job, stage, at, half)
            copies.append(self.sender.start(block, block, self.to(job, stage, by)))
        return copies

    def finish(self, near, relays):
        for copy in near:
            copy.wait_send()
        for copy in relays:
            copy.wait()


class ExpertSum:
    def __init__(self, r, layer, sender, local, xyz, core):
        self.r, self.sender, self.local, self.core = r, sender, local, core
        self.plus, self.minus = ring_devices(xyz, core, 0, (1, 3))
        self.grads, self.near, self.far, self.total = (
            getattr(r, f"{name}_{layer}") for name in ("grads", "near", "far", "total")
        )
        self.quarter = [shifted(xyz, 0, by)[0] for by in range(4)]

    def half(self, by, half):
        return self.grads.at[self.quarter[by], pl.ds(3 * half, 3)]

    def near_half(self, side, half):
        return self.near.at[side, pl.ds(3 * half, 3)]

    def send(self, part):
        go = self.sender.start
        if part == 0:
            self.passed = [
                go(self.half(2, 0), self.far.at[0], self.plus),
                go(self.half(2, 1), self.far.at[1], self.minus),
            ]
        elif part == 1:
            self.plain = [go(self.half(1, 1), self.near_half(0, 1), self.plus)]
        else:
            self.plain.append(go(self.half(3, 0), self.near_half(1, 0), self.minus))

    def start(self):
        for part in range(3):
            self.send(part)

    def relay(self):
        r, load = self.r, self.local.start
        own = [load(self.half(by, side), r.own.at[side]) for side, by in enumerate((1, 3))]
        came = []
        for side in range(2):
            self.passed[side].wait_recv()
            came.append(load(self.far.at[side], r.work.at[side]))
        for side, target in enumerate((self.plus, self.minus)):
            own[side].wait()
            came[side].wait()
            for i in range(3):
                value = r.own[side, i].astype(F32) + r.work[side, i].astype(F32)
                r.work[side, i] = value.astype(BF)
            self.plain.append(
                self.sender.start(r.work.at[side], self.near_half(side, side), target)
            )

    def finish(self):
        r, load = self.r, self.local.start
        for copy in self.plain:
            copy.wait()
        for copy in self.passed:
            copy.wait_send()

        def bring(i, slot):
            return [
                load(self.grads.at[self.quarter[0], i], r.own.at[slot, 0]),
                load(self.near.at[0, i], r.own.at[slot, 1]),
                load(self.near.at[1, i], r.own.at[slot, 2]),
            ]

        order, out = (3, 4, 5, 0, 1, 2), []
        loads = [bring(order[0], 0)]
        for k, i in enumerate(order):
            if k < 5:
                loads.append(bring(order[k + 1], (k + 1) % 2))
            for copy in loads[k]:
                copy.wait()
            slot = k % 2
            value = r.own[slot, 0].astype(F32) + r.own[slot, 1].astype(F32)
            r.ship[k] = (value + r.own[slot, 2].astype(F32)).astype(BF)
            to = self.total.at[self.core, i % 3]
            if k < 3:
                out.append(self.sender.start(r.ship.at[k], to, partner()))
            else:
                out.append(load(r.ship.at[k], to))
        for copy in out:
            copy.wait()


def tables(r):
    first = r.lengths[0, 0]
    second = first + r.lengths[0, 1]

    def place(index):
        segment = jnp.where(index >= first, 1, 0) + jnp.where(index >= second, 1, 0)
        start = jnp.where(segment == 0, 0, jnp.where(segment == 1, first, second))
        return segment, index - start

    shape = (TOKENS, TOKENS)
    lane = lax.broadcasted_iota(jnp.int32, shape, 1)
    row_segment, row_place = place(lax.broadcasted_iota(jnp.int32, shape, 0))
    key_segment, key_place = place(lane)
    allowed = (row_segment == key_segment) & (key_place <= row_place)
    r.allow[...] = jnp.where(allowed, 1.0, 0.0)
    half = jnp.where(lane < HEAD // 2, lane, lane - HEAD // 2).astype(F32)
    frequency = jnp.exp(half * (-2.0 / HEAD * math.log(rope_base)))
    angles = row_place.astype(F32) * frequency
    sign = jnp.where(lane < HEAD // 2, -1.0, 1.0)
    r.cos[...] = jnp.cos(angles)
    r.sin[...] = jnp.sin(angles) * sign


def assemble(r):
    square = (SHARD, SHARD)
    eye = lax.broadcasted_iota(jnp.int32, square, 0) == lax.broadcasted_iota(jnp.int32, square, 1)
    lane = lax.broadcasted_iota(jnp.int32, (SHARD, 128), 1)
    for l in range(LAYERS):
        r.shard[l, :, 0:768] = r.query[l]
        r.shard[l, :, 768:896] = r.key[l]
        r.shard[l, :, 896:QKV] = r.value[l]
        r.shard[l, :, QKV : QKV + OUT] = r.out[l]
        column = jnp.zeros((SHARD, 128), F32)
        for i, gain in enumerate((r.gain_a, r.gain_e)):
            spread = jnp.broadcast_to(gain[l : l + 1, :].astype(F32), square)
            spread = jnp.where(eye, spread, 0.0).astype(BF)
            column = column + dot(spread, jnp.where(lane == i, 1.0, 0.0).astype(BF))
        r.shard[l, :, QKV + OUT :] = column.astype(BF)


KEPT = dict(
    h=((TOKENS, WIDE), F32),
    n=((TOKENS, WIDE), BF),
    qkv=((TOKENS, QKV), BF),
    prob=((HEADS, TOKENS, TOKENS), F32),
    o=((TOKENS, OUT), BF),
    onehot=((SLOTS, TOKENS), BF),
    weighted=((SLOTS, TOKENS), F32),
)
KEPT_SPACE = {name: pltpu.VMEM(*spec) for name, spec in KEPT.items()}
HELD = dict(
    held_gate=pltpu.VMEM((2, WIDE, HIDDEN), BF),
    held_up=pltpu.VMEM((2, WIDE, HIDDEN), BF),
    held_down=pltpu.VMEM((2, HIDDEN, WIDE), BF),
)
ROWS = ((SLOTS, WIDE), BF)
INNER = ((2, SLOTS, HIDDEN), F32)
BLOCKS = ((PEERS, CAP, WIDE), BF)
PLANE = ((TOKENS, WIDE), F32)
FLAT = ((TOKENS, WIDE), BF)
GRADS = ((4, 6, HIDDEN, HIDDEN), BF)
BACKWARD = dict(
    z=pltpu.VMEM((SLOTS, 2 * HIDDEN), BF),
    d=pltpu.VMEM((SLOTS, 4 * HIDDEN), BF),
    dy=pltpu.VMEM(*ROWS),
    stage=pltpu.VMEM((2, 6, HIDDEN, HIDDEN), BF),
)


def sems(**counts):
    return {name: pltpu.SemaphoreType.DMA((n,)) for name, n in counts.items()}


def spaces(**specs):
    return {name: pltpu.VMEM(*spec) for name, spec in specs.items()}


def attend(r, l, x, pair, local, then=None):
    gain_a, gain_e = gain_rows(r.w)
    r.part0[...] = attention(
        x, gain_a, r.w, r.cos[...], r.sin[...], r.allow[...], r.n, r.qkv, r.prob, r.o
    ).astype(BF)
    copy = pair.start(r.part0, r.theirs0, partner())
    for name in ("n", "qkv", "prob", "o"):
        local.keep(getattr(r, name), getattr(r, f"{name}_{l}"))
    begun = then() if then else None
    copy.wait_recv()
    h = x + (r.part0[...].astype(F32) + r.theirs0[...].astype(F32))
    copy.wait_send()
    r.h[...] = h
    local.keep(r.h, getattr(r, f"h_{l}"))
    return (h * inverse_norm(h) * gain_e).astype(BF), begun


def front_body(r):
    xyz, core = coords(), lax.axis_index("blk")
    local, pair = Local(r.local), Sender(r.pair_send, r.pair_recv)
    sender = Sender(r.wide_send, r.wide_recv)
    gather = Gather(sender, xyz, core)
    held = (r.held_gate, r.held_up, r.held_down)
    count = hail(peers() + ring_devices(xyz, core, 0))
    mine = pl.ds(pl.multiple_of(core * HALF, HALF), HALF)
    here = [
        local.start(r.tok, r.tokens.at[:, mine]),
        local.start(r.cot_half, r.cot.at[:, mine]),
    ]
    assemble(r)
    here.append(local.start(r.shard.at[0], r.cube.at[xyz[0], xyz[1], xyz[2]]))
    here_later = local.start(r.shard.at[1], r.later.at[xyz[0], xyz[1], xyz[2]])
    heard(count)
    now = [(r.cube, p * PART, PART, order) for p, order in enumerate(ORDERS)]
    first = [c for job in now for c in gather.first(job, r.shard.at[0])]
    halves_sent = [
        sender.start(r.tok, r.tokens.at[:, mine], partner()),
        sender.start(r.cot_half, r.cot.at[:, mine], partner()),
    ]
    swaps = [[], []]
    for l in range(LAYERS):
        for name in ("gate", "up", "down"):
            ref = getattr(r, name).at[l, 1 - core]
            swaps[l].append(sender.start(ref, getattr(r, name + "_other").at[l], partner()))
    tables(r)
    for l, (onehot, weighted) in enumerate(((r.onehot_0, r.weighted_0), (r.onehot_1, r.weighted_1))):
        hot, heavy = slot_matrices(r.ids[l], r.weights[l])
        onehot[...] = hot.astype(BF)
        weighted[...] = heavy
    for copy in here:
        copy.wait()
    arrive(first)
    near = [gather.near(job, 1, (1, 3, 2)) for job in now]

    def onward(job, at):
        block = gather.slab(job, 1, at)
        return at, [sender.start(block, block, gather.to(job, 2, by)) for by in (1, 3)]

    last = [[onward(job, xyz)] for job in now]
    arrive(halves_sent)
    slot_weight = jnp.sum(r.weighted_1[...], axis=1, keepdims=True)
    store_rows(r.sent_g, dot(r.onehot_1[...], r.cot[...]) * slot_weight)
    for n, by in enumerate((1, 3, 2)):
        for p, job in enumerate(now):
            near[p][n].wait_recv()
            last[p].append(onward(job, shifted(xyz, job[3][1], 4 - by)))
    relays = []
    for m in range(4):
        for p, job in enumerate(now):
            at, copies = last[p][m]
            for half, by in enumerate((1, 3)):
                copies[half].wait_recv()
                block = gather.slab(job, 1, shifted(at, job[3][2], 4 - by), half)
                relays.append(sender.start(block, block, gather.to(job, 2, by)))
    arrive(swaps[0])
    loads = expert_weight_copies(0, r, local)
    arrive(relays)
    jobs = [(r.later, *job) for job in LATER]
    first_later = [c for job in jobs for c in gather.first(job, r.shard.at[1])]
    r.w[...] = r.cube[...].astype(F32).reshape(WIDE, COLS).astype(BF)
    w_kept = local.start(r.w, r.w_0)

    def second():
        here_later.wait()
        arrive(first_later)
        return [c for job in jobs for c in gather.near(job, 1, (1, 3, 2))]

    m, near_later = attend(r, 0, r.tokens[...].astype(F32), pair, local, second)
    store_rows(r.sent, dot(r.onehot_0[...], m))
    out0 = Exchange(r, 0, r.sent, r.came, False)
    out0.start()
    arrive(near_later)
    last_later = [gather.near(job, 2) for job in jobs]
    relays_later = {}
    for copy in loads:
        copy.wait()
    back0 = Exchange(r, 1, r.turn, r.back, True)
    for g in range(2):
        out0.arrive(g)
        at = pl.ds(GROUP * g, GROUP)
        r.rows[at] = rows_of(group_of(r.came, g))
        store_rows(group_of(r.turn, g), expert_forward(g, r.rows[at], held, r.a, r.b))
        back0.start(g)
    rows_kept = [local.start(r.rows, r.rows_0), local.start(r.a, r.a_0), local.start(r.b, r.b_0)]
    out0.sent()
    arrive(swaps[1])
    loads = expert_weight_copies(1, r, local)
    for i in range(len(jobs)):
        relays_later[i] = gather.relay(jobs[i], 2, last_later[i])
    back0.arrive()
    out_g = Exchange(r, 3, r.sent_g, r.came_g, False)
    out_g.start()
    r.part1[...] = combine(r.weighted_0[...], rows_of(r.back)).astype(BF)
    copy = pair.start(r.part1, r.theirs1, partner())
    w_kept.wait()
    local.wait_kept()
    local.kept = []
    copy.wait_recv()
    x = r.h[...] + (r.part1[...].astype(F32) + r.theirs1[...].astype(F32))
    r.stream[...] = x
    copy.wait_send()
    for i in range(len(jobs)):
        arrive(relays_later[i])
    for copy in relays + [c for n in near for c in n] + [c for n in last for _, two in n for c in two]:
        copy.wait_send()
    load = local.start(r.later, r.cube)
    load.wait()
    r.w[...] = r.cube[...].astype(F32).reshape(WIDE, COLS).astype(BF)
    local.keep(r.w, r.w_1)
    m, _ = attend(r, 1, x, pair, local)
    store_rows(r.sent, dot(r.onehot_1[...], m))
    out1 = Exchange(r, 2, r.sent, r.came, False)
    out1.start()
    back0.sent()
    out_g.arrive()
    r.dy[...] = rows_of(r.came_g)
    for copy in loads + rows_kept:
        copy.wait()
    for g in range(2):
        out1.arrive(g)
        at = pl.ds(GROUP * g, GROUP)
        r.rows[at] = rows_of(group_of(r.came, g))
        store_rows(group_of(r.back, g), expert_forward(g, r.rows[at], held, r.a, r.b))
        result = expert_backward(g, r.dy[at], held, r.a, r.b, r.z, r.d)
        store_rows(group_of(r.turn, g), result)
    local.keep(r.back, r.y_1)
    local.keep(r.turn, r.m_1)
    expert_gradients(r.rows, r.dy, r.z, r.d, r.stage, r.grads_1, local, xyz)
    out1.sent()
    out_g.sent()
    for copy in first + first_later + near_later + halves_sent + swaps[0] + swaps[1]:
        copy.wait_send()
    for i in range(len(jobs)):
        for copy in last_later[i] + relays_later[i]:
            copy.wait_send()
    local.wait_kept()


def turned(value):
    return value.astype(F32).T.reshape(4, 4, 4, SHARD, TOKENS).astype(BF)


def own_part(ref, axis, index):
    return ref.at[:, index] if axis == 1 else ref.at[:, :, index]


def share_factor(ref, into, axis, sender, xyz, core):
    copies = []
    for by in (1, 3, 2):
        there = shifted(xyz, axis, by)
        copies.append(
            sender.start(own_part(ref, axis, there[axis]), into.at[by - 1], device_at(there, core))
        )
    return copies


def share_whole(ref, axis, sender, xyz, core):
    return [
        sender.start(
            ref.at[pl.ds(0, TOKENS)],
            ref.at[pl.ds(by * TOKENS, TOKENS)],
            device_at(shifted(xyz, axis, by), core),
        )
        for by in (1, 3, 2)
    ]


def quarter_sum(own, came, axis, xyz, right):
    first = own_part(own, axis, xyz[axis])[...]
    pieces = [first] + [came[i] for i in range(3)]
    left = [p.astype(F32).reshape(HIDDEN, TOKENS).astype(BF) for p in pieces]
    return dot(jnp.concatenate(left, axis=1), right[...])


def back_body(r):
    xyz, core = coords(), lax.axis_index("blk")
    local, pair = Local(r.local), Sender(r.pair_send, r.pair_recv)
    sender = Sender(r.wide_send, r.wide_recv)

    def load_layer(l):
        names = ("w", "h", "qkv", "prob", "o")
        return [local.start(getattr(r, f"{name}_{l}"), getattr(r, name)) for name in names]

    loads = load_layer(1)
    count = hail(peers() + ring_devices(xyz, core, 0))
    sums = [ExpertSum(r, l, sender, local, xyz, core) for l in range(LAYERS)]
    heard(count)
    came_m, onehot = (r.came_0, r.came_1), (r.onehot_0, r.onehot_1)
    back = [Exchange(r, 2, r.turn, r.came_0, True), Exchange(r, 0, r.m_1, r.came_1, True)]
    out_g = Exchange(r, 1, r.sent, r.came_g, False)
    y_back = Exchange(r, 3, r.y_1, r.came_1, True)
    back[1].start()
    sums[1].start()
    weights = expert_weight_copies(0, r, local)
    weights += [local.start(getattr(r, name + "_0"), getattr(r, name)) for name in ("rows", "a", "b")]
    r.n_turned[1] = turned(r.n_1[...])
    r.n_turned[0] = turned(r.n_0[...])
    for copy in loads:
        copy.wait()
    shared = [[], []]
    scale = HEAD ** (-0.5)
    row = lax.broadcasted_iota(jnp.int32, (8, WIDE), 0)
    r.gain_sum[1] = jnp.zeros((8, WIDE), F32)
    inner, across = [None] * 2, [None] * 2
    for l in (1, 0):
        x = (r.stream if l == 1 else r.tokens)[...].astype(F32)
        gain_a, gain_e = gain_rows(r.w)
        r.o_all[l, 0:TOKENS] = r.o[...]
        back[l].arrive()
        r.part[0] = dot(onehot[l][...], rows_of(came_m[l]), 0, 0)
        inner[l] = pair.start(r.part.at[0], r.theirs.at[l, 0], partner())
        if l == 1:
            for i in (1, 0):
                shared[i] += share_factor(r.n_turned.at[i], r.n_came.at[i], 1, sender, xyz, core)
        shared[l] += share_whole(r.o_all.at[l], 2, sender, xyz, core)
        inner[l].wait_recv()
        dm = r.part[0] + r.theirs[l, 0]
        hidden = r.h[...]
        inward, gain_grad_e = norm_back(hidden, inverse_norm(hidden), gain_e, dm)
        gh = (r.cot[...].astype(F32) if l == 1 else r.flow[...]) + inward
        r.flow[...] = gh
        da = gh.astype(BF)
        r.da_turned[l] = turned(gh)
        shared[l] += share_factor(r.da_turned.at[l], r.da_came.at[l], 2, sender, xyz, core)
        do = dot(da, r.w[:, QKV : QKV + OUT]).astype(BF)
        key = r.qkv[:, HEADS * HEAD : (HEADS + 1) * HEAD]
        value = r.qkv[:, (HEADS + 1) * HEAD :]
        key_grad, value_grad = None, None
        cosine, sine = r.cos[...], r.sin[...]
        lin = r.lin_all.at[l]
        for i in range(HEADS):
            prob_i = r.prob[i]
            do_i = head_of(do, i)
            q_i = r.qkv[:, i * HEAD : (i + 1) * HEAD]
            dprob = dot(do_i, value, 1, 1)
            centre = jnp.sum(prob_i * dprob, axis=-1, keepdims=True)
            ds = (prob_i * (dprob - centre)).astype(BF)
            dq = dot(ds, key) * scale
            lin[0:TOKENS, i * HEAD : (i + 1) * HEAD] = unrotate(dq, cosine, sine).astype(BF)
            dk = dot(ds, q_i, 0, 0)
            dv = dot(prob_i.astype(BF), do_i, 0, 0)
            key_grad = dk if key_grad is None else key_grad + dk
            value_grad = dv if value_grad is None else value_grad + dv
        lin[0:TOKENS, HEADS * HEAD : (HEADS + 1) * HEAD] = unrotate(
            key_grad * scale, cosine, sine
        ).astype(BF)
        lin[0:TOKENS, (HEADS + 1) * HEAD :] = value_grad.astype(BF)
        r.part[1] = dot(lin[0:TOKENS, :], r.w[:, 0:QKV], 1, 1)
        across[l] = pair.start(r.part.at[1], r.theirs.at[l, 1], partner())
        if l == 1:
            r.kept_half[...] = jnp.where(core == 1, r.h[:, HALF:], r.h[:, :HALF])
            loads = load_layer(0)
        else:
            shared[0] += share_whole(r.lin_all.at[0], 1, sender, xyz, core)
            sums[0].relay()
        across[l].wait_recv()
        dn = r.part[1] + r.theirs[l, 1]
        inward, gain_grad_a = norm_back(x, inverse_norm(x), gain_a, dn)
        flow = r.flow[...] + inward
        gains = r.gain_sum[1]
        for i, grad in enumerate((gain_grad_a, gain_grad_e)):
            grad = jnp.sum(grad, axis=0, keepdims=True)
            gains = jnp.where(row == 2 * l + i, jnp.broadcast_to(grad, (8, WIDE)), gains)
        r.gain_sum[1] = gains
        inner[l].wait_send()
        across[l].wait_send()
        if l == 0:
            r.tokens_grad[...] = jnp.where(core == 1, flow[:, HALF:], flow[:, :HALF])
            continue
        r.flow[...] = flow
        slot_weight = jnp.sum(r.weighted_0[...], axis=1, keepdims=True)
        high, low = halves(flow)
        hot = r.onehot_0[...]
        store_rows(r.sent, (dot(hot, high) + dot(hot, low)) * slot_weight)
        out_g.start()
        sums[1].relay()
        for copy in weights:
            copy.wait()
        held = (r.held_gate, r.held_up, r.held_down)
        for g in range(2):
            out_g.arrive(g)
            at = pl.ds(GROUP * g, GROUP)
            r.dy[at] = rows_of(group_of(r.came_g, g))
            result = expert_backward(g, r.dy[at], held, r.a, r.b, r.z, r.d)
            store_rows(group_of(r.turn, g), result)
            back[0].start(g)
        shared[1] += share_whole(r.lin_all.at[1], 1, sender, xyz, core)
        expert_gradients(
            r.rows, r.dy, r.z, r.d, r.stage, r.grads_0, local, xyz, sums[0].send
        )
        sums[1].finish()
        for copy in loads:
            copy.wait()
    last_sums = finish_sums(r, shared, y_back, sender, xyz, core)
    y_back.arrive()
    mixed = combine(r.weighted_1[...], rows_of(r.came_1))
    r.half[...] = jnp.where(core == 1, mixed[:, :HALF], mixed[:, HALF:])
    third = pair.start(r.half, r.half_theirs, partner())
    own = jnp.where(core == 1, mixed[:, HALF:], mixed[:, :HALF])
    third.wait()
    r.block_out[...] = (r.kept_half[...] + (own + r.half_theirs[...])).astype(BF)
    sums[0].finish()
    last_sums()
    for exchange in (*back, out_g, y_back):
        exchange.sent()


def late_start(r, l, sender, xyz, core):
    copies = []
    for ref, came, axis in ((r.sum_a, r.near_a, 2), (r.sum_b, r.near_b, 1)):
        for by in (1, 3, 2):
            there = shifted(xyz, axis, by)
            copies.append(
                sender.start(ref.at[l, :, there[axis]], came.at[l, by - 1], device_at(there, core))
            )
    return copies


def late_middle(r, l, sender, xyz, core, copies):
    arrive(copies)
    for ref, came, axis, lanes in (
        (r.sum_a, r.near_a, 2, slice(0, QKV)),
        (r.sum_b, r.near_b, 1, slice(QKV, QKV + OUT)),
    ):
        total = ref[l, :, xyz[axis]].astype(F32)
        for i in range(3):
            total = total + came[l, i].astype(F32)
        r.line[l, :, :, lanes] = total.astype(BF)
    copies = []
    for by in (1, 3, 2):
        there = shifted(xyz, 0, by)
        copies.append(
            sender.start(r.line.at[l, there[0]], r.line_came.at[l, by - 1], device_at(there, core))
        )
    return copies


def late_end(r, l, xyz, copies):
    for copy in copies:
        copy.wait()
    total = r.line[l, xyz[0]].astype(F32)
    for i in range(3):
        total = total + r.line_came[l, i].astype(F32)
    r.weight_grad[l] = total


def gains_along(r, axis, sender, xyz, core):
    copies = []
    for by in (1, 3, 2):
        there = shifted(xyz, axis, by)
        if axis == 0:
            quarter = pl.ds(pl.multiple_of(there[0] * HIDDEN, 128), HIDDEN)
            src, dst = r.gain_sum.at[0, :, quarter], r.gain_last.at[by - 1]
        else:
            src, dst = r.gain_sum.at[axis], r.gain_came.at[axis - 1, by - 1]
        copies.append(sender.start(src, dst, device_at(there, core)))
    return copies


def gains_next(r, axis, xyz, copies):
    for copy in copies:
        copy.wait()
    if axis == 0:
        total = r.gain_sum[0, :, pl.ds(pl.multiple_of(xyz[0] * HIDDEN, 128), HIDDEN)]
        for i in range(3):
            total = total + r.gain_last[i]
        return total
    total = r.gain_sum[axis]
    for i in range(3):
        total = total + r.gain_came[axis - 1, i]
    return total


def finish_sums(r, shared, y_back, sender, xyz, core):
    def quarter(l):
        arrive(shared[l])
        wide = (4, 4, SHARD, QKV)
        total = quarter_sum(r.n_turned.at[l], r.n_came.at[l], 1, xyz, r.lin_all.at[l])
        r.sum_a[l] = total.reshape(wide).astype(BF)
        wide = (4, 4, SHARD, OUT)
        total = quarter_sum(r.da_turned.at[l], r.da_came.at[l], 2, xyz, r.o_all.at[l])
        r.sum_b[l] = total.reshape(wide).astype(BF)
        return late_start(r, l, sender, xyz, core)

    along = gains_along(r, 1, sender, xyz, core)
    above = quarter(1)
    r.gain_sum[2] = gains_next(r, 1, xyz, along)
    along = gains_along(r, 2, sender, xyz, core)
    above_last = late_middle(r, 1, sender, xyz, core, above)
    y_back.start()
    r.gain_sum[0] = gains_next(r, 2, xyz, along)
    along = gains_along(r, 0, sender, xyz, core)
    lower = quarter(0)
    lower_last = late_middle(r, 0, sender, xyz, core, lower)

    def end():
        late_end(r, 1, xyz, above_last)
        r.gain_total[...] = gains_next(r, 0, xyz, along)
        late_end(r, 0, xyz, lower_last)
        for copy in shared[0] + shared[1] + above + lower:
            copy.wait_send()

    return end


def finish_body(r):
    local = Local(r.local)
    loads = [
        [local.start(total.at[:, i], r.narrow.at[l, i]) for i in range(3)]
        for l, total in enumerate((r.total_below, r.total_above))
    ]
    r.block_out[...] = r.block_in[...]
    r.tokens_grad[...] = r.tokens_in[...]
    place = lax.axis_index("expert") * SHARD
    near = pltpu.roll(r.gain_total[...], lax.rem(HIDDEN - place, HIDDEN), 1)
    for l in range(LAYERS):
        r.gain_a[l : l + 1, :] = near[2 * l : 2 * l + 1, :SHARD]
        r.gain_e[l : l + 1, :] = near[2 * l + 1 : 2 * l + 2, :SHARD]
        r.query[l] = r.weight_grad[l, :, :768]
        r.key[l] = r.weight_grad[l, :, 768:896]
        r.value[l] = r.weight_grad[l, :, 896:QKV]
        r.out[l] = r.weight_grad[l, :, QKV:]
    for l in range(LAYERS):
        for i, out in enumerate((r.gate, r.up, r.down)):
            loads[l][i].wait()
            r.broad[l, i] = r.narrow[l, i].astype(F32)
            local.keep(r.broad.at[l, i], out.at[l])
    local.wait_kept()


def kernel_call(body, name, cid, ins, outs, scratch, aliases=()):
    names = [*ins, *outs, *scratch]
    assert len(set(names)) == len(names)

    def kernel(*refs):
        body(types.SimpleNamespace(**dict(zip(names, refs))))

    results = pl.pallas_call(
        kernel,
        out_shape=[jax.ShapeDtypeStruct(shape, kind) for shape, kind, _ in outs.values()],
        in_specs=[space for _, space in ins.values()],
        out_specs=[space for _, _, space in outs.values()],
        scratch_shapes=list(scratch.values()),
        input_output_aliases={list(ins).index(a): list(outs).index(b) for a, b in aliases},
        compiler_params=pltpu.CompilerParams(
            collective_id=cid, has_side_effects=cid is not None, vmem_limit_bytes=LIMIT
        ),
        name=name,
    )(*[array for array, _ in ins.values()])
    return types.SimpleNamespace(**dict(zip(outs, results)))


def per_device(
    tokens_in,
    seq_lengths,
    expert_ids,
    gate_weights,
    attention_gain,
    query_weight,
    key_weight,
    value_weight,
    out_weight,
    expert_gain,
    gate_weight,
    up_weight,
    down_weight,
    cotangent,
):
    cube = (4, 4, 4, SHARD, COLS)
    own = dict(gate=(gate_weight, ANY), up=(up_weight, ANY), down=(down_weight, ANY))
    exchanges = sems(
        **{f"{way}{i}": PEERS for way in ("send", "recv") for i in range(4)}, pair_send=5, pair_recv=5
    )
    kept = ("h", "n", "qkv", "prob", "o")
    w_space = dict(w=pltpu.VMEM((WIDE, COLS), BF))
    start = kernel_call(
        front_body,
        "front",
        1,
        dict(
            lengths=(seq_lengths, SMEM),
            query=(query_weight, VMEM),
            key=(key_weight, VMEM),
            value=(value_weight, VMEM),
            out=(jnp.swapaxes(out_weight, 1, 2), VMEM),
            gain_a=(attention_gain, VMEM),
            gain_e=(expert_gain, VMEM),
            tok=(tokens_in, VMEM),
            cot_half=(cotangent, VMEM),
            ids=(jnp.swapaxes(expert_ids, 1, 2), VMEM),
            weights=(jnp.swapaxes(gate_weights, 1, 2), VMEM),
            **own,
        ),
        dict(
            w_0=((WIDE, COLS), BF, ANY),
            w_1=((WIDE, COLS), BF, ANY),
            later=(cube, BF, ANY),
            tokens=((TOKENS, WIDE), BF, VMEM),
            cot=((TOKENS, WIDE), BF, VMEM),
            stream=(*PLANE, VMEM),
            cos=((TOKENS, HEAD), F32, VMEM),
            sin=((TOKENS, HEAD), F32, VMEM),
            gate_other=((LAYERS, WIDE, HIDDEN), BF, ANY),
            up_other=((LAYERS, WIDE, HIDDEN), BF, ANY),
            down_other=((LAYERS, HIDDEN, WIDE), BF, ANY),
            rows_0=(*ROWS, ANY),
            a_0=(*INNER, ANY),
            b_0=(*INNER, ANY),
            y_1=(*BLOCKS, ANY),
            m_1=(*BLOCKS, ANY),
            grads_1=(*GRADS, ANY),
            **{f"{name}_{l}": (*KEPT[name], ANY) for l in range(LAYERS) for name in kept},
            **{
                f"{name}_{l}": (*KEPT[name], VMEM)
                for l in range(LAYERS)
                for name in ("onehot", "weighted")
            },
        ),
        dict(
            shard=pltpu.VMEM((LAYERS, SHARD, COLS), BF),
            cube=pltpu.VMEM(cube, BF),
            allow=pltpu.VMEM((TOKENS, TOKENS), F32),
            **w_space,
            **{name: KEPT_SPACE[name] for name in kept},
            **HELD,
            **BACKWARD,
            **spaces(sent=BLOCKS, came=BLOCKS, back=BLOCKS, sent_g=BLOCKS, came_g=BLOCKS),
            **spaces(turn=BLOCKS, rows=ROWS, a=INNER, b=INNER),
            **spaces(part0=FLAT, theirs0=FLAT, part1=FLAT, theirs1=FLAT),
            **exchanges,
            **sems(wide_send=114, wide_recv=114, local=50),
        ),
    )
    experts = dict(
        own,
        gate_other=(start.gate_other, ANY),
        up_other=(start.up_other, ANY),
        down_other=(start.down_other, ANY),
    )
    part_a, part_b = (4, 4, SHARD, QKV), (4, 4, SHARD, OUT)
    total = ((2, 3, HIDDEN, HIDDEN), BF, ANY)
    near, far = ((2, 6, HIDDEN, HIDDEN), BF, ANY), ((2, 3, HIDDEN, HIDDEN), BF, ANY)
    factor, quarter = (4, 4, 4, SHARD, TOKENS), (3, 4, 4, SHARD, TOKENS)
    by_layer = {}
    for l in range(LAYERS):
        for name in ("h", "qkv", "prob", "o", "w"):
            by_layer[f"{name}_{l}"] = (getattr(start, f"{name}_{l}"), ANY)
        for name in ("n", "onehot", "weighted"):
            by_layer[f"{name}_{l}"] = (getattr(start, f"{name}_{l}"), VMEM)
    end = kernel_call(
        back_body,
        "backward",
        4,
        dict(
            stream=(start.stream, VMEM),
            tokens=(start.tokens, VMEM),
            cot=(start.cot, VMEM),
            cos=(start.cos, VMEM),
            sin=(start.sin, VMEM),
            **by_layer,
            **{
                name: (getattr(start, name), ANY)
                for name in ("m_1", "y_1", "grads_1", "rows_0", "a_0", "b_0")
            },
            **experts,
        ),
        dict(
            block_out=((TOKENS, HALF), BF, VMEM),
            tokens_grad=((TOKENS, HALF), F32, VMEM),
            weight_grad=((LAYERS, SHARD, QKV + OUT), F32, VMEM),
            gain_total=((8, HIDDEN), F32, VMEM),
            total_0=total,
            total_1=total,
            grads_0=(*GRADS, ANY),
            near_0=near,
            near_1=near,
            far_0=far,
            far_1=far,
        ),
        dict(
            **w_space,
            **HELD,
            **BACKWARD,
            **{name: KEPT_SPACE[name] for name in ("h", "qkv", "prob", "o")},
            **spaces(rows=ROWS, a=INNER, b=INNER, flow=PLANE),
            **spaces(sent=BLOCKS, turn=BLOCKS),
            **spaces(came_0=BLOCKS, came_1=BLOCKS, came_g=BLOCKS),
            part=pltpu.VMEM((2, TOKENS, WIDE), F32),
            theirs=pltpu.VMEM((LAYERS, 2, TOKENS, WIDE), F32),
            half=pltpu.VMEM((TOKENS, HALF), F32),
            half_theirs=pltpu.VMEM((TOKENS, HALF), F32),
            kept_half=pltpu.VMEM((TOKENS, HALF), F32),
            own=pltpu.VMEM((2, 3, HIDDEN, HIDDEN), BF),
            work=pltpu.VMEM((2, 3, HIDDEN, HIDDEN), BF),
            ship=pltpu.VMEM((6, HIDDEN, HIDDEN), BF),
            n_turned=pltpu.VMEM((LAYERS, *factor), BF),
            da_turned=pltpu.VMEM((LAYERS, *factor), BF),
            n_came=pltpu.VMEM((LAYERS, *quarter), BF),
            da_came=pltpu.VMEM((LAYERS, *quarter), BF),
            lin_all=pltpu.VMEM((LAYERS, 4 * TOKENS, QKV), BF),
            o_all=pltpu.VMEM((LAYERS, 4 * TOKENS, OUT), BF),
            sum_a=pltpu.VMEM((LAYERS, *part_a), BF),
            sum_b=pltpu.VMEM((LAYERS, *part_b), BF),
            near_a=pltpu.VMEM((LAYERS, 3, 4, SHARD, QKV), BF),
            near_b=pltpu.VMEM((LAYERS, 3, 4, SHARD, OUT), BF),
            line=pltpu.VMEM((LAYERS, 4, SHARD, QKV + OUT), BF),
            line_came=pltpu.VMEM((LAYERS, 3, SHARD, QKV + OUT), BF),
            gain_sum=pltpu.VMEM((3, 8, WIDE), F32),
            gain_came=pltpu.VMEM((2, 3, 8, WIDE), F32),
            gain_last=pltpu.VMEM((3, 8, HIDDEN), F32),
            **exchanges,
            **sems(wide_send=72, wide_recv=72, local=84),
        ),
    )
    expert_out = ((LAYERS, 2, HIDDEN, HIDDEN), F32, ANY)
    out = kernel_call(
        finish_body,
        "finish",
        None,
        dict(
            block_in=(end.block_out, VMEM),
            tokens_in=(end.tokens_grad, VMEM),
            total_above=(end.total_1, ANY),
            total_below=(end.total_0, ANY),
            weight_grad=(end.weight_grad, VMEM),
            gain_total=(end.gain_total, VMEM),
        ),
        dict(
            block_out=((TOKENS, HALF), BF, VMEM),
            tokens_grad=((TOKENS, HALF), F32, VMEM),
            gain_a=((LAYERS, SHARD), F32, VMEM),
            query=((LAYERS, SHARD, 768), F32, VMEM),
            key=((LAYERS, SHARD, 128), F32, VMEM),
            value=((LAYERS, SHARD, 128), F32, VMEM),
            out=((LAYERS, SHARD, OUT), F32, VMEM),
            gain_e=((LAYERS, SHARD), F32, VMEM),
            gate=expert_out,
            up=expert_out,
            down=expert_out,
        ),
        dict(
            narrow=pltpu.VMEM((LAYERS, 3, 2, HIDDEN, HIDDEN), BF),
            broad=pltpu.VMEM((LAYERS, 3, 2, HIDDEN, HIDDEN), F32),
            **sems(local=14),
        ),
    )
    return (
        out.block_out,
        out.tokens_grad,
        out.gain_a,
        out.query,
        out.key,
        out.value,
        jnp.swapaxes(out.out, 1, 2),
        out.gain_e,
        out.gate,
        out.up,
        out.down,
    )


def solution(mesh):
    placed = (
        P(("dp", "expert"), "blk"),
        P(("dp", "expert"), None),
        P(None, ("dp", "expert"), None),
        P(None, ("dp", "expert"), None),
        P(None, ("dp", "expert")),
        P(None, ("dp", "expert"), "blk"),
        P(None, ("dp", "expert"), "blk"),
        P(None, ("dp", "expert"), "blk"),
        P(None, "blk", ("dp", "expert")),
        P(None, ("dp", "expert")),
        P(None, "expert", None, "blk"),
        P(None, "expert", None, "blk"),
        P(None, "expert", "blk", None),
        P(("dp", "expert"), "blk"),
    )
    return jax.shard_map(
        per_device,
        mesh=mesh,
        in_specs=placed,
        out_specs=(
            P(("dp", "expert"), "blk"),
            P(("dp", "expert"), "blk"),
            P(None, ("dp", "expert")),
            P(None, ("dp", "expert"), "blk"),
            P(None, ("dp", "expert"), "blk"),
            P(None, ("dp", "expert"), "blk"),
            P(None, "blk", ("dp", "expert")),
            P(None, ("dp", "expert")),
            P(None, "expert", "dp", "blk"),
            P(None, "expert", "dp", "blk"),
            P(None, "expert", "blk", "dp"),
        ),
        check_vma=False,
    )
```
